32 devices in a mesh: grp: 2 (over y), dp: 4 (over z), query: 2 (over x), proj: 2 (over core).
Axes of the slice: x: 2, y: 2, z: 4, core: 2. Of those that a mesh axis runs over, the one named last changes fastest.
Arguments:
- activations: bfloat16 [8192, 4096], P(('grp', 'dp', 'query'), 'proj'), parts along dimension 0
- out_grads: bfloat16 [8192, 14336], P(('grp', 'dp', 'query'), 'proj'), parts along dimension 0
- proj_in: bfloat16 [4096, 32], P('proj'), may hold values from -0.09375 to 0.09375
- proj_out: bfloat16 [14336, 32], P('proj'), may hold values from -0.046875 to 0.046875
- lengths: int32 [16, 17], P(('grp', 'dp', 'query')), parts along dimension 0, may hold values from 1 to 128, 512 in all within a row
- queries: float32 [2, 512, 1024], P('query', 'dp'), may hold values from -6 to 6
Outputs:
- scores: float32 [256, 1024], P(('grp', 'dp'), 'query'), parts along dimension 0
The draws below stay inside these ranges and needn't reach their ends.
There are 2 independent parts, one for each index of `grp`. The reference program is written for one: setup_inputs(seed, part) draws one part's arguments, and reference() takes and returns one part's arrays. A program takes and returns all parts, laid end to end along the dimension named above; an argument that names none is the same for every part. Nothing has to cross between parts.
Inputs may be any that keep to these rules, and one draw needn't show every extreme that they name: `lengths`: each row sums to 512; some entry equals 128.
All inputs are finite; a program needn't handle non-finite values.
Results may differ from the reference program's by a relative error of at most 0.0003.
Values sent between devices are 32-bit elements; how exact they have to be, the bound alone decides.
No kernel may reach another device: no remote copies, remote signals or barrier semaphores. Data moves between devices by JAX's collectives and lax.ppermute only.
A program may use at most 64 MiB of HBM per device.

```python
import math
import jax
import jax.numpy as jnp
import numpy as np
from jax import lax

D = 4096
FF = 14336
R = 32
TOK_DEV = 512
EX_DEV = 16
QDEV = 128
TOKENS = 4096
N_DP = 4
N_QUERY = 2


def spiked(background, key, rows, columns):
    direction_key, loading_key = jax.random.split(key)
    directions = jax.random.normal(direction_key, (4, columns), jnp.float32)
    strengths = jnp.array([1.0, 0.7, 0.5, 0.35], jnp.float32)
    loadings = jax.random.normal(loading_key, (rows, 4), jnp.float32) * strengths[None, :]
    summed = background
    for column in range(4):
        summed = summed + loadings[:, column:column + 1] * directions[column][None, :]
    return summed.astype(jnp.bfloat16)


def leading(background, key, block_rows, lead_scale):
    total_rows, columns = background.shape
    blocks = total_rows // block_rows
    direction_key, loading_key, shift_key, pick_key = jax.random.split(key, 4)
    directions = jax.random.normal(direction_key, (4, columns), jnp.float32)
    shifts = jax.random.normal(shift_key, (blocks, columns), jnp.float32) * 0.05
    chosen = jax.random.permutation(pick_key, blocks)
    active = jnp.where(chosen < blocks // 2, 1.0, 0.0).astype(jnp.float32)
    strengths = jnp.array([1.0, 0.7, 0.5, 0.35], jnp.float32)
    loadings = jax.random.normal(loading_key, (total_rows, 4), jnp.float32)
    summed = background
    for column in range(1, 4):
        summed = summed + loadings[:, column:column + 1] * strengths[column] * directions[column][None, :]
    lead_part = (loadings[:, 0] * lead_scale).reshape(blocks, block_rows, 1) * active[:, None, None]
    tilted = (directions[0][None, :] + shifts)[:, None, :]
    summed = summed.reshape(blocks, block_rows, columns) + lead_part * tilted
    return summed.reshape(total_rows, columns).astype(jnp.bfloat16)


def draw_activations(key, part):
    key = jax.random.fold_in(key, 11)
    background_key, rest_key = jax.random.split(key)
    background = jax.random.normal(background_key, (TOKENS, D), jnp.float32)
    return leading(background, rest_key, TOK_DEV, 20.0)


def draw_out_grads(key, part):
    key = jax.random.fold_in(key, 23)
    background_key, rest_key = jax.random.split(key)
    background = jax.random.normal(background_key, (TOKENS, FF), jnp.float32)
    return spiked(background, rest_key, TOKENS, FF)


def level_of(key, shape, cuts, smallest, high):
    def one(position, parts):
        steps = jax.random.uniform(jax.random.fold_in(jax.random.fold_in(key, 6), position), (parts,), jnp.float32, smallest / len(cuts), high / len(cuts))
        return jnp.repeat(jnp.exp(steps), shape[position] // parts).reshape((-1,) + (1,) * (len(shape) - position - 1))

    loudness = one(*cuts[0])
    for cut in cuts[1:]:
        loudness = loudness * one(*cut)
    return loudness


def split_up(count, total, bound, skew):
    portions = [(1 << 20) // math.isqrt(rank ** skew) + 1 for rank in range(2, count + 1)]
    spare, holding = total - bound - (count - 1), [1] * (count - 1)
    while spare > 0:
        candidates = [i for i in range(count - 1) if holding[i] < bound]
        pool, budget = sum([portions[i] for i in candidates]), spare
        for i in candidates:
            more = min(bound - holding[i], max(1, budget * portions[i] // pool), spare)
            holding[i] = holding[i] + more
            spare = spare - more
    return np.array([bound] + holding)


def ragged_sizes(own_key, number_of, total, most, lean):
    if number_of == 2:
        one = jax.random.randint(own_key, (), max(1, total - most), min(most, total - 1) + 1)
        return jnp.stack([one, total - one])
    sizes = jnp.asarray(split_up(number_of, total, most, lean), jnp.int32)
    pairs = (number_of - 1) // 2
    source_of, receiver = sizes[1:1 + 2 * pairs:2], sizes[2:2 + 2 * pairs:2]
    slack = jnp.minimum(source_of - 1, most - receiver)
    passed = jax.random.randint(jax.random.fold_in(own_key, 1), (pairs,), 0, 1 << 20) % (slack + 1)
    sizes = sizes.at[1:1 + 2 * pairs:2].set(source_of - passed).at[2:2 + 2 * pairs:2].set(receiver + passed)
    return sizes[jax.random.permutation(jax.random.fold_in(own_key, 2), number_of)]


def normal_values(own_key, shape, scale, limit, shards=(), held_as=jnp.bfloat16):
    values = jax.random.normal(own_key, shape, jnp.float32) * scale
    if len(shards) > 0:
        values = level_of(own_key, shape, shards, -0.22, 0.18) * values
    return jnp.clip(values, min=-limit, max=limit).astype(held_as)


def setup_inputs(seed: int = 0, part: int = 0) -> dict:
    key_list = jax.random.split(jax.random.key(seed), 7)
    part_splits = jax.random.split(jax.random.fold_in(key_list[6], part), 7)
    return {
        "activations": draw_activations(jax.random.fold_in(jax.random.fold_in(key_list[6], part), 71), part),
        "out_grads": draw_out_grads(jax.random.fold_in(jax.random.fold_in(key_list[6], part), 71), part),
        "proj_in": normal_values(key_list[2], (D, R), D ** -0.5, 0.09375, ((0, 2),)),
        "proj_out": normal_values(key_list[3], (FF, R), FF ** -0.5, 0.046875, ((0, 2),)),
        "lengths": jax.vmap(lambda own: ragged_sizes(own, EX_DEV + 1, TOK_DEV, TOK_DEV // 4, 2))(jax.random.split(part_splits[4], (N_DP * N_QUERY))).reshape((N_DP * N_QUERY, EX_DEV + 1)).astype(jnp.int32),
        "queries": normal_values(key_list[5], (N_QUERY, N_DP * QDEV, R * R), 1.0, 6.0, ((0, 2), (1, 4)), jnp.float32),
    }


def membership(lengths, slots):
    counts = lengths[:, :-1]
    ends = jnp.cumsum(counts, axis=1)
    starts = ends - counts
    positions = jnp.arange(slots, dtype=jnp.int32)
    inside = (positions[None, None, :] >= starts[:, :, None]) & (positions[None, None, :] < ends[:, :, None])
    member = inside.astype(jnp.float32)
    live = jnp.sum(member, axis=1)
    return (member, live, counts.astype(jnp.float32))

def precondition(input_fisher, output_fisher, grads):
    width = input_fisher.shape[0]
    identity = jnp.eye(width, dtype=jnp.float32)

    def inverse(fisher):
        scaled = fisher * (width / jnp.trace(fisher)) + 1.0 * identity
        factor = jnp.linalg.cholesky(scaled)
        return jax.scipy.linalg.cho_solve((factor, True), identity)
    in_inverse = inverse(input_fisher)
    out_inverse = inverse(output_fisher)
    left_side = jnp.einsum('ik,nkl->nil', out_inverse, grads, precision=lax.Precision.HIGHEST)
    both_sides = jnp.einsum('nil,lj->nij', left_side, in_inverse, precision=lax.Precision.HIGHEST)
    return both_sides.reshape(grads.shape[0], width * width)

def reference(activations, out_grads, proj_in, proj_out, lengths, queries):
    width = proj_in.shape[1]
    groups = lengths.shape[0]
    input_proj = jnp.dot(activations.astype(jnp.float32), proj_in.astype(jnp.float32), preferred_element_type=jnp.float32)
    output_proj = jnp.dot(out_grads.astype(jnp.float32), proj_out.astype(jnp.float32), preferred_element_type=jnp.float32)
    member, live, counts = membership(lengths, TOK_DEV)
    input_blocks = input_proj.reshape(groups, TOK_DEV, width)
    output_blocks = output_proj.reshape(groups, TOK_DEV, width)
    outer = (output_blocks[:, :, :, None] * input_blocks[:, :, None, :]).reshape(groups, TOK_DEV, width * width)
    summed = jnp.einsum('get,gtk->gek', member, outer, precision=lax.Precision.HIGHEST)
    example_grads = (summed / counts[:, :, None]).reshape(-1, width * width)
    masked_in = input_blocks * live[:, :, None]
    masked_out = output_blocks * live[:, :, None]
    input_fisher = jnp.einsum('gti,gtj->ij', masked_in, input_blocks, precision=lax.Precision.HIGHEST)
    output_fisher = jnp.einsum('gti,gtj->ij', masked_out, output_blocks, precision=lax.Precision.HIGHEST)
    conditioned = precondition(input_fisher, output_fisher, queries.reshape(-1, width, width))
    scores = jnp.einsum('ek,nk->en', example_grads, conditioned, precision=lax.Precision.HIGHEST) / width
    return scores
```

```python
import functools

import jax
import jax.numpy as jnp
from jax import lax
from jax.experimental import pallas as pl
from jax.experimental.pallas import tpu as pltpu
from jax.sharding import PartitionSpec as P

F32 = jnp.float32
BF16 = jnp.bfloat16
HIGHEST = lax.Precision.HIGHEST
NT = (((1,), (1,)), ((), ()))
AXES = ("dp", "query", "proj")
MIB = 2**20


def swap(value, mesh, mask):
    count = mesh.shape["dp"] * mesh.shape["query"] * mesh.shape["proj"]
    return lax.ppermute(value, AXES, [(i, i ^ mask) for i in range(count)])


def bits_of(size):
    return [1 << b for b in range(size.bit_length() - 1)]


def project_kernel(plan, a_hbm, g_hbm, p_in_hbm, p_out_hbm, out_ref, a_buf, g_buf, p_in, p_out, sems, p_sems):
    width = p_in.shape[0]
    p_copies = {
        "a": pltpu.make_async_copy(p_in_hbm, p_in, p_sems.at[0]),
        "g": pltpu.make_async_copy(p_out_hbm, p_out, p_sems.at[1]),
    }
    source, buffer, proj = {"a": a_hbm, "g": g_hbm}, {"a": a_buf, "g": g_buf}, {"a": p_in, "g": p_out}
    steps, seen = [], set()
    for i, (name, start, size) in enumerate(plan):
        cols = pl.ds(start, size)
        copy = pltpu.make_async_copy(source[name].at[:, cols], buffer[name].at[:, cols], sems.at[i])
        if name not in seen:
            seen.add(name)
            p_copies[name].start()
        copy.start()
        steps.append((name, slice(start, start + size), copy))
    waited, total = set(), {}
    for name, cols, copy in steps:
        if name not in waited:
            waited.add(name)
            p_copies[name].wait()
        copy.wait()
        part = lax.dot_general(proj[name][:, cols], buffer[name][:, cols], NT, preferred_element_type=F32)
        total[name] = part if name not in total else total[name] + part
    out_ref[0:width, :] = total["a"]
    out_ref[width : 2 * width, :] = total["g"]


def project(activations, out_grads, proj_in, proj_out):
    slots, d = activations.shape
    ff = out_grads.shape[1]
    width = proj_in.shape[1]
    quarter = ff // 4
    plan = tuple(("g", i * quarter, quarter) for i in range(4)) + (("a", 0, d),)
    return pl.pallas_call(
        functools.partial(project_kernel, plan),
        out_shape=jax.ShapeDtypeStruct((2 * width, slots), F32),
        in_specs=[pl.BlockSpec(memory_space=pl.ANY)] * 4,
        out_specs=pl.BlockSpec(memory_space=pltpu.VMEM),
        scratch_shapes=[
            pltpu.VMEM((slots, d), BF16),
            pltpu.VMEM((slots, ff), BF16),
            pltpu.VMEM((width, d), BF16),
            pltpu.VMEM((width, ff), BF16),
            pltpu.SemaphoreType.DMA((len(plan),)),
            pltpu.SemaphoreType.DMA((2,)),
        ],
        compiler_params=pltpu.CompilerParams(vmem_limit_bytes=60 * MIB),
        name="project",
    )(activations, out_grads, proj_in.T, proj_out.T)


def fisher_kernel(lengths_ref, own_ref, other_ref, out_ref):
    width = out_ref.shape[0]
    both = own_ref[...] + other_ref[...]
    live_slots = lax.fori_loop(0, lengths_ref.shape[1] - 1, lambda e, n: n + lengths_ref[0, e], jnp.int32(0))
    slot = lax.broadcasted_iota(jnp.int32, both.shape, 1)
    live = jnp.where(slot < live_slots, both, 0.0)
    gram = lax.dot_general(live, both, NT, precision=HIGHEST, preferred_element_type=F32)
    out_ref[...] = jnp.zeros_like(out_ref)
    out_ref[:, 0:width] = gram[0:width, 0:width]
    out_ref[:, width : 2 * width] = gram[width : 2 * width, width : 2 * width]


def fisher(lengths, own, other):
    width = own.shape[0] // 2
    return pl.pallas_call(
        fisher_kernel,
        out_shape=jax.ShapeDtypeStruct((width, 128), F32),
        in_specs=[pl.BlockSpec(memory_space=pltpu.SMEM)] + [pl.BlockSpec(memory_space=pltpu.VMEM)] * 2,
        out_specs=pl.BlockSpec(memory_space=pltpu.VMEM),
        name="fisher",
    )(lengths, own, other)


def split3(value):
    high = value.astype(BF16)
    rest = value - high.astype(F32)
    middle = rest.astype(BF16)
    return high, middle, (rest - middle.astype(F32)).astype(BF16)


def examples_kernel(lengths_ref, own_ref, other_ref, out_ref):
    examples = out_ref.shape[0]
    width = own_ref.shape[0] // 2
    slots = own_ref.shape[1]
    both = own_ref[...] + other_ref[...]
    inputs, outputs = both[0:width], both[width : 2 * width]
    index = lax.broadcasted_iota(jnp.int32, (examples, 1), 0)
    starts = jnp.zeros((examples, 1), jnp.int32)
    counts = jnp.zeros((examples, 1), jnp.int32)
    begin = jnp.int32(0)
    for e in range(examples):
        length = lengths_ref[0, e]
        starts = jnp.where(index == e, begin, starts)
        counts = jnp.where(index == e, length, counts)
        begin = begin + length
    slot = lax.broadcasted_iota(jnp.int32, (examples, slots), 1)
    member = jnp.where((slot >= starts) & (slot < starts + counts), 1.0, 0.0).astype(BF16)
    divisor = counts.astype(F32)
    group = 8
    for first in range(0, width, group):
        outer = jnp.concatenate([outputs[i : i + 1] * inputs for i in range(first, first + group)], axis=0)
        total = None
        for piece in reversed(split3(outer)):
            part = lax.dot_general(member, piece, NT, preferred_element_type=F32)
            total = part if total is None else total + part
        out_ref[:, first * width : (first + group) * width] = total / divisor


def example_grads(lengths, own, other):
    width = own.shape[0] // 2
    return pl.pallas_call(
        examples_kernel,
        out_shape=jax.ShapeDtypeStruct((lengths.shape[1] - 1, width * width), F32),
        in_specs=[pl.BlockSpec(memory_space=pltpu.SMEM)] + [pl.BlockSpec(memory_space=pltpu.VMEM)] * 2,
        out_specs=pl.BlockSpec(memory_space=pltpu.VMEM),
        name="examples",
    )(lengths, own, other)


def arrange_examples_kernel(n_query, blocks_ref, out_ref, rows):
    blocks, examples, columns = blocks_ref.shape
    query = lax.axis_index("query")
    for b in range(blocks):
        place = (b // n_query) * n_query + (query ^ (b % n_query))
        rows[pl.ds(pl.multiple_of(place * examples, 8), examples), :] = blocks_ref[b]
    for c in range(0, columns, 128):
        out_ref[c : c + 128, :] = rows[:, c : c + 128].T


def arrange_examples(blocks, n_query):
    count, examples, columns = blocks.shape
    return pl.pallas_call(
        functools.partial(arrange_examples_kernel, n_query),
        out_shape=jax.ShapeDtypeStruct((columns, count * examples), F32),
        in_specs=[pl.BlockSpec(memory_space=pltpu.VMEM)],
        out_specs=pl.BlockSpec(memory_space=pltpu.VMEM),
        scratch_shapes=[pltpu.VMEM((count * examples, columns), F32)],
        name="arrange_examples",
    )(blocks)


def split_queries_kernel(low_dp, own_ref, *refs):
    same_refs, other_refs, (high_ref, low_ref) = refs[: low_dp - 1], refs[low_dp - 1 : -2], refs[-2:]
    rows = own_ref.shape[1]
    half = rows // 2
    place = lax.axis_index("dp") % low_dp
    core = lax.axis_index("proj")

    def put(start, value):
        at = pl.ds(pl.multiple_of(start, 16), value.shape[0])
        high = value.astype(BF16)
        high_ref[at, :] = high
        low_ref[at, :] = (value - high.astype(F32)).astype(BF16)

    put(place * rows, own_ref[0])
    for r in range(1, low_dp):
        put((place ^ r) * rows + core * half, same_refs[r - 1][...])
        put((place ^ r) * rows + (1 - core) * half, other_refs[r - 1][...])


def split_queries(low_dp, own, same, other):
    rows, columns = own.shape[1:]
    shape = jax.ShapeDtypeStruct((low_dp * rows, columns), BF16)
    return pl.pallas_call(
        functools.partial(split_queries_kernel, low_dp),
        out_shape=(shape, shape),
        in_specs=[pl.BlockSpec(memory_space=pltpu.VMEM)] * (1 + len(same) + len(other)),
        out_specs=(pl.BlockSpec(memory_space=pltpu.VMEM),) * 2,
        name="split_queries",
    )(own, *same, *other)


def inverse_tiled(fisher_sum):
    width = fisher_sum.shape[0]
    row = lax.broadcasted_iota(jnp.int32, (width, width), 0)
    column = lax.broadcasted_iota(jnp.int32, (width, width), 1)
    trace = jnp.sum(jnp.where(row == column, fisher_sum, 0.0), keepdims=True)
    damped = fisher_sum * (width / trace) + jnp.where(row == column, 1.0, 0.0)
    state = jnp.concatenate([damped] * (128 // width), axis=1)
    lane = lax.broadcasted_iota(jnp.int32, state.shape, 1) % width
    sublane = lax.broadcasted_iota(jnp.int32, state.shape, 0)
    for k in range(width):
        scale = 1.0 / state[k : k + 1, k : k + 1]
        pivot_row = jnp.where(lane[0:1] == k, 1.0, state[k : k + 1, :]) * scale
        pivot_column = jnp.where(sublane == k, 0.0, jnp.broadcast_to(state[:, k : k + 1], state.shape))
        cleared = jnp.where(lane == k, 0.0, state)
        state = jnp.where(sublane == k, pivot_row, cleared - pivot_column * pivot_row)
    return state


def block_diagonal(tiled):
    width, lanes = tiled.shape
    size = 256
    value = jnp.concatenate([jnp.concatenate([tiled] * (size // lanes), axis=1)] * (size // width), axis=0)
    row = lax.broadcasted_iota(jnp.int32, (size, size), 0) // width
    column = lax.broadcasted_iota(jnp.int32, (size, size), 1) // width
    return jnp.where(row == column, value, 0.0)


def score_kernel(own_ref, other_ref, examples_ref, high_ref, low_ref, mine_ref, theirs_ref, turn, back):
    width = own_ref.shape[0]
    total = own_ref[...] + other_ref[...]
    in_blocks = block_diagonal(inverse_tiled(total[:, 0:width]))
    out_blocks = block_diagonal(inverse_tiled(total[:, width : 2 * width]))
    size = in_blocks.shape[0]
    rows, count = examples_ref.shape
    for c in range(0, rows, size):
        turn[c : c + size, :] = jnp.dot(in_blocks, examples_ref[c : c + size, :], precision=HIGHEST, preferred_element_type=F32)
    for c in range(0, rows, size):
        block = jnp.concatenate(
            [turn[pl.ds(j, width, stride=width), :] for j in range(c // width, (c + size) // width)], axis=0
        )
        back[c : c + size, :] = jnp.dot(out_blocks, block, precision=HIGHEST, preferred_element_type=F32)
    conditioned = jnp.concatenate([back[pl.ds(i, width, stride=width), :] for i in range(width)], axis=0)
    high = conditioned.astype(BF16)
    low = (conditioned - high.astype(F32)).astype(BF16)
    scores = (
        jnp.dot(low_ref[...], high, preferred_element_type=F32)
        + jnp.dot(high_ref[...], low, preferred_element_type=F32)
        + jnp.dot(high_ref[...], high, preferred_element_type=F32)
    )
    scores = (scores * (1.0 / width)).T
    mine_ref[...] = scores[0 : count // 2]
    theirs_ref[...] = scores[count // 2 : count]


def score(own, other, examples, high, low):
    rows, count = examples.shape
    shape = jax.ShapeDtypeStruct((count // 2, high.shape[0]), F32)
    return pl.pallas_call(
        score_kernel,
        out_shape=(shape, shape),
        in_specs=[pl.BlockSpec(memory_space=pltpu.VMEM)] * 5,
        out_specs=(pl.BlockSpec(memory_space=pltpu.VMEM),) * 2,
        scratch_shapes=[pltpu.VMEM((rows, count), F32)] * 2,
        compiler_params=pltpu.CompilerParams(vmem_limit_bytes=40 * MIB),
        name="score",
    )(own, other, examples, high, low)


def body(mesh, activations, out_grads, proj_in, proj_out, lengths, queries):
    n_dp, n_query = mesh.shape["dp"], mesh.shape["query"]
    core_bit = 1
    query_bits = [2 * b for b in bits_of(n_query)]
    dp_bits = [2 * n_query * b for b in bits_of(n_dp)]
    low_bits, top_bit = dp_bits[:-1], dp_bits[-1]
    low_dp = n_dp // 2

    own = project(activations, out_grads, proj_in, proj_out)
    other = swap(own, mesh, core_bit)

    half = queries.shape[1] // 2
    mine = lax.dynamic_slice_in_dim(queries[0], lax.axis_index("proj") * half, half, 0)
    halves = [mine]
    for bit in low_bits:
        halves = halves + [swap(h, mesh, bit) for h in halves]
    same = halves[1:]
    other_half = [swap(h, mesh, core_bit) for h in same]

    factor = fisher(lengths, own, other)
    blocks = example_grads(lengths, own, other)[None]
    bits = query_bits + dp_bits
    for bit in bits[:-1]:
        factor = factor + swap(factor, mesh, bit | core_bit)
    factor_other = swap(factor, mesh, bits[-1] | core_bit)
    for bit in query_bits + [top_bit]:
        blocks = jnp.concatenate([blocks, swap(blocks, mesh, bit | core_bit)], axis=0)

    examples = arrange_examples(blocks, n_query)
    high, low = split_queries(low_dp, queries, same, other_half)
    kept, sent = score(factor, factor_other, examples, high, low)
    received = swap(sent, mesh, top_bit | core_bit)
    upper = lax.axis_index("dp") >= low_dp
    return jnp.concatenate([jnp.where(upper, received, kept), jnp.where(upper, kept, received)], axis=1)


def solution(mesh):
    in_specs = (
        P(("grp", "dp", "query"), "proj"),
        P(("grp", "dp", "query"), "proj"),
        P("proj", None),
        P("proj", None),
        P(("grp", "dp", "query"), None),
        P("query", "dp", None),
    )
    out_specs = P(("grp", "dp"), "query")
    return jax.shard_map(
        functools.partial(body, mesh), mesh=mesh, in_specs=in_specs, out_specs=out_specs, check_vma=False
    )
```

```python
import functools
import math

import jax
import jax.numpy as jnp
from jax import lax
from jax.experimental import pallas as pl
from jax.experimental.pallas import tpu as pltpu
from jax.sharding import PartitionSpec as P

F32 = jnp.float32
BF16 = jnp.bfloat16
HIGHEST = lax.Precision.HIGHEST
NT = (((1,), (1,)), ((), ()))
AXES = ("dp", "query", "proj")
MIB = 2**20
CHUNK = 256
QUERY_STEP = 1


def swap(value, mesh, mask):
    count = math.prod(mesh.shape[axis] for axis in AXES)
    return lax.ppermute(value, AXES, [(i, i ^ mask) for i in range(count)])


def bits_of(size):
    return [1 << b for b in range(size.bit_length() - 1)]


def pick_kernel(queries_hbm, half_ref, sem):
    half = half_ref.shape[0]
    start = pl.multiple_of(lax.axis_index("proj") * half, 8)
    copy = pltpu.make_async_copy(queries_hbm.at[0, pl.ds(start, half)], half_ref, sem)
    copy.start()
    copy.wait()


def pick_queries(queries):
    rows, columns = queries.shape[1:]
    return pl.pallas_call(
        pick_kernel,
        out_shape=jax.ShapeDtypeStruct((rows // 2, columns), F32),
        in_specs=[pl.BlockSpec(memory_space=pl.ANY)],
        out_specs=pl.BlockSpec(memory_space=pltpu.VMEM),
        scratch_shapes=[pltpu.SemaphoreType.DMA],
        compiler_params=pltpu.CompilerParams(vmem_limit_bytes=4 * MIB),
        cost_estimate=pl.CostEstimate(flops=4 * 10**9, bytes_accessed=10**6, transcendentals=0),
        name="pick_queries",
    )(pltpu.with_memory_space_constraint(queries, pltpu.HBM))


def project_kernel(a_ref, g_ref, p_in_ref, p_out_ref, after_ref, out_ref):
    width = p_in_ref.shape[0]
    out_ref[0:width, :] = lax.dot_general(p_in_ref[...], a_ref[...], NT, preferred_element_type=F32)
    out_ref[width : 2 * width, :] = lax.dot_general(p_out_ref[...], g_ref[...], NT, preferred_element_type=F32)


def project(activations, out_grads, proj_in, proj_out, after):
    return pl.pallas_call(
        project_kernel,
        out_shape=jax.ShapeDtypeStruct((2 * proj_in.shape[1], activations.shape[0]), F32),
        in_specs=[pl.BlockSpec(memory_space=pltpu.VMEM)] * 4 + [pl.BlockSpec(memory_space=pl.ANY)],
        out_specs=pl.BlockSpec(memory_space=pltpu.VMEM),
        compiler_params=pltpu.CompilerParams(vmem_limit_bytes=16 * MIB),
        name="project",
    )(activations, out_grads, proj_in.T, proj_out.T, after)


def fisher_kernel(lengths_ref, own_ref, other_ref, out_ref):
    width = out_ref.shape[0]
    both = own_ref[...] + other_ref[...]
    live_slots = lax.fori_loop(0, lengths_ref.shape[1] - 1, lambda e, n: n + lengths_ref[0, e], jnp.int32(0))
    slot = lax.broadcasted_iota(jnp.int32, both.shape, 1)
    live = jnp.where(slot < live_slots, both, 0.0)
    gram = lax.dot_general(live, both, NT, precision=HIGHEST, preferred_element_type=F32)
    out_ref[...] = jnp.zeros_like(out_ref)
    out_ref[:, 0:width] = gram[0:width, 0:width]
    out_ref[:, width : 2 * width] = gram[width : 2 * width, width : 2 * width]


def fisher(lengths, own, other):
    width = own.shape[0] // 2
    return pl.pallas_call(
        fisher_kernel,
        out_shape=jax.ShapeDtypeStruct((width, 128), F32),
        in_specs=[pl.BlockSpec(memory_space=pltpu.SMEM)] + [pl.BlockSpec(memory_space=pltpu.VMEM)] * 2,
        out_specs=pl.BlockSpec(memory_space=pltpu.VMEM),
        compiler_params=pltpu.CompilerParams(vmem_limit_bytes=8 * MIB),
        name="fisher",
    )(lengths, own, other)


def split3(value):
    high = value.astype(BF16)
    rest = value - high.astype(F32)
    middle = rest.astype(BF16)
    return high, middle, (rest - middle.astype(F32)).astype(BF16)


def examples_kernel(lengths_ref, own_ref, other_ref, out_ref):
    examples = out_ref.shape[0]
    width = own_ref.shape[0] // 2
    slots = own_ref.shape[1]
    both = own_ref[...] + other_ref[...]
    inputs, outputs = both[0:width], both[width : 2 * width]
    index = lax.broadcasted_iota(jnp.int32, (examples, 1), 0)
    starts = jnp.zeros((examples, 1), jnp.int32)
    counts = jnp.zeros((examples, 1), jnp.int32)
    begin = jnp.int32(0)
    for e in range(examples):
        length = lengths_ref[0, e]
        starts = jnp.where(index == e, begin, starts)
        counts = jnp.where(index == e, length, counts)
        begin = begin + length
    slot = lax.broadcasted_iota(jnp.int32, (examples, slots), 1)
    member = jnp.where((slot >= starts) & (slot < starts + counts), 1.0, 0.0).astype(BF16)
    divisor = counts.astype(F32)
    group = 8
    for first in range(0, width, group):
        outer = jnp.concatenate([outputs[i : i + 1] * inputs for i in range(first, first + group)], axis=0)
        total = None
        for piece in reversed(split3(outer)):
            part = lax.dot_general(member, piece, NT, preferred_element_type=F32)
            total = part if total is None else total + part
        out_ref[:, first * width : (first + group) * width] = total / divisor


def example_grads(lengths, own, other):
    width = own.shape[0] // 2
    return pl.pallas_call(
        examples_kernel,
        out_shape=jax.ShapeDtypeStruct((lengths.shape[1] - 1, width * width), F32),
        in_specs=[pl.BlockSpec(memory_space=pltpu.SMEM)] + [pl.BlockSpec(memory_space=pltpu.VMEM)] * 2,
        out_specs=pl.BlockSpec(memory_space=pltpu.VMEM),
        compiler_params=pltpu.CompilerParams(vmem_limit_bytes=8 * MIB),
        cost_estimate=pl.CostEstimate(flops=2 * 10**9, bytes_accessed=10**6, transcendentals=0),
        name="examples",
    )(lengths, own, other)


def split2(value):
    high = value.astype(BF16)
    return high, (value - high.astype(F32)).astype(BF16)


def turn_pairs(load, scratch, width):
    columns, count = scratch.shape
    for c in range(columns // CHUNK):
        scratch[c * CHUNK : (c + 1) * CHUNK, :] = load(c).T
    chunks = []
    for c in range(columns // CHUNK):
        lines = range(c * CHUNK // width, (c + 1) * CHUNK // width)
        chunks.append(jnp.concatenate([scratch[pl.ds(j, width, stride=width), :] for j in lines], axis=0).T)
    return jnp.concatenate(chunks, axis=0)


def arrange_examples_kernel(n_query, blocks_ref, *refs):
    out_refs, (rows, scratch) = refs[:-2], refs[-2:]
    blocks, examples, columns = blocks_ref.shape
    query = lax.axis_index("query")
    for b in range(blocks):
        place = (b // n_query) * n_query + (query ^ (b % n_query))
        rows[pl.ds(pl.multiple_of(place * examples, 8), examples), :] = blocks_ref[b]
    width = math.isqrt(columns)
    turned = turn_pairs(lambda c: rows[:, c * CHUNK : (c + 1) * CHUNK], scratch, width)
    for out_ref, piece in zip(out_refs, split3(turned)):
        out_ref[...] = piece


def arrange_examples(blocks, n_query):
    number, examples, columns = blocks.shape
    count = number * examples
    shape = jax.ShapeDtypeStruct((count * columns // CHUNK, CHUNK), BF16)
    return pl.pallas_call(
        functools.partial(arrange_examples_kernel, n_query),
        out_shape=(shape,) * 3,
        in_specs=[pl.BlockSpec(memory_space=pltpu.VMEM)],
        out_specs=(pl.BlockSpec(memory_space=pltpu.VMEM),) * 3,
        scratch_shapes=[pltpu.VMEM((count, columns), F32), pltpu.VMEM((columns, count), F32)],
        compiler_params=pltpu.CompilerParams(vmem_limit_bytes=12 * MIB),
        name="arrange_examples",
    )(blocks)


def split_queries_kernel(bits, own_ref, *refs):
    parts = 1 << len(bits)
    same_refs, other_refs, (high_ref, low_ref) = refs[: parts - 1], refs[parts - 1 : -2], refs[-2:]
    rows = own_ref.shape[1]
    half = rows // 2
    dp, core = lax.axis_index("dp"), lax.axis_index("proj")
    place = sum(((dp // bit) % 2) << b for b, bit in enumerate(bits))

    def put(start, value):
        at = pl.ds(pl.multiple_of(start, 16), value.shape[0])
        high_ref[at, :], low_ref[at, :] = split2(value)

    put(place * rows, own_ref[0])
    for r in range(1, parts):
        put((place ^ r) * rows + core * half, same_refs[r - 1][...])
        put((place ^ r) * rows + (1 - core) * half, other_refs[r - 1][...])


def split_queries(bits, own, same, other):
    parts = 1 + len(same)
    rows, columns = own.shape[1:]
    shape = jax.ShapeDtypeStruct((parts * rows, columns), BF16)
    return pl.pallas_call(
        functools.partial(split_queries_kernel, bits),
        out_shape=(shape, shape),
        in_specs=[pl.BlockSpec(memory_space=pltpu.VMEM)] * (1 + len(same) + len(other)),
        out_specs=(pl.BlockSpec(memory_space=pltpu.VMEM),) * 2,
        compiler_params=pltpu.CompilerParams(vmem_limit_bytes=(4 + 2 * parts) * MIB),
        name="split_queries",
    )(own, *same, *other)


def inverse_tiled(fisher_sum):
    width = fisher_sum.shape[0]
    row = lax.broadcasted_iota(jnp.int32, (width, width), 0)
    column = lax.broadcasted_iota(jnp.int32, (width, width), 1)
    trace = jnp.sum(jnp.where(row == column, fisher_sum, 0.0), keepdims=True)
    damped = fisher_sum * (width / trace) + jnp.where(row == column, 1.0, 0.0)
    state = jnp.concatenate([damped] * (128 // width), axis=1)
    lane = lax.broadcasted_iota(jnp.int32, state.shape, 1) % width
    sublane = lax.broadcasted_iota(jnp.int32, state.shape, 0)
    top = lane[0:1]

    def apply(m, x, y):
        return m[0][0] * x + m[0][1] * y, m[1][0] * x + m[1][1] * y

    def invert(m):
        scale = 1.0 / (m[0][0] * m[1][1] - m[0][1] * m[1][0])
        return (m[1][1] * scale, -m[0][1] * scale), (-m[1][0] * scale, m[0][0] * scale)

    for k in range(0, width, 4):
        columns = [jnp.broadcast_to(state[:, k + c : k + c + 1], state.shape) for c in range(4)]
        pivot = [[columns[c][k + r : k + r + 1, :] for c in range(4)] for r in range(4)]
        inside = (top >= k) & (top < k + 4)
        rows = [
            jnp.where(top == k + r, 1.0, jnp.where(inside, 0.0, state[k + r : k + r + 1, :])) for r in range(4)
        ]
        corner = invert((pivot[0][0:2], pivot[1][0:2]))
        upper = apply(corner, rows[0], rows[1])
        right = [apply(corner, pivot[0][c], pivot[1][c]) for c in (2, 3)]
        schur = [
            [pivot[r][c] - pivot[r][0] * right[c - 2][0] - pivot[r][1] * right[c - 2][1] for c in (2, 3)] for r in (2, 3)
        ]
        lower = apply(
            invert(schur), *(rows[r] - pivot[r][0] * upper[0] - pivot[r][1] * upper[1] for r in (2, 3))
        )
        solved = [upper[r] - right[0][r] * lower[0] - right[1][r] * lower[1] for r in range(2)] + list(lower)
        change = columns[0] * solved[0] + columns[1] * solved[1] + columns[2] * solved[2] + columns[3] * solved[3]
        state = jnp.where((lane >= k) & (lane < k + 4), 0.0, state) - change
        for r in range(4):
            state = jnp.where(sublane == k + r, solved[r], state)
    return state


def block_diagonal(tiled):
    width, lanes = tiled.shape
    value = jnp.concatenate([jnp.concatenate([tiled] * (CHUNK // lanes), axis=1)] * (CHUNK // width), axis=0)
    row = lax.broadcasted_iota(jnp.int32, (CHUNK, CHUNK), 0) // width
    column = lax.broadcasted_iota(jnp.int32, (CHUNK, CHUNK), 1) // width
    return jnp.where(row == column, value, 0.0)


def inverses_kernel(own_ref, other_ref, in_ref, out_ref):
    width = own_ref.shape[0]
    total = own_ref[...] + other_ref[...]
    for ref, fisher_sum in ((in_ref, total[:, 0:width]), (out_ref, total[:, width : 2 * width])):
        for piece, value in enumerate(split3(block_diagonal(inverse_tiled(fisher_sum)))):
            ref[piece] = value


def inverses(own, other):
    shape = jax.ShapeDtypeStruct((3, CHUNK, CHUNK), BF16)
    return pl.pallas_call(
        inverses_kernel,
        out_shape=(shape, shape),
        in_specs=[pl.BlockSpec(memory_space=pltpu.VMEM)] * 2,
        out_specs=(pl.BlockSpec(memory_space=pltpu.VMEM),) * 2,
        compiler_params=pltpu.CompilerParams(vmem_limit_bytes=8 * MIB),
        name="inverses",
    )(own, other)


def times_blocks(high, middle, low, blocks_ref):
    rows = high.shape[0]
    by_high = jnp.dot(jnp.concatenate([high, middle, low], axis=0), blocks_ref[0], preferred_element_type=F32)
    by_middle = jnp.dot(jnp.concatenate([high, middle], axis=0), blocks_ref[1], preferred_element_type=F32)
    by_low = jnp.dot(high, blocks_ref[2], preferred_element_type=F32)
    small = by_high[2 * rows :] + by_middle[rows:] + by_low
    return by_high[0:rows] + (by_high[rows : 2 * rows] + by_middle[0:rows] + small)


def score_kernel(high_ref, middle_ref, low_ref, in_ref, out_ref, q_high_ref, q_low_ref, mine_ref, theirs_ref, scratch):
    columns, count = scratch.shape
    width = math.isqrt(columns)
    left = times_blocks(high_ref[...], middle_ref[...], low_ref[...], out_ref)
    turned = turn_pairs(lambda c: left[c * count : (c + 1) * count], scratch, width)
    high, low = split2(times_blocks(*split3(turned), in_ref))
    total = None
    for c in range(columns // CHUNK):
        at, cols = slice(c * count, (c + 1) * count), slice(c * CHUNK, (c + 1) * CHUNK)
        both = jnp.concatenate([high[at], low[at]], axis=0)
        by_high = lax.dot_general(both, q_high_ref[:, cols], NT, preferred_element_type=F32)
        by_low = lax.dot_general(high[at], q_low_ref[:, cols], NT, preferred_element_type=F32)
        part = by_high[0:count] + (by_high[count:] + by_low)
        total = part if total is None else total + part
    total = total * (1.0 / width)
    mine_ref[...] = total[0 : count // 2]
    theirs_ref[...] = total[count // 2 :]


def score(pieces, in_blocks, out_blocks, high, low):
    columns = high.shape[1]
    count = pieces[0].shape[0] * CHUNK // columns
    shape = jax.ShapeDtypeStruct((count // 2, high.shape[0]), F32)
    return pl.pallas_call(
        score_kernel,
        out_shape=(shape, shape),
        in_specs=[pl.BlockSpec(memory_space=pltpu.VMEM)] * 7,
        out_specs=(pl.BlockSpec(memory_space=pltpu.VMEM),) * 2,
        scratch_shapes=[pltpu.VMEM((columns, count), F32)],
        compiler_params=pltpu.CompilerParams(vmem_limit_bytes=(8 + high.shape[0] // 128) * MIB),
        name="score",
    )(*pieces, in_blocks, out_blocks, high, low)


def place_kernel(bit, size, kept_ref, received_ref, out_ref):
    mine = (lax.axis_index("dp") // bit) % 2
    for k in range(kept_ref.shape[1] // size):
        first = (k // bit) * 2 * bit + k % bit
        for ref, value in ((kept_ref, mine), (received_ref, 1 - mine)):
            start = pl.multiple_of((first + value * bit) * size, size)
            out_ref[:, pl.ds(start, size)] = ref[:, k * size : (k + 1) * size]


def place(bit, size, kept, received):
    rows, columns = kept.shape
    return pl.pallas_call(
        functools.partial(place_kernel, bit, size),
        out_shape=jax.ShapeDtypeStruct((rows, 2 * columns), F32),
        in_specs=[pl.BlockSpec(memory_space=pltpu.VMEM)] * 2,
        out_specs=pl.BlockSpec(memory_space=pltpu.VMEM),
        compiler_params=pltpu.CompilerParams(vmem_limit_bytes=8 * MIB),
        name="place",
    )(kept, received)


FINAL_LOW = False
ORDER = "21x"
E_STAGES = (1, 2)
Q_STAGE = 1


def body(mesh, activations, out_grads, proj_in, proj_out, lengths, queries):
    n_dp, n_query = mesh.shape["dp"], mesh.shape["query"]
    core_bit = 1
    query_bits = [2 * b for b in bits_of(n_query)]
    unit = 2 * n_query
    final = 1 if FINAL_LOW else n_dp // 2
    far = tuple(b for b in bits_of(n_dp) if b != final)

    half = pick_queries(queries)
    same = [half]
    for bit in far:
        same = same + [swap(h, mesh, bit * unit) for h in same]
    same = same[1:]

    own = project(activations, out_grads, proj_in, proj_out, half)
    other = swap(own, mesh, core_bit)

    own, other, same = lax.optimization_barrier((own, other, same))

    factor = fisher(lengths, own, other)
    factor, own, other = lax.optimization_barrier((factor, own, other))
    blocks = example_grads(lengths, own, other)[None]
    dp_bits = [b * unit for b in bits_of(n_dp)]
    groups = {"x": query_bits, "1": dp_bits[:1], "2": dp_bits[1:]}
    steps = [bit | core_bit for name in ORDER for bit in groups[name]]
    exchange = [bit | core_bit for bit in query_bits + [final * unit]]
    stages = {E_STAGES[0] + i: [m] for i, m in enumerate(exchange[:-1])}
    stages.setdefault(max(E_STAGES[1], E_STAGES[0] + len(exchange) - 1), []).append(exchange[-1])

    def beside(stage, factor, blocks, same):
        for mask in stages.get(stage, ()):
            blocks, factor = lax.optimization_barrier((blocks, factor))
            blocks = jnp.concatenate([blocks, swap(blocks, mesh, mask)], axis=0)
        if stage == Q_STAGE:
            same, factor = lax.optimization_barrier((same, factor))
        return factor, blocks, same

    for step, mask in enumerate(steps):
        factor, blocks, same = beside(step, factor, blocks, same)
        received = swap(factor, mesh, mask)
        if step < len(steps) - 1:
            factor = factor + received
    received, blocks, same = beside(len(steps), received, blocks, same)
    others = [swap(h, mesh, core_bit) for h in same]
    in_blocks, out_blocks = inverses(factor, received)

    arranged = arrange_examples(blocks, n_query)
    high, low = split_queries(far, queries, same, others)
    kept, sent = score(arranged, in_blocks, out_blocks, high, low)
    return place(final, queries.shape[1], kept, swap(sent, mesh, final * unit | core_bit))


def solution(mesh):
    in_specs = (
        P(("grp", "dp", "query"), "proj"),
        P(("grp", "dp", "query"), "proj"),
        P("proj", None),
        P("proj", None),
        P(("grp", "dp", "query"), None),
        P("query", "dp", None),
    )
    out_specs = P(("grp", "dp"), "query")
    return jax.shard_map(
        functools.partial(body, mesh), mesh=mesh, in_specs=in_specs, out_specs=out_specs, check_vma=False
    )
```

```python
import functools
import math

import jax
import jax.numpy as jnp
from jax import lax
from jax.experimental import pallas as pl
from jax.experimental.pallas import tpu as pltpu
from jax.sharding import PartitionSpec as P

F32 = jnp.float32
BF16 = jnp.bfloat16
HIGHEST = lax.Precision.HIGHEST
NT = (((1,), (1,)), ((), ()))
AXES = ("grp", "dp", "query", "proj")
MIB = 2**20
CHUNK = 256
QUERY_STEP = 1


def swap(value, mesh, mask):
    count = math.prod(mesh.shape[axis] for axis in AXES)
    return lax.ppermute(value, AXES, [(i, i ^ mask) for i in range(count)])


def bits_of(size):
    return [1 << b for b in range(size.bit_length() - 1)]


def pick_kernel(groups, queries_hbm, half_ref, piece_ref, sems):
    half, piece = half_ref.shape[0], piece_ref.shape[0]
    core = lax.axis_index("proj")
    index = core * groups + lax.axis_index("grp")
    copies = [
        pltpu.make_async_copy(queries_hbm.at[0, pl.ds(pl.multiple_of(core * half, 8), half)], half_ref, sems.at[0]),
        pltpu.make_async_copy(queries_hbm.at[0, pl.ds(pl.multiple_of(index * piece, 8), piece)], piece_ref, sems.at[1]),
    ]
    for copy in copies:
        copy.start()
    for copy in copies:
        copy.wait()


def pick_queries(queries, groups):
    rows, columns = queries.shape[1:]
    return pl.pallas_call(
        functools.partial(pick_kernel, groups),
        out_shape=tuple(jax.ShapeDtypeStruct((rows // n, columns), F32) for n in (2, 2 * groups)),
        in_specs=[pl.BlockSpec(memory_space=pl.ANY)],
        out_specs=(pl.BlockSpec(memory_space=pltpu.VMEM),) * 2,
        scratch_shapes=[pltpu.SemaphoreType.DMA((2,))],
        compiler_params=pltpu.CompilerParams(vmem_limit_bytes=4 * MIB),
        cost_estimate=pl.CostEstimate(flops=4 * 10**9, bytes_accessed=10**6, transcendentals=0),
        name="pick_queries",
    )(pltpu.with_memory_space_constraint(queries, pltpu.HBM))


def project_kernel(a_ref, g_ref, p_in_ref, p_out_ref, after_ref, out_ref):
    width = p_in_ref.shape[0]
    out_ref[0:width, :] = lax.dot_general(p_in_ref[...], a_ref[...], NT, preferred_element_type=F32)
    out_ref[width : 2 * width, :] = lax.dot_general(p_out_ref[...], g_ref[...], NT, preferred_element_type=F32)


def project(activations, out_grads, proj_in, proj_out, after):
    return pl.pallas_call(
        project_kernel,
        out_shape=jax.ShapeDtypeStruct((2 * proj_in.shape[1], activations.shape[0]), F32),
        in_specs=[pl.BlockSpec(memory_space=pltpu.VMEM)] * 4 + [pl.BlockSpec(memory_space=pl.ANY)],
        out_specs=pl.BlockSpec(memory_space=pltpu.VMEM),
        compiler_params=pltpu.CompilerParams(vmem_limit_bytes=16 * MIB),
        name="project",
    )(activations, out_grads, proj_in.T, proj_out.T, after)


def masks_kernel(lengths_ref, after_ref, member_ref, live_ref, count_ref):
    examples, slots = member_ref.shape
    index = lax.broadcasted_iota(jnp.int32, (examples, 1), 0)
    starts = jnp.zeros((examples, 1), jnp.int32)
    counts = jnp.zeros((examples, 1), jnp.int32)
    begin = jnp.int32(0)
    for e in range(examples):
        length = lengths_ref[0, e]
        starts = jnp.where(index == e, begin, starts)
        counts = jnp.where(index == e, length, counts)
        begin = begin + length
    slot = lax.broadcasted_iota(jnp.int32, (examples, slots), 1)
    member_ref[...] = jnp.where((slot >= starts) & (slot < starts + counts), 1.0, 0.0).astype(BF16)
    live_ref[...] = jnp.where(slot[0:8] < begin, 1.0, 0.0)
    count_ref[...] = jnp.broadcast_to(counts.astype(F32), count_ref.shape)


def masks(lengths, after):
    examples, slots = lengths.shape[1] - 1, after.shape[1]
    return pl.pallas_call(
        masks_kernel,
        out_shape=(
            jax.ShapeDtypeStruct((examples, slots), BF16),
            jax.ShapeDtypeStruct((8, slots), F32),
            jax.ShapeDtypeStruct((examples, 128), F32),
        ),
        in_specs=[pl.BlockSpec(memory_space=pltpu.SMEM), pl.BlockSpec(memory_space=pl.ANY)],
        out_specs=(pl.BlockSpec(memory_space=pltpu.VMEM),) * 3,
        compiler_params=pltpu.CompilerParams(vmem_limit_bytes=4 * MIB),
        cost_estimate=pl.CostEstimate(flops=2 * 10**9, bytes_accessed=10**6, transcendentals=0),
        name="masks",
    )(lengths, after)


def fisher_kernel(live_ref, own_ref, other_ref, out_ref):
    width = out_ref.shape[0]
    both = own_ref[...] + other_ref[...]
    gram = lax.dot_general(both * live_ref[0:1, :], both, NT, precision=HIGHEST, preferred_element_type=F32)
    out_ref[...] = jnp.zeros_like(out_ref)
    out_ref[:, 0:width] = gram[0:width, 0:width]
    out_ref[:, width : 2 * width] = gram[width : 2 * width, width : 2 * width]


def fisher(live, own, other):
    width = own.shape[0] // 2
    return pl.pallas_call(
        fisher_kernel,
        out_shape=jax.ShapeDtypeStruct((width, 128), F32),
        in_specs=[pl.BlockSpec(memory_space=pltpu.VMEM)] * 3,
        out_specs=pl.BlockSpec(memory_space=pltpu.VMEM),
        compiler_params=pltpu.CompilerParams(vmem_limit_bytes=8 * MIB),
        name="fisher",
    )(live, own, other)


def split3(value):
    high = value.astype(BF16)
    rest = value - high.astype(F32)
    middle = rest.astype(BF16)
    return high, middle, (rest - middle.astype(F32)).astype(BF16)


def examples_kernel(member_ref, count_ref, own_ref, other_ref, out_ref):
    width = own_ref.shape[0] // 2
    both = own_ref[...] + other_ref[...]
    inputs, outputs = both[0:width], both[width : 2 * width]
    member, divisor = member_ref[...], count_ref[:, 0:1]
    group = 8
    for first in range(0, width, group):
        outer = jnp.concatenate([outputs[i : i + 1] * inputs for i in range(first, first + group)], axis=0)
        total = None
        for piece in reversed(split3(outer)):
            part = lax.dot_general(member, piece, NT, preferred_element_type=F32)
            total = part if total is None else total + part
        out_ref[:, first * width : (first + group) * width] = total / divisor


def example_grads(member, count, own, other):
    width = own.shape[0] // 2
    return pl.pallas_call(
        examples_kernel,
        out_shape=jax.ShapeDtypeStruct((member.shape[0], width * width), F32),
        in_specs=[pl.BlockSpec(memory_space=pltpu.VMEM)] * 4,
        out_specs=pl.BlockSpec(memory_space=pltpu.VMEM),
        compiler_params=pltpu.CompilerParams(vmem_limit_bytes=8 * MIB),
        cost_estimate=pl.CostEstimate(flops=2 * 10**9, bytes_accessed=10**6, transcendentals=0),
        name="examples",
    )(member, count, own, other)


def split2(value):
    high = value.astype(BF16)
    return high, (value - high.astype(F32)).astype(BF16)


def turn_pairs(load, scratch, width):
    columns, count = scratch.shape
    for c in range(columns // CHUNK):
        scratch[c * CHUNK : (c + 1) * CHUNK, :] = load(c).T
    chunks = []
    for c in range(columns // CHUNK):
        lines = range(c * CHUNK // width, (c + 1) * CHUNK // width)
        chunks.append(jnp.concatenate([scratch[pl.ds(j, width, stride=width), :] for j in lines], axis=0).T)
    return jnp.concatenate(chunks, axis=0)


def arrange_examples_kernel(n_query, blocks_ref, *refs):
    out_refs, (rows, scratch) = refs[:-2], refs[-2:]
    blocks, examples, columns = blocks_ref.shape
    query = lax.axis_index("query")
    for b in range(blocks):
        place = (b // n_query) * n_query + (query ^ (b % n_query))
        rows[pl.ds(pl.multiple_of(place * examples, 8), examples), :] = blocks_ref[b]
    width = math.isqrt(columns)
    turned = turn_pairs(lambda c: rows[:, c * CHUNK : (c + 1) * CHUNK], scratch, width)
    for out_ref, piece in zip(out_refs, split3(turned)):
        out_ref[...] = piece


def arrange_examples(blocks, n_query):
    number, examples, columns = blocks.shape
    count = number * examples
    shape = jax.ShapeDtypeStruct((count * columns // CHUNK, CHUNK), BF16)
    return pl.pallas_call(
        functools.partial(arrange_examples_kernel, n_query),
        out_shape=(shape,) * 3,
        in_specs=[pl.BlockSpec(memory_space=pltpu.VMEM)],
        out_specs=(pl.BlockSpec(memory_space=pltpu.VMEM),) * 3,
        scratch_shapes=[pltpu.VMEM((count, columns), F32), pltpu.VMEM((columns, count), F32)],
        compiler_params=pltpu.CompilerParams(vmem_limit_bytes=12 * MIB),
        name="arrange_examples",
    )(blocks)


def split_queries_kernel(groups, own_ref, *refs):
    fetched_refs, (high_ref, low_ref) = refs[:-2], refs[-2:]
    half = own_ref.shape[1] // 2
    piece = half // groups
    place, group, core = lax.axis_index("dp"), lax.axis_index("grp"), lax.axis_index("proj")

    def put(start, value):
        at = pl.ds(pl.multiple_of(start, 16), value.shape[0])
        high_ref[at, :], low_ref[at, :] = split2(value)

    put(place * half, own_ref[0, pl.ds(pl.multiple_of(core * half, 8), half), :])
    for r, ref in enumerate(fetched_refs, 1):
        if r == 1:
            put((place ^ r) * half, ref[...])
            continue
        for g in range(groups):
            put((place ^ r) * half + (group ^ g) * piece, ref[g * piece : (g + 1) * piece, :])


def split_queries(groups, own, fetched):
    parts = 1 + len(fetched)
    rows, columns = own.shape[1:]
    shape = jax.ShapeDtypeStruct((parts * rows // 2, columns), BF16)
    return pl.pallas_call(
        functools.partial(split_queries_kernel, groups),
        out_shape=(shape, shape),
        in_specs=[pl.BlockSpec(memory_space=pltpu.VMEM)] * parts,
        out_specs=(pl.BlockSpec(memory_space=pltpu.VMEM),) * 2,
        compiler_params=pltpu.CompilerParams(vmem_limit_bytes=(4 + parts) * MIB),
        name="split_queries",
    )(own, *fetched)


def inverse_tiled(fisher_sum):
    width = fisher_sum.shape[0]
    row = lax.broadcasted_iota(jnp.int32, (width, width), 0)
    column = lax.broadcasted_iota(jnp.int32, (width, width), 1)
    trace = jnp.sum(jnp.where(row == column, fisher_sum, 0.0), keepdims=True)
    damped = fisher_sum * (width / trace) + jnp.where(row == column, 1.0, 0.0)
    state = jnp.concatenate([damped] * (128 // width), axis=1)
    lane = lax.broadcasted_iota(jnp.int32, state.shape, 1) % width
    sublane = lax.broadcasted_iota(jnp.int32, state.shape, 0)
    top = lane[0:1]

    def apply(m, x, y):
        return m[0][0] * x + m[0][1] * y, m[1][0] * x + m[1][1] * y

    def invert(m):
        scale = 1.0 / (m[0][0] * m[1][1] - m[0][1] * m[1][0])
        return (m[1][1] * scale, -m[0][1] * scale), (-m[1][0] * scale, m[0][0] * scale)

    for k in range(0, width, 4):
        columns = [jnp.broadcast_to(state[:, k + c : k + c + 1], state.shape) for c in range(4)]
        pivot = [[columns[c][k + r : k + r + 1, :] for c in range(4)] for r in range(4)]
        inside = (top >= k) & (top < k + 4)
        rows = [
            jnp.where(top == k + r, 1.0, jnp.where(inside, 0.0, state[k + r : k + r + 1, :])) for r in range(4)
        ]
        corner = invert((pivot[0][0:2], pivot[1][0:2]))
        upper = apply(corner, rows[0], rows[1])
        right = [apply(corner, pivot[0][c], pivot[1][c]) for c in (2, 3)]
        schur = [
            [pivot[r][c] - pivot[r][0] * right[c - 2][0] - pivot[r][1] * right[c - 2][1] for c in (2, 3)] for r in (2, 3)
        ]
        lower = apply(
            invert(schur), *(rows[r] - pivot[r][0] * upper[0] - pivot[r][1] * upper[1] for r in (2, 3))
        )
        solved = [upper[r] - right[0][r] * lower[0] - right[1][r] * lower[1] for r in range(2)] + list(lower)
        change = columns[0] * solved[0] + columns[1] * solved[1] + columns[2] * solved[2] + columns[3] * solved[3]
        state = jnp.where((lane >= k) & (lane < k + 4), 0.0, state) - change
        for r in range(4):
            state = jnp.where(sublane == k + r, solved[r], state)
    return state


def block_diagonal(tiled):
    width, lanes = tiled.shape
    value = jnp.concatenate([jnp.concatenate([tiled] * (CHUNK // lanes), axis=1)] * (CHUNK // width), axis=0)
    row = lax.broadcasted_iota(jnp.int32, (CHUNK, CHUNK), 0) // width
    column = lax.broadcasted_iota(jnp.int32, (CHUNK, CHUNK), 1) // width
    return jnp.where(row == column, value, 0.0)


def inverses_kernel(own_ref, other_ref, in_ref, out_ref):
    width = own_ref.shape[0]
    total = own_ref[...] + other_ref[...]
    for ref, fisher_sum in ((in_ref, total[:, 0:width]), (out_ref, total[:, width : 2 * width])):
        for piece, value in enumerate(split3(block_diagonal(inverse_tiled(fisher_sum)))):
            ref[piece] = value


def inverses(own, other):
    shape = jax.ShapeDtypeStruct((3, CHUNK, CHUNK), BF16)
    return pl.pallas_call(
        inverses_kernel,
        out_shape=(shape, shape),
        in_specs=[pl.BlockSpec(memory_space=pltpu.VMEM)] * 2,
        out_specs=(pl.BlockSpec(memory_space=pltpu.VMEM),) * 2,
        compiler_params=pltpu.CompilerParams(vmem_limit_bytes=8 * MIB),
        name="inverses",
    )(own, other)


def times_blocks(high, middle, low, blocks_ref):
    rows = high.shape[0]
    by_high = jnp.dot(jnp.concatenate([high, middle, low], axis=0), blocks_ref[0], preferred_element_type=F32)
    by_middle = jnp.dot(jnp.concatenate([high, middle], axis=0), blocks_ref[1], preferred_element_type=F32)
    by_low = jnp.dot(high, blocks_ref[2], preferred_element_type=F32)
    small = by_high[2 * rows :] + by_middle[rows:] + by_low
    return by_high[0:rows] + (by_high[rows : 2 * rows] + by_middle[0:rows] + small)


def score_kernel(high_ref, middle_ref, low_ref, in_ref, out_ref, q_high_ref, q_low_ref, scores_ref, scratch):
    columns, count = scratch.shape
    width = math.isqrt(columns)
    left = times_blocks(high_ref[...], middle_ref[...], low_ref[...], out_ref)
    turned = turn_pairs(lambda c: left[c * count : (c + 1) * count], scratch, width)
    high, low = split2(times_blocks(*split3(turned), in_ref))
    total = None
    for c in range(columns // CHUNK):
        at, cols = slice(c * count, (c + 1) * count), slice(c * CHUNK, (c + 1) * CHUNK)
        both = jnp.concatenate([high[at], low[at]], axis=0)
        by_high = lax.dot_general(both, q_high_ref[:, cols], NT, preferred_element_type=F32)
        by_low = lax.dot_general(high[at], q_low_ref[:, cols], NT, preferred_element_type=F32)
        part = by_high[0:count] + (by_high[count:] + by_low)
        total = part if total is None else total + part
    scores_ref[...] = total * (1.0 / width)


def score(pieces, in_blocks, out_blocks, high, low):
    rows, columns = high.shape
    count = pieces[0].shape[0] * CHUNK // columns
    return pl.pallas_call(
        score_kernel,
        out_shape=jax.ShapeDtypeStruct((count, rows), F32),
        in_specs=[pl.BlockSpec(memory_space=pltpu.VMEM)] * 7,
        out_specs=pl.BlockSpec(memory_space=pltpu.VMEM),
        scratch_shapes=[pltpu.VMEM((columns, count), F32)],
        compiler_params=pltpu.CompilerParams(vmem_limit_bytes=(6 + rows // 128) * MIB),
        name="score",
    )(*pieces, in_blocks, out_blocks, high, low)


def place_kernel(half, kept_ref, received_ref, out_ref):
    core = lax.axis_index("proj")
    kept, received = kept_ref[...], received_ref[...]
    first = jnp.where(core == 0, kept, received)
    second = jnp.where(core == 0, received, kept)
    for k in range(kept.shape[1] // half):
        at = slice(k * half, (k + 1) * half)
        out_ref[:, 2 * k * half : 2 * (k + 1) * half] = jnp.concatenate([first[:, at], second[:, at]], axis=1)


def place(half, kept, received):
    rows, columns = kept.shape
    return pl.pallas_call(
        functools.partial(place_kernel, half),
        out_shape=jax.ShapeDtypeStruct((rows, 2 * columns), F32),
        in_specs=[pl.BlockSpec(memory_space=pltpu.VMEM)] * 2,
        out_specs=pl.BlockSpec(memory_space=pltpu.VMEM),
        compiler_params=pltpu.CompilerParams(vmem_limit_bytes=8 * MIB),
        name="place",
    )(kept, received)


ORDER = "x12"
E_STAGE = 1
Y_STAGE = 2


def body(mesh, activations, out_grads, proj_in, proj_out, lengths, queries):
    groups, n_dp, n_query = mesh.shape["grp"], mesh.shape["dp"], mesh.shape["query"]
    core_bit = 1
    unit = 2 * n_query
    query_bits = [2 * b for b in bits_of(n_query)]
    dp_bits = [b * unit for b in bits_of(n_dp)]
    group_bits = [b * unit * n_dp for b in bits_of(groups)]

    half, piece = pick_queries(queries, groups)
    fetched = [swap(half if r == 1 else piece, mesh, r * unit) for r in range(1, n_dp)]

    own = project(activations, out_grads, proj_in, proj_out, half)
    member, live, count = masks(lengths, own)
    other = swap(own, mesh, core_bit)
    own, other, live = lax.optimization_barrier((own, other, live))

    factor = fisher(live, own, other)
    factor, own, other = lax.optimization_barrier((factor, own, other))
    blocks = example_grads(member, count, own, other)[None]
    groups_of = {"x": query_bits, "1": dp_bits[:1], "2": dp_bits[1:]}
    steps = [bit | core_bit for name in ORDER for bit in groups_of[name]]

    def beside(stage, factor, blocks, fetched):
        i = stage - E_STAGE
        if 0 <= i < len(query_bits):
            blocks, factor = lax.optimization_barrier((blocks, factor))
            blocks = jnp.concatenate([blocks, swap(blocks, mesh, query_bits[i] | core_bit)], axis=0)
        if stage == Y_STAGE:
            fetched, factor = lax.optimization_barrier((fetched, factor))
            for bit in group_bits:
                fetched = fetched[:1] + [jnp.concatenate([p, swap(p, mesh, bit)], axis=0) for p in fetched[1:]]
        return factor, blocks, fetched

    for step, mask in enumerate(steps):
        factor, blocks, fetched = beside(step, factor, blocks, fetched)
        received = swap(factor, mesh, mask)
        if step < len(steps) - 1:
            factor = factor + received
    in_blocks, out_blocks = inverses(factor, received)

    arranged = arrange_examples(blocks, n_query)
    high, low = split_queries(groups, queries, fetched)
    scores = score(arranged, in_blocks, out_blocks, high, low)
    return place(queries.shape[1] // 2, scores, swap(scores, mesh, core_bit))


def solution(mesh):
    in_specs = (
        P(("grp", "dp", "query"), "proj"),
        P(("grp", "dp", "query"), "proj"),
        P("proj", None),
        P("proj", None),
        P(("grp", "dp", "query"), None),
        P("query", "dp", None),
    )
    out_specs = P(("grp", "dp"), "query")
    return jax.shard_map(
        functools.partial(body, mesh), mesh=mesh, in_specs=in_specs, out_specs=out_specs, check_vma=False
    )
```

```python
import functools
import math

import jax
import jax.numpy as jnp
from jax import lax
from jax.experimental import pallas as pl
from jax.experimental.pallas import tpu as pltpu
from jax.sharding import PartitionSpec as P

F32 = jnp.float32
BF16 = jnp.bfloat16
HIGHEST = lax.Precision.HIGHEST
NT = (((1,), (1,)), ((), ()))
AXES = ("grp", "dp", "query", "proj")
MIB = 2**20
CHUNK = 256
QUERY_STEP = 1


def swap(value, mesh, mask):
    count = math.prod(mesh.shape[axis] for axis in AXES)
    return lax.ppermute(value, AXES, [(i, i ^ mask) for i in range(count)])


def bits_of(size):
    return [1 << b for b in range(size.bit_length() - 1)]


def pick_kernel(groups, queries_hbm, half_ref, piece_ref, sems):
    half, piece = half_ref.shape[0], piece_ref.shape[0]
    core = lax.axis_index("proj")
    index = core * groups + lax.axis_index("grp")
    copies = [
        pltpu.make_async_copy(queries_hbm.at[0, pl.ds(pl.multiple_of(core * half, 8), half)], half_ref, sems.at[0]),
        pltpu.make_async_copy(queries_hbm.at[0, pl.ds(pl.multiple_of(index * piece, 8), piece)], piece_ref, sems.at[1]),
    ]
    for copy in copies:
        copy.start()
    for copy in copies:
        copy.wait()


def pick_queries(queries, groups):
    rows, columns = queries.shape[1:]
    return pl.pallas_call(
        functools.partial(pick_kernel, groups),
        out_shape=tuple(jax.ShapeDtypeStruct((rows // n, columns), F32) for n in (2, 2 * groups)),
        in_specs=[pl.BlockSpec(memory_space=pl.ANY)],
        out_specs=(pl.BlockSpec(memory_space=pltpu.VMEM),) * 2,
        scratch_shapes=[pltpu.SemaphoreType.DMA((2,))],
        compiler_params=pltpu.CompilerParams(vmem_limit_bytes=4 * MIB),
        cost_estimate=pl.CostEstimate(flops=4 * 10**9, bytes_accessed=10**6, transcendentals=0),
        name="pick_queries",
    )(pltpu.with_memory_space_constraint(queries, pltpu.HBM))


def project_kernel(a_ref, g_ref, p_in_ref, p_out_ref, after_ref, out_ref):
    width = p_in_ref.shape[0]
    out_ref[0:width, :] = lax.dot_general(p_in_ref[...], a_ref[...], NT, preferred_element_type=F32)
    out_ref[width : 2 * width, :] = lax.dot_general(p_out_ref[...], g_ref[...], NT, preferred_element_type=F32)


def project(activations, out_grads, proj_in, proj_out, after):
    return pl.pallas_call(
        project_kernel,
        out_shape=jax.ShapeDtypeStruct((2 * proj_in.shape[1], activations.shape[0]), F32),
        in_specs=[pl.BlockSpec(memory_space=pltpu.VMEM)] * 4 + [pl.BlockSpec(memory_space=pl.ANY)],
        out_specs=pl.BlockSpec(memory_space=pltpu.VMEM),
        compiler_params=pltpu.CompilerParams(vmem_limit_bytes=16 * MIB),
        name="project",
    )(activations, out_grads, proj_in.T, proj_out.T, after)


def masks_kernel(lengths_ref, after_ref, member_ref, live_ref, count_ref):
    examples, slots = member_ref.shape
    index = lax.broadcasted_iota(jnp.int32, (examples, 1), 0)
    starts = jnp.zeros((examples, 1), jnp.int32)
    counts = jnp.zeros((examples, 1), jnp.int32)
    begin = jnp.int32(0)
    for e in range(examples):
        length = lengths_ref[0, e]
        starts = jnp.where(index == e, begin, starts)
        counts = jnp.where(index == e, length, counts)
        begin = begin + length
    slot = lax.broadcasted_iota(jnp.int32, (examples, slots), 1)
    member_ref[...] = jnp.where((slot >= starts) & (slot < starts + counts), 1.0, 0.0).astype(BF16)
    live_ref[...] = jnp.where(slot[0:8] < begin, 1.0, 0.0)
    count_ref[...] = jnp.broadcast_to(counts.astype(F32), count_ref.shape)


def masks(lengths, after):
    examples, slots = lengths.shape[1] - 1, after.shape[1]
    return pl.pallas_call(
        masks_kernel,
        out_shape=(
            jax.ShapeDtypeStruct((examples, slots), BF16),
            jax.ShapeDtypeStruct((8, slots), F32),
            jax.ShapeDtypeStruct((examples, 128), F32),
        ),
        in_specs=[pl.BlockSpec(memory_space=pltpu.SMEM), pl.BlockSpec(memory_space=pl.ANY)],
        out_specs=(pl.BlockSpec(memory_space=pltpu.VMEM),) * 3,
        compiler_params=pltpu.CompilerParams(vmem_limit_bytes=4 * MIB),
        cost_estimate=pl.CostEstimate(flops=2 * 10**9, bytes_accessed=10**6, transcendentals=0),
        name="masks",
    )(lengths, after)


def fisher_kernel(live_ref, own_ref, other_ref, out_ref):
    width = out_ref.shape[0]
    both = own_ref[...] + other_ref[...]
    gram = lax.dot_general(both * live_ref[0:1, :], both, NT, precision=HIGHEST, preferred_element_type=F32)
    out_ref[...] = jnp.zeros_like(out_ref)
    out_ref[:, 0:width] = gram[0:width, 0:width]
    out_ref[:, width : 2 * width] = gram[width : 2 * width, width : 2 * width]


def fisher(live, own, other):
    width = own.shape[0] // 2
    return pl.pallas_call(
        fisher_kernel,
        out_shape=jax.ShapeDtypeStruct((width, 128), F32),
        in_specs=[pl.BlockSpec(memory_space=pltpu.VMEM)] * 3,
        out_specs=pl.BlockSpec(memory_space=pltpu.VMEM),
        compiler_params=pltpu.CompilerParams(vmem_limit_bytes=8 * MIB),
        name="fisher",
    )(live, own, other)


def split3(value):
    high = value.astype(BF16)
    rest = value - high.astype(F32)
    middle = rest.astype(BF16)
    return high, middle, (rest - middle.astype(F32)).astype(BF16)


def examples_kernel(member_ref, count_ref, own_ref, other_ref, out_ref):
    width = own_ref.shape[0] // 2
    both = own_ref[...] + other_ref[...]
    inputs, outputs = both[0:width], both[width : 2 * width]
    member, divisor = member_ref[...], count_ref[:, 0:1]
    group = 8
    for first in range(0, width, group):
        outer = jnp.concatenate([outputs[i : i + 1] * inputs for i in range(first, first + group)], axis=0)
        total = None
        for piece in reversed(split3(outer)):
            part = lax.dot_general(member, piece, NT, preferred_element_type=F32)
            total = part if total is None else total + part
        out_ref[:, first * width : (first + group) * width] = total / divisor


def example_grads(member, count, own, other):
    width = own.shape[0] // 2
    return pl.pallas_call(
        examples_kernel,
        out_shape=jax.ShapeDtypeStruct((member.shape[0], width * width), F32),
        in_specs=[pl.BlockSpec(memory_space=pltpu.VMEM)] * 4,
        out_specs=pl.BlockSpec(memory_space=pltpu.VMEM),
        compiler_params=pltpu.CompilerParams(vmem_limit_bytes=8 * MIB),
        cost_estimate=pl.CostEstimate(flops=2 * 10**9, bytes_accessed=10**6, transcendentals=0),
        name="examples",
    )(member, count, own, other)


def split2(value):
    high = value.astype(BF16)
    return high, (value - high.astype(F32)).astype(BF16)


def turn_pairs(load, scratch, width):
    columns, count = scratch.shape
    for c in range(columns // CHUNK):
        scratch[c * CHUNK : (c + 1) * CHUNK, :] = load(c).T
    chunks = []
    for c in range(columns // CHUNK):
        lines = range(c * CHUNK // width, (c + 1) * CHUNK // width)
        chunks.append(jnp.concatenate([scratch[pl.ds(j, width, stride=width), :] for j in lines], axis=0).T)
    return jnp.concatenate(chunks, axis=0)


def arrange_examples_kernel(n_query, blocks_ref, *refs):
    out_refs, (rows, scratch) = refs[:-2], refs[-2:]
    blocks, examples, columns = blocks_ref.shape
    query = lax.axis_index("query")
    for b in range(blocks):
        place = (b // n_query) * n_query + (query ^ (b % n_query))
        rows[pl.ds(pl.multiple_of(place * examples, 8), examples), :] = blocks_ref[b]
    width = math.isqrt(columns)
    turned = turn_pairs(lambda c: rows[:, c * CHUNK : (c + 1) * CHUNK], scratch, width)
    for out_ref, piece in zip(out_refs, split3(turned)):
        out_ref[...] = piece


def arrange_examples(blocks, n_query):
    number, examples, columns = blocks.shape
    count = number * examples
    shape = jax.ShapeDtypeStruct((count * columns // CHUNK, CHUNK), BF16)
    return pl.pallas_call(
        functools.partial(arrange_examples_kernel, n_query),
        out_shape=(shape,) * 3,
        in_specs=[pl.BlockSpec(memory_space=pltpu.VMEM)],
        out_specs=(pl.BlockSpec(memory_space=pltpu.VMEM),) * 3,
        scratch_shapes=[pltpu.VMEM((count, columns), F32), pltpu.VMEM((columns, count), F32)],
        compiler_params=pltpu.CompilerParams(vmem_limit_bytes=12 * MIB),
        name="arrange_examples",
    )(blocks)


def split_queries_kernel(groups, own_ref, *refs):
    fetched_refs, (high_ref, low_ref) = refs[:-2], refs[-2:]
    half = own_ref.shape[1] // 2
    piece = half // groups
    place, group, core = lax.axis_index("dp"), lax.axis_index("grp"), lax.axis_index("proj")

    def put(start, value):
        at = pl.ds(pl.multiple_of(start, 16), value.shape[0])
        high_ref[at, :], low_ref[at, :] = split2(value)

    put(place * half, own_ref[0, pl.ds(pl.multiple_of(core * half, 8), half), :])
    for r, ref in enumerate(fetched_refs, 1):
        if r == 1:
            put((place ^ r) * half, ref[...])
            continue
        for g in range(groups):
            put((place ^ r) * half + (group ^ g) * piece, ref[g * piece : (g + 1) * piece, :])


def split_queries(groups, own, fetched):
    parts = 1 + len(fetched)
    rows, columns = own.shape[1:]
    shape = jax.ShapeDtypeStruct((parts * rows // 2, columns), BF16)
    return pl.pallas_call(
        functools.partial(split_queries_kernel, groups),
        out_shape=(shape, shape),
        in_specs=[pl.BlockSpec(memory_space=pltpu.VMEM)] * parts,
        out_specs=(pl.BlockSpec(memory_space=pltpu.VMEM),) * 2,
        compiler_params=pltpu.CompilerParams(vmem_limit_bytes=(4 + parts) * MIB),
        name="split_queries",
    )(own, *fetched)


def inverse_tiled(fisher_sum):
    width = fisher_sum.shape[0]
    row = lax.broadcasted_iota(jnp.int32, (width, width), 0)
    column = lax.broadcasted_iota(jnp.int32, (width, width), 1)
    trace = jnp.sum(jnp.where(row == column, fisher_sum, 0.0), keepdims=True)
    damped = fisher_sum * (width / trace) + jnp.where(row == column, 1.0, 0.0)
    state = jnp.concatenate([damped] * (128 // width), axis=1)
    lane = lax.broadcasted_iota(jnp.int32, state.shape, 1) % width
    sublane = lax.broadcasted_iota(jnp.int32, state.shape, 0)
    top = lane[0:1]

    def apply(m, x, y):
        return m[0][0] * x + m[0][1] * y, m[1][0] * x + m[1][1] * y

    def invert(m):
        scale = 1.0 / (m[0][0] * m[1][1] - m[0][1] * m[1][0])
        return (m[1][1] * scale, -m[0][1] * scale), (-m[1][0] * scale, m[0][0] * scale)

    for k in range(0, width, 4):
        columns = [jnp.broadcast_to(state[:, k + c : k + c + 1], state.shape) for c in range(4)]
        pivot = [[columns[c][k + r : k + r + 1, :] for c in range(4)] for r in range(4)]
        inside = (top >= k) & (top < k + 4)
        rows = [
            jnp.where(top == k + r, 1.0, jnp.where(inside, 0.0, state[k + r : k + r + 1, :])) for r in range(4)
        ]
        corner = invert((pivot[0][0:2], pivot[1][0:2]))
        upper = apply(corner, rows[0], rows[1])
        right = [apply(corner, pivot[0][c], pivot[1][c]) for c in (2, 3)]
        schur = [
            [pivot[r][c] - pivot[r][0] * right[c - 2][0] - pivot[r][1] * right[c - 2][1] for c in (2, 3)] for r in (2, 3)
        ]
        lower = apply(
            invert(schur), *(rows[r] - pivot[r][0] * upper[0] - pivot[r][1] * upper[1] for r in (2, 3))
        )
        solved = [upper[r] - right[0][r] * lower[0] - right[1][r] * lower[1] for r in range(2)] + list(lower)
        change = columns[0] * solved[0] + columns[1] * solved[1] + columns[2] * solved[2] + columns[3] * solved[3]
        state = jnp.where((lane >= k) & (lane < k + 4), 0.0, state) - change
        for r in range(4):
            state = jnp.where(sublane == k + r, solved[r], state)
    return state


def block_diagonal(tiled):
    width, lanes = tiled.shape
    value = jnp.concatenate([jnp.concatenate([tiled] * (CHUNK // lanes), axis=1)] * (CHUNK // width), axis=0)
    row = lax.broadcasted_iota(jnp.int32, (CHUNK, CHUNK), 0) // width
    column = lax.broadcasted_iota(jnp.int32, (CHUNK, CHUNK), 1) // width
    return jnp.where(row == column, value, 0.0)


def inverses_kernel(own_ref, other_ref, in_ref, out_ref):
    width = own_ref.shape[0]
    total = own_ref[...] + other_ref[...]
    for ref, fisher_sum in ((in_ref, total[:, 0:width]), (out_ref, total[:, width : 2 * width])):
        for piece, value in enumerate(split3(block_diagonal(inverse_tiled(fisher_sum)))):
            ref[piece] = value


def inverses(own, other):
    shape = jax.ShapeDtypeStruct((3, CHUNK, CHUNK), BF16)
    return pl.pallas_call(
        inverses_kernel,
        out_shape=(shape, shape),
        in_specs=[pl.BlockSpec(memory_space=pltpu.VMEM)] * 2,
        out_specs=(pl.BlockSpec(memory_space=pltpu.VMEM),) * 2,
        compiler_params=pltpu.CompilerParams(vmem_limit_bytes=8 * MIB),
        name="inverses",
    )(own, other)


def times_blocks(high, middle, low, blocks_ref):
    rows = high.shape[0]
    by_high = jnp.dot(jnp.concatenate([high, middle, low], axis=0), blocks_ref[0], preferred_element_type=F32)
    by_middle = jnp.dot(jnp.concatenate([high, middle], axis=0), blocks_ref[1], preferred_element_type=F32)
    by_low = jnp.dot(high, blocks_ref[2], preferred_element_type=F32)
    small = by_high[2 * rows :] + by_middle[rows:] + by_low
    return by_high[0:rows] + (by_high[rows : 2 * rows] + by_middle[0:rows] + small)


def condition_kernel(high_ref, middle_ref, low_ref, in_ref, out_ref, both_ref, scratch):
    columns, count = scratch.shape
    left = times_blocks(high_ref[...], middle_ref[...], low_ref[...], out_ref)
    turned = turn_pairs(lambda c: left[c * count : (c + 1) * count], scratch, math.isqrt(columns))
    high, low = split2(times_blocks(*split3(turned), in_ref))
    for c in range(columns // CHUNK):
        both_ref[c, 0:count] = high[c * count : (c + 1) * count]
        both_ref[c, count:] = low[c * count : (c + 1) * count]


def condition(pieces, in_blocks, out_blocks, columns):
    count = pieces[0].shape[0] * CHUNK // columns
    return pl.pallas_call(
        condition_kernel,
        out_shape=jax.ShapeDtypeStruct((columns // CHUNK, 2 * count, CHUNK), BF16),
        in_specs=[pl.BlockSpec(memory_space=pltpu.VMEM)] * 5,
        out_specs=pl.BlockSpec(memory_space=pltpu.VMEM),
        scratch_shapes=[pltpu.VMEM((columns, count), F32)],
        compiler_params=pltpu.CompilerParams(vmem_limit_bytes=8 * MIB),
        cost_estimate=pl.CostEstimate(flops=2 * 10**9, bytes_accessed=10**6, transcendentals=0),
        name="condition",
    )(*pieces, in_blocks, out_blocks)


def score_kernel(both_ref, q_high_ref, q_low_ref, scores_ref):
    chunks, count = both_ref.shape[0], both_ref.shape[1] // 2
    total = None
    for c in range(chunks):
        cols = slice(c * CHUNK, (c + 1) * CHUNK)
        by_high = lax.dot_general(both_ref[c], q_high_ref[:, cols], NT, preferred_element_type=F32)
        by_low = lax.dot_general(both_ref[c, 0:count], q_low_ref[:, cols], NT, preferred_element_type=F32)
        part = by_high[0:count] + (by_high[count:] + by_low)
        total = part if total is None else total + part
    scores_ref[...] = total * (1.0 / math.isqrt(chunks * CHUNK))


def score(both, high, low):
    rows = high.shape[0]
    return pl.pallas_call(
        score_kernel,
        out_shape=jax.ShapeDtypeStruct((both.shape[1] // 2, rows), F32),
        in_specs=[pl.BlockSpec(memory_space=pltpu.VMEM)] * 3,
        out_specs=pl.BlockSpec(memory_space=pltpu.VMEM),
        compiler_params=pltpu.CompilerParams(vmem_limit_bytes=(6 + rows // 128) * MIB),
        name="score",
    )(both, high, low)


def place_kernel(half, kept_ref, received_ref, out_ref):
    core = lax.axis_index("proj")
    kept, received = kept_ref[...], received_ref[...]
    first = jnp.where(core == 0, kept, received)
    second = jnp.where(core == 0, received, kept)
    for k in range(kept.shape[1] // half):
        at = slice(k * half, (k + 1) * half)
        out_ref[:, 2 * k * half : 2 * (k + 1) * half] = jnp.concatenate([first[:, at], second[:, at]], axis=1)


def place(half, kept, received):
    rows, columns = kept.shape
    return pl.pallas_call(
        functools.partial(place_kernel, half),
        out_shape=jax.ShapeDtypeStruct((rows, 2 * columns), F32),
        in_specs=[pl.BlockSpec(memory_space=pltpu.VMEM)] * 2,
        out_specs=pl.BlockSpec(memory_space=pltpu.VMEM),
        compiler_params=pltpu.CompilerParams(vmem_limit_bytes=8 * MIB),
        name="place",
    )(kept, received)


def hold_kernel(value_ref, after_ref, out_ref):
    out_ref[...] = value_ref[...]


def hold(value, after):
    return pl.pallas_call(
        hold_kernel,
        out_shape=jax.ShapeDtypeStruct(value.shape, value.dtype),
        in_specs=[pl.BlockSpec(memory_space=pltpu.VMEM), pl.BlockSpec(memory_space=pl.ANY)],
        out_specs=pl.BlockSpec(memory_space=pltpu.VMEM),
        compiler_params=pltpu.CompilerParams(vmem_limit_bytes=4 * MIB),
        cost_estimate=pl.CostEstimate(flops=10**9, bytes_accessed=10**6, transcendentals=0),
        name="hold",
    )(value, after)


ORDER = "x12"
E_STAGE = 1
Y_STAGES = (1, 2)


def body(mesh, activations, out_grads, proj_in, proj_out, lengths, queries):
    groups, n_dp, n_query = mesh.shape["grp"], mesh.shape["dp"], mesh.shape["query"]
    core_bit = 1
    unit = 2 * n_query
    query_bits = [2 * b for b in bits_of(n_query)]
    dp_bits = [b * unit for b in bits_of(n_dp)]
    group_bits = [b * unit * n_dp for b in bits_of(groups)]

    half, piece = pick_queries(queries, groups)
    fetched = [swap(half if r == 1 else piece, mesh, r * unit) for r in range(1, n_dp)]

    own = project(activations, out_grads, proj_in, proj_out, half)
    member, live, count = masks(lengths, own)
    other = swap(own, mesh, core_bit)
    own, other, live = lax.optimization_barrier((own, other, live))

    factor = fisher(live, own, other)
    factor, own, other = lax.optimization_barrier((factor, own, other))
    blocks = example_grads(member, count, own, other)[None]
    groups_of = {"x": query_bits, "1": dp_bits[:1], "2": dp_bits[1:]}
    steps = [bit | core_bit for name in ORDER for bit in groups_of[name]]

    def beside(stage, factor, blocks, fetched):
        i = stage - E_STAGE
        if 0 <= i < len(query_bits):
            blocks = hold(blocks, factor)
            blocks = jnp.concatenate([blocks, swap(blocks, mesh, query_bits[i] | core_bit)], axis=0)
        if stage in Y_STAGES:
            first, end = ((1, 2), (2, n_dp - 1))[Y_STAGES.index(stage)]
            for r in range(first, end):
                fetched[r] = hold(fetched[r], factor)
                for bit in group_bits:
                    fetched[r] = jnp.concatenate([fetched[r], swap(fetched[r], mesh, bit)], axis=0)
        return blocks

    for step, mask in enumerate(steps):
        blocks = beside(step, factor, blocks, fetched)
        received = swap(factor, mesh, mask)
        if step < len(steps) - 1:
            factor = factor + received
    arranged = arrange_examples(blocks, n_query)
    arranged, received = lax.optimization_barrier((arranged, received))
    both = condition(arranged, *inverses(factor, received), queries.shape[2])

    high, low = split_queries(groups, queries, fetched)
    scores = score(both, high, low)
    return place(queries.shape[1] // 2, scores, swap(scores, mesh, core_bit))


def solution(mesh):
    in_specs = (
        P(("grp", "dp", "query"), "proj"),
        P(("grp", "dp", "query"), "proj"),
        P("proj", None),
        P("proj", None),
        P(("grp", "dp", "query"), None),
        P("query", "dp", None),
    )
    out_specs = P(("grp", "dp"), "query")
    return jax.shard_map(
        functools.partial(body, mesh), mesh=mesh, in_specs=in_specs, out_specs=out_specs, check_vma=False
    )
```

```python
import functools
import math

import jax
import jax.numpy as jnp
from jax import lax
from jax.experimental import pallas as pl
from jax.experimental.pallas import tpu as pltpu
from jax.sharding import PartitionSpec as P

F32 = jnp.float32
BF16 = jnp.bfloat16
HIGHEST = lax.Precision.HIGHEST
NT = (((1,), (1,)), ((), ()))
AXES = ("grp", "dp", "query", "proj")
MIB = 2**20
CHUNK = 256
QUERY_STEP = 1


def swap(value, mesh, mask):
    count = math.prod(mesh.shape[axis] for axis in AXES)
    return lax.ppermute(value, AXES, [(i, i ^ mask) for i in range(count)])


def bits_of(size):
    return [1 << b for b in range(size.bit_length() - 1)]


def pick_kernel(groups, queries_hbm, half_ref, piece_ref, sems):
    half, piece = half_ref.shape[0], piece_ref.shape[0]
    core = lax.axis_index("proj")
    index = core * groups + lax.axis_index("grp")
    copies = [
        pltpu.make_async_copy(queries_hbm.at[0, pl.ds(pl.multiple_of(core * half, 8), half)], half_ref, sems.at[0]),
        pltpu.make_async_copy(queries_hbm.at[0, pl.ds(pl.multiple_of(index * piece, 8), piece)], piece_ref, sems.at[1]),
    ]
    for copy in copies:
        copy.start()
    for copy in copies:
        copy.wait()


def pick_queries(queries, groups):
    rows, columns = queries.shape[1:]
    return pl.pallas_call(
        functools.partial(pick_kernel, groups),
        out_shape=tuple(jax.ShapeDtypeStruct((rows // n, columns), F32) for n in (2, 2 * groups)),
        in_specs=[pl.BlockSpec(memory_space=pl.ANY)],
        out_specs=(pl.BlockSpec(memory_space=pltpu.VMEM),) * 2,
        scratch_shapes=[pltpu.SemaphoreType.DMA((2,))],
        compiler_params=pltpu.CompilerParams(vmem_limit_bytes=4 * MIB),
        cost_estimate=pl.CostEstimate(flops=4 * 10**9, bytes_accessed=10**6, transcendentals=0),
        name="pick_queries",
    )(pltpu.with_memory_space_constraint(queries, pltpu.HBM))


def project_kernel(a_ref, g_ref, p_in_ref, p_out_ref, after_ref, out_ref):
    width = p_in_ref.shape[0]
    out_ref[0:width, :] = lax.dot_general(a_ref[...], p_in_ref[...], NT, preferred_element_type=F32).T
    out_ref[width : 2 * width, :] = lax.dot_general(g_ref[...], p_out_ref[...], NT, preferred_element_type=F32).T


def project(activations, out_grads, proj_in, proj_out, after):
    return pl.pallas_call(
        project_kernel,
        out_shape=jax.ShapeDtypeStruct((2 * proj_in.shape[1], activations.shape[0]), F32),
        in_specs=[pl.BlockSpec(memory_space=pltpu.VMEM)] * 4 + [pl.BlockSpec(memory_space=pl.ANY)],
        out_specs=pl.BlockSpec(memory_space=pltpu.VMEM),
        compiler_params=pltpu.CompilerParams(vmem_limit_bytes=16 * MIB),
        name="project",
    )(activations, out_grads, proj_in.T, proj_out.T, after)


def masks_kernel(lengths_ref, after_ref, member_ref, live_ref, count_ref):
    examples, slots = member_ref.shape
    index = lax.broadcasted_iota(jnp.int32, (examples, 1), 0)
    starts = jnp.zeros((examples, 1), jnp.int32)
    counts = jnp.zeros((examples, 1), jnp.int32)
    begin = jnp.int32(0)
    for e in range(examples):
        length = lengths_ref[0, e]
        starts = jnp.where(index == e, begin, starts)
        counts = jnp.where(index == e, length, counts)
        begin = begin + length
    slot = lax.broadcasted_iota(jnp.int32, (examples, slots), 1)
    member_ref[...] = jnp.where((slot >= starts) & (slot < starts + counts), 1.0, 0.0).astype(BF16)
    live_ref[...] = jnp.where(slot[0:8] < begin, 1.0, 0.0)
    count_ref[...] = jnp.broadcast_to(counts.astype(F32), count_ref.shape)


def masks(lengths, after):
    examples, slots = lengths.shape[1] - 1, after.shape[1]
    return pl.pallas_call(
        masks_kernel,
        out_shape=(
            jax.ShapeDtypeStruct((examples, slots), BF16),
            jax.ShapeDtypeStruct((8, slots), F32),
            jax.ShapeDtypeStruct((examples, 128), F32),
        ),
        in_specs=[pl.BlockSpec(memory_space=pltpu.SMEM), pl.BlockSpec(memory_space=pl.ANY)],
        out_specs=(pl.BlockSpec(memory_space=pltpu.VMEM),) * 3,
        compiler_params=pltpu.CompilerParams(vmem_limit_bytes=4 * MIB),
        cost_estimate=pl.CostEstimate(flops=2 * 10**9, bytes_accessed=10**6, transcendentals=0),
        name="masks",
    )(lengths, after)


def fisher_kernel(live_ref, own_ref, other_ref, out_ref):
    width = out_ref.shape[0]
    both = own_ref[...] + other_ref[...]
    gram = lax.dot_general(both * live_ref[0:1, :], both, NT, precision=HIGHEST, preferred_element_type=F32)
    out_ref[...] = jnp.zeros_like(out_ref)
    out_ref[:, 0:width] = gram[0:width, 0:width]
    out_ref[:, width : 2 * width] = gram[width : 2 * width, width : 2 * width]


def fisher(live, own, other):
    width = own.shape[0] // 2
    return pl.pallas_call(
        fisher_kernel,
        out_shape=jax.ShapeDtypeStruct((width, 128), F32),
        in_specs=[pl.BlockSpec(memory_space=pltpu.VMEM)] * 3,
        out_specs=pl.BlockSpec(memory_space=pltpu.VMEM),
        compiler_params=pltpu.CompilerParams(vmem_limit_bytes=8 * MIB),
        name="fisher",
    )(live, own, other)


def split3(value):
    high = value.astype(BF16)
    rest = value - high.astype(F32)
    middle = rest.astype(BF16)
    return high, middle, (rest - middle.astype(F32)).astype(BF16)


def examples_kernel(member_ref, count_ref, own_ref, other_ref, out_ref):
    width = own_ref.shape[0] // 2
    both = own_ref[...] + other_ref[...]
    inputs, outputs = both[0:width], both[width : 2 * width]
    member, divisor = member_ref[...], count_ref[:, 0:1]
    group = 8
    for first in range(0, width, group):
        outer = jnp.concatenate([outputs[i : i + 1] * inputs for i in range(first, first + group)], axis=0)
        total = None
        for piece in reversed(split3(outer)):
            part = lax.dot_general(member, piece, NT, preferred_element_type=F32)
            total = part if total is None else total + part
        out_ref[:, first * width : (first + group) * width] = total / divisor


def example_grads(member, count, own, other):
    width = own.shape[0] // 2
    return pl.pallas_call(
        examples_kernel,
        out_shape=jax.ShapeDtypeStruct((member.shape[0], width * width), F32),
        in_specs=[pl.BlockSpec(memory_space=pltpu.VMEM)] * 4,
        out_specs=pl.BlockSpec(memory_space=pltpu.VMEM),
        compiler_params=pltpu.CompilerParams(vmem_limit_bytes=8 * MIB),
        cost_estimate=pl.CostEstimate(flops=2 * 10**9, bytes_accessed=10**6, transcendentals=0),
        name="examples",
    )(member, count, own, other)


def split2(value):
    high = value.astype(BF16)
    return high, (value - high.astype(F32)).astype(BF16)


def turn_pairs(load, scratch, width):
    columns, count = scratch.shape
    for c in range(columns // CHUNK):
        scratch[c * CHUNK : (c + 1) * CHUNK, :] = load(c).T
    chunks = []
    for c in range(columns // CHUNK):
        lines = range(c * CHUNK // width, (c + 1) * CHUNK // width)
        chunks.append(jnp.concatenate([scratch[pl.ds(j, width, stride=width), :] for j in lines], axis=0).T)
    return jnp.concatenate(chunks, axis=0)


def arrange_examples_kernel(n_query, blocks_ref, *refs):
    out_refs, (rows, scratch) = refs[:-2], refs[-2:]
    blocks, examples, columns = blocks_ref.shape
    query = lax.axis_index("query")
    for b in range(blocks):
        place = (b // n_query) * n_query + (query ^ (b % n_query))
        rows[pl.ds(pl.multiple_of(place * examples, 8), examples), :] = blocks_ref[b]
    width = math.isqrt(columns)
    turned = turn_pairs(lambda c: rows[:, c * CHUNK : (c + 1) * CHUNK], scratch, width)
    for out_ref, piece in zip(out_refs, split3(turned)):
        out_ref[...] = piece


def arrange_examples(blocks, n_query):
    number, examples, columns = blocks.shape
    count = number * examples
    shape = jax.ShapeDtypeStruct((count * columns // CHUNK, CHUNK), BF16)
    return pl.pallas_call(
        functools.partial(arrange_examples_kernel, n_query),
        out_shape=(shape,) * 3,
        in_specs=[pl.BlockSpec(memory_space=pltpu.VMEM)],
        out_specs=(pl.BlockSpec(memory_space=pltpu.VMEM),) * 3,
        scratch_shapes=[pltpu.VMEM((count, columns), F32), pltpu.VMEM((columns, count), F32)],
        compiler_params=pltpu.CompilerParams(vmem_limit_bytes=12 * MIB),
        name="arrange_examples",
    )(blocks)


def put_queries(first, groups, refs, high_ref, low_ref, half):
    piece = half // groups
    place, group, core = lax.axis_index("dp"), lax.axis_index("grp"), lax.axis_index("proj")

    def put(start, value):
        at = pl.ds(pl.multiple_of(start, 16), value.shape[0])
        high_ref[at, :], low_ref[at, :] = split2(value)

    for r, ref in enumerate(refs, first):
        if r == 0:
            put(place * half, ref[0, pl.ds(pl.multiple_of(core * half, 8), half), :])
        elif r == 1:
            put((place ^ r) * half, ref[...])
        else:
            for g in range(groups):
                put((place ^ r) * half + (group ^ g) * piece, ref[g * piece : (g + 1) * piece, :])


def inverse_tiled(fisher_sum):
    width = fisher_sum.shape[0]
    row = lax.broadcasted_iota(jnp.int32, (width, width), 0)
    column = lax.broadcasted_iota(jnp.int32, (width, width), 1)
    trace = jnp.sum(jnp.where(row == column, fisher_sum, 0.0), keepdims=True)
    damped = fisher_sum * (width / trace) + jnp.where(row == column, 1.0, 0.0)
    state = jnp.concatenate([damped] * (128 // width), axis=1)
    lane = lax.broadcasted_iota(jnp.int32, state.shape, 1) % width
    sublane = lax.broadcasted_iota(jnp.int32, state.shape, 0)
    top = lane[0:1]

    def apply(m, x, y):
        return m[0][0] * x + m[0][1] * y, m[1][0] * x + m[1][1] * y

    def invert(m):
        scale = 1.0 / (m[0][0] * m[1][1] - m[0][1] * m[1][0])
        return (m[1][1] * scale, -m[0][1] * scale), (-m[1][0] * scale, m[0][0] * scale)

    for k in range(0, width, 4):
        columns = [jnp.broadcast_to(state[:, k + c : k + c + 1], state.shape) for c in range(4)]
        pivot = [[columns[c][k + r : k + r + 1, :] for c in range(4)] for r in range(4)]
        inside = (top >= k) & (top < k + 4)
        rows = [
            jnp.where(top == k + r, 1.0, jnp.where(inside, 0.0, state[k + r : k + r + 1, :])) for r in range(4)
        ]
        corner = invert((pivot[0][0:2], pivot[1][0:2]))
        upper = apply(corner, rows[0], rows[1])
        right = [apply(corner, pivot[0][c], pivot[1][c]) for c in (2, 3)]
        schur = [
            [pivot[r][c] - pivot[r][0] * right[c - 2][0] - pivot[r][1] * right[c - 2][1] for c in (2, 3)] for r in (2, 3)
        ]
        lower = apply(
            invert(schur), *(rows[r] - pivot[r][0] * upper[0] - pivot[r][1] * upper[1] for r in (2, 3))
        )
        solved = [upper[r] - right[0][r] * lower[0] - right[1][r] * lower[1] for r in range(2)] + list(lower)
        change = columns[0] * solved[0] + columns[1] * solved[1] + columns[2] * solved[2] + columns[3] * solved[3]
        state = jnp.where((lane >= k) & (lane < k + 4), 0.0, state) - change
        for r in range(4):
            state = jnp.where(sublane == k + r, solved[r], state)
    return state


def block_diagonal(tiled):
    width, lanes = tiled.shape
    value = jnp.concatenate([jnp.concatenate([tiled] * (CHUNK // lanes), axis=1)] * (CHUNK // width), axis=0)
    row = lax.broadcasted_iota(jnp.int32, (CHUNK, CHUNK), 0) // width
    column = lax.broadcasted_iota(jnp.int32, (CHUNK, CHUNK), 1) // width
    return jnp.where(row == column, value, 0.0)


def inverses_kernel(own_ref, other_ref, in_ref, out_ref):
    width = own_ref.shape[0]
    total = own_ref[...] + other_ref[...]
    for ref, fisher_sum in ((in_ref, total[:, 0:width]), (out_ref, total[:, width : 2 * width])):
        for piece, value in enumerate(split3(block_diagonal(inverse_tiled(fisher_sum)))):
            ref[piece] = value


def inverses(own, other):
    shape = jax.ShapeDtypeStruct((3, CHUNK, CHUNK), BF16)
    return pl.pallas_call(
        inverses_kernel,
        out_shape=(shape, shape),
        in_specs=[pl.BlockSpec(memory_space=pltpu.VMEM)] * 2,
        out_specs=(pl.BlockSpec(memory_space=pltpu.VMEM),) * 2,
        compiler_params=pltpu.CompilerParams(vmem_limit_bytes=8 * MIB),
        name="inverses",
    )(own, other)


def times_blocks(high, middle, low, blocks_ref):
    rows = high.shape[0]
    by_high = jnp.dot(jnp.concatenate([high, middle, low], axis=0), blocks_ref[0], preferred_element_type=F32)
    by_middle = jnp.dot(jnp.concatenate([high, middle], axis=0), blocks_ref[1], preferred_element_type=F32)
    by_low = jnp.dot(high, blocks_ref[2], preferred_element_type=F32)
    small = by_high[2 * rows :] + by_middle[rows:] + by_low
    return by_high[0:rows] + (by_high[rows : 2 * rows] + by_middle[0:rows] + small)


def condition_kernel(high_ref, middle_ref, low_ref, in_ref, out_ref, both_ref, scratch):
    columns, count = scratch.shape
    left = times_blocks(high_ref[...], middle_ref[...], low_ref[...], out_ref)
    turned = turn_pairs(lambda c: left[c * count : (c + 1) * count], scratch, math.isqrt(columns))
    high, low = split2(times_blocks(*split3(turned), in_ref))
    for c in range(columns // CHUNK):
        both_ref[c, 0:count] = high[c * count : (c + 1) * count]
        both_ref[c, count:] = low[c * count : (c + 1) * count]


def condition(pieces, in_blocks, out_blocks, columns):
    count = pieces[0].shape[0] * CHUNK // columns
    return pl.pallas_call(
        condition_kernel,
        out_shape=jax.ShapeDtypeStruct((columns // CHUNK, 2 * count, CHUNK), BF16),
        in_specs=[pl.BlockSpec(memory_space=pltpu.VMEM)] * 5,
        out_specs=pl.BlockSpec(memory_space=pltpu.VMEM),
        scratch_shapes=[pltpu.VMEM((columns, count), F32)],
        compiler_params=pltpu.CompilerParams(vmem_limit_bytes=8 * MIB),
        cost_estimate=pl.CostEstimate(flops=2 * 10**9, bytes_accessed=10**6, transcendentals=0),
        name="condition",
    )(*pieces, in_blocks, out_blocks)


def score_kernel(parts, groups, half, both_ref, *refs):
    query_refs, (scores_ref, q_high_ref, q_low_ref) = refs[:parts], refs[parts:]
    put_queries(0, groups, query_refs, q_high_ref, q_low_ref, half)
    chunks, count = both_ref.shape[0], both_ref.shape[1] // 2
    total = None
    for c in range(chunks):
        cols = slice(c * CHUNK, (c + 1) * CHUNK)
        by_high = lax.dot_general(both_ref[c], q_high_ref[:, cols], NT, preferred_element_type=F32)
        by_low = lax.dot_general(both_ref[c, 0:count], q_low_ref[:, cols], NT, preferred_element_type=F32)
        part = by_high[0:count] + (by_high[count:] + by_low)
        total = part if total is None else total + part
    scores_ref[...] = total * (1.0 / math.isqrt(chunks * CHUNK))


def score(groups, both, own, fetched):
    parts = 1 + len(fetched)
    half, columns = own.shape[1] // 2, own.shape[2]
    return pl.pallas_call(
        functools.partial(score_kernel, parts, groups, half),
        out_shape=jax.ShapeDtypeStruct((both.shape[1] // 2, parts * half), F32),
        in_specs=[pl.BlockSpec(memory_space=pltpu.VMEM)] * (1 + parts),
        out_specs=pl.BlockSpec(memory_space=pltpu.VMEM),
        scratch_shapes=[pltpu.VMEM((parts * half, columns), BF16)] * 2,
        compiler_params=pltpu.CompilerParams(vmem_limit_bytes=(6 + parts) * MIB),
        name="score",
    )(both, own, *fetched)


def place_kernel(half, kept_ref, received_ref, out_ref):
    core = lax.axis_index("proj")
    kept, received = kept_ref[...], received_ref[...]
    first = jnp.where(core == 0, kept, received)
    second = jnp.where(core == 0, received, kept)
    for k in range(kept.shape[1] // half):
        at = slice(k * half, (k + 1) * half)
        out_ref[:, 2 * k * half : 2 * (k + 1) * half] = jnp.concatenate([first[:, at], second[:, at]], axis=1)


def place(half, kept, received):
    rows, columns = kept.shape
    return pl.pallas_call(
        functools.partial(place_kernel, half),
        out_shape=jax.ShapeDtypeStruct((rows, 2 * columns), F32),
        in_specs=[pl.BlockSpec(memory_space=pltpu.VMEM)] * 2,
        out_specs=pl.BlockSpec(memory_space=pltpu.VMEM),
        compiler_params=pltpu.CompilerParams(vmem_limit_bytes=8 * MIB),
        name="place",
    )(kept, received)


def hold_kernel(value_ref, after_ref, out_ref):
    out_ref[...] = value_ref[...]


def hold(value, after):
    return pl.pallas_call(
        hold_kernel,
        out_shape=jax.ShapeDtypeStruct(value.shape, value.dtype),
        in_specs=[pl.BlockSpec(memory_space=pltpu.VMEM), pl.BlockSpec(memory_space=pl.ANY)],
        out_specs=pl.BlockSpec(memory_space=pltpu.VMEM),
        compiler_params=pltpu.CompilerParams(vmem_limit_bytes=4 * MIB),
        cost_estimate=pl.CostEstimate(flops=10**9, bytes_accessed=10**6, transcendentals=0),
        name="hold",
    )(value, after)


ORDER = "x21"
E_STAGE = 0
Y_STAGES = (1,)


def body(mesh, activations, out_grads, proj_in, proj_out, lengths, queries):
    groups, n_dp, n_query = mesh.shape["grp"], mesh.shape["dp"], mesh.shape["query"]
    core_bit = 1
    unit = 2 * n_query
    query_bits = [2 * b for b in bits_of(n_query)]
    dp_bits = [b * unit for b in bits_of(n_dp)]
    group_bits = [b * unit * n_dp for b in bits_of(groups)]

    half, piece = pick_queries(queries, groups)
    fetched = [swap(half if r == 1 else piece, mesh, r * unit) for r in range(1, n_dp)]

    own = project(activations, out_grads, proj_in, proj_out, half)
    member, live, count = masks(lengths, own)
    other = swap(own, mesh, core_bit)
    own, other, live = lax.optimization_barrier((own, other, live))

    factor = fisher(live, own, other)
    factor, own, other = lax.optimization_barrier((factor, own, other))
    blocks = example_grads(member, count, own, other)[None]
    groups_of = {"x": query_bits, "1": dp_bits[:1], "2": dp_bits[1:]}
    steps = [bit | core_bit for name in ORDER for bit in groups_of[name]]

    def beside(stage, factor, blocks, fetched):
        i = stage - E_STAGE
        if 0 <= i < len(query_bits):
            blocks = hold(blocks, factor)
            blocks = jnp.concatenate([blocks, swap(blocks, mesh, query_bits[i] | core_bit)], axis=0)
        if stage in Y_STAGES:
            first, end = (1, n_dp - 1)
            for r in range(first, end):
                fetched[r] = hold(fetched[r], factor)
                for bit in group_bits:
                    fetched[r] = jnp.concatenate([fetched[r], swap(fetched[r], mesh, bit)], axis=0)
        return blocks

    for step, mask in enumerate(steps):
        blocks = beside(step, factor, blocks, fetched)
        received = swap(factor, mesh, mask)
        if step < len(steps) - 1:
            factor = factor + received
    arranged = arrange_examples(blocks, n_query)
    arranged, received = lax.optimization_barrier((arranged, received))
    both = condition(arranged, *inverses(factor, received), queries.shape[2])

    scores = score(groups, both, queries, fetched)
    return place(queries.shape[1] // 2, scores, swap(scores, mesh, core_bit))


def solution(mesh):
    in_specs = (
        P(("grp", "dp", "query"), "proj"),
        P(("grp", "dp", "query"), "proj"),
        P("proj", None),
        P("proj", None),
        P(("grp", "dp", "query"), None),
        P("query", "dp", None),
    )
    out_specs = P(("grp", "dp"), "query")
    return jax.shard_map(
        functools.partial(body, mesh), mesh=mesh, in_specs=in_specs, out_specs=out_specs, check_vma=False
    )
```

```python
import functools
import math

import jax
import jax.numpy as jnp
from jax import lax
from jax.experimental import pallas as pl
from jax.experimental.pallas import tpu as pltpu
from jax.sharding import PartitionSpec as P

F32 = jnp.float32
BF16 = jnp.bfloat16
HIGHEST = lax.Precision.HIGHEST
NT = (((1,), (1,)), ((), ()))
AXES = ("grp", "dp", "query", "proj")
MIB = 2**20
CHUNK = 256
QUERY_STEP = 1


def swap(value, mesh, mask):
    count = math.prod(mesh.shape[axis] for axis in AXES)
    return lax.ppermute(value, AXES, [(i, i ^ mask) for i in range(count)])


def bits_of(size):
    return [1 << b for b in range(size.bit_length() - 1)]


def pick_kernel(groups, queries_hbm, half_ref, piece_ref, sems):
    half, piece = half_ref.shape[0], piece_ref.shape[0]
    core = 1 - lax.axis_index("proj")
    index = core * groups + lax.axis_index("grp")
    copies = [
        pltpu.make_async_copy(queries_hbm.at[0, pl.ds(pl.multiple_of(core * half, 8), half)], half_ref, sems.at[0]),
        pltpu.make_async_copy(queries_hbm.at[0, pl.ds(pl.multiple_of(index * piece, 8), piece)], piece_ref, sems.at[1]),
    ]
    for copy in copies:
        copy.start()
    for copy in copies:
        copy.wait()


def pick_queries(queries, groups):
    rows, columns = queries.shape[1:]
    return pl.pallas_call(
        functools.partial(pick_kernel, groups),
        out_shape=tuple(jax.ShapeDtypeStruct((rows // n, columns), F32) for n in (2, 2 * groups)),
        in_specs=[pl.BlockSpec(memory_space=pl.ANY)],
        out_specs=(pl.BlockSpec(memory_space=pltpu.VMEM),) * 2,
        scratch_shapes=[pltpu.SemaphoreType.DMA((2,))],
        compiler_params=pltpu.CompilerParams(vmem_limit_bytes=4 * MIB),
        cost_estimate=pl.CostEstimate(flops=4 * 10**9, bytes_accessed=10**6, transcendentals=0),
        name="pick_queries",
    )(pltpu.with_memory_space_constraint(queries, pltpu.HBM))


def project_kernel(a_ref, g_ref, p_in_ref, p_out_ref, after_ref, out_ref):
    width = p_in_ref.shape[0]
    out_ref[0:width, :] = lax.dot_general(a_ref[...], p_in_ref[...], NT, preferred_element_type=F32).T
    out_ref[width : 2 * width, :] = lax.dot_general(g_ref[...], p_out_ref[...], NT, preferred_element_type=F32).T


def project(activations, out_grads, proj_in, proj_out, after):
    return pl.pallas_call(
        project_kernel,
        out_shape=jax.ShapeDtypeStruct((2 * proj_in.shape[1], activations.shape[0]), F32),
        in_specs=[pl.BlockSpec(memory_space=pltpu.VMEM)] * 4 + [pl.BlockSpec(memory_space=pl.ANY)],
        out_specs=pl.BlockSpec(memory_space=pltpu.VMEM),
        compiler_params=pltpu.CompilerParams(vmem_limit_bytes=16 * MIB),
        name="project",
    )(activations, out_grads, proj_in.T, proj_out.T, after)


def masks_kernel(lengths_ref, after_ref, member_ref, live_ref, count_ref):
    examples, slots = member_ref.shape
    index = lax.broadcasted_iota(jnp.int32, (examples, 1), 0)
    starts = jnp.zeros((examples, 1), jnp.int32)
    counts = jnp.zeros((examples, 1), jnp.int32)
    begin = jnp.int32(0)
    for e in range(examples):
        length = lengths_ref[0, e]
        starts = jnp.where(index == e, begin, starts)
        counts = jnp.where(index == e, length, counts)
        begin = begin + length
    slot = lax.broadcasted_iota(jnp.int32, (examples, slots), 1)
    member_ref[...] = jnp.where((slot >= starts) & (slot < starts + counts), 1.0, 0.0).astype(BF16)
    live_ref[...] = jnp.where(slot[0:8] < begin, 1.0, 0.0)
    count_ref[...] = jnp.broadcast_to(counts.astype(F32), count_ref.shape)


def masks(lengths, after):
    examples, slots = lengths.shape[1] - 1, after.shape[1]
    return pl.pallas_call(
        masks_kernel,
        out_shape=(
            jax.ShapeDtypeStruct((examples, slots), BF16),
            jax.ShapeDtypeStruct((8, slots), F32),
            jax.ShapeDtypeStruct((examples, 128), F32),
        ),
        in_specs=[pl.BlockSpec(memory_space=pltpu.SMEM), pl.BlockSpec(memory_space=pl.ANY)],
        out_specs=(pl.BlockSpec(memory_space=pltpu.VMEM),) * 3,
        compiler_params=pltpu.CompilerParams(vmem_limit_bytes=4 * MIB),
        cost_estimate=pl.CostEstimate(flops=2 * 10**9, bytes_accessed=10**6, transcendentals=0),
        name="masks",
    )(lengths, after)


def fisher_kernel(live_ref, own_ref, other_ref, out_ref):
    width = out_ref.shape[0]
    both = own_ref[...] + other_ref[...]
    gram = lax.dot_general(both * live_ref[0:1, :], both, NT, precision=HIGHEST, preferred_element_type=F32)
    out_ref[...] = jnp.zeros_like(out_ref)
    out_ref[:, 0:width] = gram[0:width, 0:width]
    out_ref[:, width : 2 * width] = gram[width : 2 * width, width : 2 * width]


def fisher(live, own, other):
    width = own.shape[0] // 2
    return pl.pallas_call(
        fisher_kernel,
        out_shape=jax.ShapeDtypeStruct((width, 128), F32),
        in_specs=[pl.BlockSpec(memory_space=pltpu.VMEM)] * 3,
        out_specs=pl.BlockSpec(memory_space=pltpu.VMEM),
        compiler_params=pltpu.CompilerParams(vmem_limit_bytes=8 * MIB),
        name="fisher",
    )(live, own, other)


def split3(value):
    high = value.astype(BF16)
    rest = value - high.astype(F32)
    middle = rest.astype(BF16)
    return high, middle, (rest - middle.astype(F32)).astype(BF16)


def examples_kernel(member_ref, count_ref, own_ref, other_ref, out_ref):
    width = own_ref.shape[0] // 2
    both = own_ref[...] + other_ref[...]
    inputs, outputs = both[0:width], both[width : 2 * width]
    member, divisor = member_ref[...], count_ref[:, 0:1]
    group = 8
    for first in range(0, width, group):
        outer = jnp.concatenate([outputs[i : i + 1] * inputs for i in range(first, first + group)], axis=0)
        total = None
        for piece in reversed(split3(outer)):
            part = lax.dot_general(member, piece, NT, preferred_element_type=F32)
            total = part if total is None else total + part
        out_ref[:, first * width : (first + group) * width] = total / divisor


def example_grads(member, count, own, other):
    width = own.shape[0] // 2
    return pl.pallas_call(
        examples_kernel,
        out_shape=jax.ShapeDtypeStruct((member.shape[0], width * width), F32),
        in_specs=[pl.BlockSpec(memory_space=pltpu.VMEM)] * 4,
        out_specs=pl.BlockSpec(memory_space=pltpu.VMEM),
        compiler_params=pltpu.CompilerParams(vmem_limit_bytes=8 * MIB),
        cost_estimate=pl.CostEstimate(flops=2 * 10**9, bytes_accessed=10**6, transcendentals=0),
        name="examples",
    )(member, count, own, other)


def split2(value):
    high = value.astype(BF16)
    return high, (value - high.astype(F32)).astype(BF16)


def turn_pairs(load, scratch, width):
    columns, count = scratch.shape
    for c in range(columns // CHUNK):
        scratch[c * CHUNK : (c + 1) * CHUNK, :] = load(c).T
    chunks = []
    for c in range(columns // CHUNK):
        lines = range(c * CHUNK // width, (c + 1) * CHUNK // width)
        chunks.append(jnp.concatenate([scratch[pl.ds(j, width, stride=width), :] for j in lines], axis=0).T)
    return jnp.concatenate(chunks, axis=0)


def arrange_examples_kernel(n_query, blocks_ref, *refs):
    out_refs, (rows, scratch) = refs[:-2], refs[-2:]
    blocks, examples, columns = blocks_ref.shape
    query = lax.axis_index("query")
    for b in range(blocks):
        place = (b // n_query) * n_query + (query ^ (b % n_query))
        rows[pl.ds(pl.multiple_of(place * examples, 8), examples), :] = blocks_ref[b]
    width = math.isqrt(columns)
    turned = turn_pairs(lambda c: rows[:, c * CHUNK : (c + 1) * CHUNK], scratch, width)
    for out_ref, piece in zip(out_refs, split3(turned)):
        out_ref[...] = piece


def arrange_examples(blocks, n_query):
    number, examples, columns = blocks.shape
    count = number * examples
    shape = jax.ShapeDtypeStruct((count * columns // CHUNK, CHUNK), BF16)
    return pl.pallas_call(
        functools.partial(arrange_examples_kernel, n_query),
        out_shape=(shape,) * 3,
        in_specs=[pl.BlockSpec(memory_space=pltpu.VMEM)],
        out_specs=(pl.BlockSpec(memory_space=pltpu.VMEM),) * 3,
        scratch_shapes=[pltpu.VMEM((count, columns), F32), pltpu.VMEM((columns, count), F32)],
        compiler_params=pltpu.CompilerParams(vmem_limit_bytes=12 * MIB),
        name="arrange_examples",
    )(blocks)


def split_near_kernel(own_ref, near_ref, high_ref, low_ref):
    half = near_ref.shape[0]
    start = pl.multiple_of(lax.axis_index("proj") * half, 8)
    for i, value in enumerate((own_ref[0, pl.ds(start, half), :], near_ref[...])):
        at = slice(i * half, (i + 1) * half)
        high_ref[at, :], low_ref[at, :] = split2(value)


def split_near(own, near):
    half, columns = near.shape
    shape = jax.ShapeDtypeStruct((2 * half, columns), BF16)
    return pl.pallas_call(
        split_near_kernel,
        out_shape=(shape, shape),
        in_specs=[pl.BlockSpec(memory_space=pltpu.VMEM)] * 2,
        out_specs=(pl.BlockSpec(memory_space=pltpu.VMEM),) * 2,
        compiler_params=pltpu.CompilerParams(vmem_limit_bytes=6 * MIB),
        name="split_near",
    )(own, near)


def damped(fisher_sum):
    width = fisher_sum.shape[0]
    row = lax.broadcasted_iota(jnp.int32, (width, width), 0)
    column = lax.broadcasted_iota(jnp.int32, (width, width), 1)
    trace = jnp.sum(jnp.where(row == column, fisher_sum, 0.0), keepdims=True)
    return fisher_sum * (width / trace) + jnp.where(row == column, 1.0, 0.0)


def inverse_pair(pair):
    width, group = pair.shape[0], 8
    both = jnp.concatenate([damped(pair[:, 0:width]), damped(pair[:, width : 2 * width])], axis=1)
    state = jnp.concatenate([both] * (128 // (2 * width)), axis=1)
    state = [state[i : i + group] for i in range(0, width, group)]
    lane = lax.broadcasted_iota(jnp.int32, (group, 128), 1)
    own = lane % width
    first = lane - own
    sublane = lax.broadcasted_iota(jnp.int32, (group, 128), 0)

    def spread(value, index):
        return jnp.take_along_axis(value, index, axis=1, mode="promise_in_bounds")

    columns = [[spread(part, first + c) for c in range(4)] for part in state]
    for k in range(0, width, 4):
        at, offset = k // group, k % group
        more = k + 4 < width
        ahead = [[spread(part, first + (k + 4 + c)) for c in range(4)] for part in state] if more else None
        inside = (own >= k) & (own < k + 4)

        def row(value, r):
            return value[offset + r : offset + r + 1, :]

        p = [[row(columns[at][c], r) for c in range(4)] for r in range(4)]
        scale = 1.0 / (p[0][0] * p[1][1] - p[0][1] * p[1][0])
        a = ((p[1][1] * scale, -p[0][1] * scale), (-p[1][0] * scale, p[0][0] * scale))
        right = [[a[r][0] * p[0][c] + a[r][1] * p[1][c] for r in range(2)] for c in (2, 3)]
        s = [[p[r][c] - (p[r][0] * right[c - 2][0] + p[r][1] * right[c - 2][1]) for c in (2, 3)] for r in (2, 3)]
        scale = 1.0 / (s[0][0] * s[1][1] - s[0][1] * s[1][0])
        d = ((s[1][1] * scale, -s[0][1] * scale), (-s[1][0] * scale, s[0][0] * scale))

        def solve(q):
            upper = [a[r][0] * q[0] + a[r][1] * q[1] for r in range(2)]
            rest = [q[r] - (p[r][0] * upper[0] + p[r][1] * upper[1]) for r in (2, 3)]
            lower = [d[r][0] * rest[0] + d[r][1] * rest[1] for r in range(2)]
            return [upper[r] - (right[0][r] * lower[0] + right[1][r] * lower[1]) for r in range(2)] + lower

        def step(i, value, solved):
            c = columns[i]
            value = value - ((c[0] * solved[0] + c[1] * solved[1]) + (c[2] * solved[2] + c[3] * solved[3]))
            if i == at:
                for r in range(4):
                    value = jnp.where(sublane == offset + r, solved[r], value)
            return value

        rows = [jnp.where(own[0:1] == k + r, 1.0, jnp.where(inside[0:1], 0.0, row(state[at], r))) for r in range(4)]
        solved = solve(rows)
        following = columns
        if more:
            solved_ahead = [solve([row(ahead[at][c], r) for r in range(4)]) for c in range(4)]
            following = [[step(i, ahead[i][c], solved_ahead[c]) for c in range(4)] for i in range(len(state))]
        state = [step(i, jnp.where(inside, 0.0, part), solved) for i, part in enumerate(state)]
        columns = following
    return [jnp.concatenate([spread(part, own + start) for part in state], axis=0) for start in (0, width)]


def block_diagonal(tiled):
    width, lanes = tiled.shape
    value = jnp.concatenate([jnp.concatenate([tiled] * (CHUNK // lanes), axis=1)] * (CHUNK // width), axis=0)
    row = lax.broadcasted_iota(jnp.int32, (CHUNK, CHUNK), 0) // width
    column = lax.broadcasted_iota(jnp.int32, (CHUNK, CHUNK), 1) // width
    return jnp.where(row == column, value, 0.0)


def inverses_kernel(own_ref, other_ref, in_ref, out_ref):
    width = own_ref.shape[0]
    total = own_ref[...] + other_ref[...]
    for ref, inverse in zip((in_ref, out_ref), inverse_pair(total[:, 0 : 2 * width])):
        for piece, value in enumerate(split3(block_diagonal(inverse))):
            ref[piece] = value


def inverses(own, other):
    shape = jax.ShapeDtypeStruct((3, CHUNK, CHUNK), BF16)
    return pl.pallas_call(
        inverses_kernel,
        out_shape=(shape, shape),
        in_specs=[pl.BlockSpec(memory_space=pltpu.VMEM)] * 2,
        out_specs=(pl.BlockSpec(memory_space=pltpu.VMEM),) * 2,
        compiler_params=pltpu.CompilerParams(vmem_limit_bytes=8 * MIB),
        name="inverses",
    )(own, other)


def times_blocks(high, middle, low, blocks_ref):
    rows = high.shape[0]
    by_high = jnp.dot(jnp.concatenate([high, middle, low], axis=0), blocks_ref[0], preferred_element_type=F32)
    by_middle = jnp.dot(jnp.concatenate([high, middle], axis=0), blocks_ref[1], preferred_element_type=F32)
    by_low = jnp.dot(high, blocks_ref[2], preferred_element_type=F32)
    small = by_high[2 * rows :] + by_middle[rows:] + by_low
    return by_high[0:rows] + (by_high[rows : 2 * rows] + by_middle[0:rows] + small)


def condition_kernel(high_ref, middle_ref, low_ref, in_ref, out_ref, both_ref, scratch):
    columns, count = scratch.shape
    left = times_blocks(high_ref[...], middle_ref[...], low_ref[...], out_ref)
    turned = turn_pairs(lambda c: left[c * count : (c + 1) * count], scratch, math.isqrt(columns))
    high, low = split2(times_blocks(*split3(turned), in_ref))
    for c in range(columns // CHUNK):
        both_ref[c, 0:count] = high[c * count : (c + 1) * count]
        both_ref[c, count:] = low[c * count : (c + 1) * count]


def condition(pieces, in_blocks, out_blocks, columns):
    count = pieces[0].shape[0] * CHUNK // columns
    return pl.pallas_call(
        condition_kernel,
        out_shape=jax.ShapeDtypeStruct((columns // CHUNK, 2 * count, CHUNK), BF16),
        in_specs=[pl.BlockSpec(memory_space=pltpu.VMEM)] * 5,
        out_specs=pl.BlockSpec(memory_space=pltpu.VMEM),
        scratch_shapes=[pltpu.VMEM((columns, count), F32)],
        compiler_params=pltpu.CompilerParams(vmem_limit_bytes=8 * MIB),
        cost_estimate=pl.CostEstimate(flops=2 * 10**9, bytes_accessed=10**6, transcendentals=0),
        name="condition",
    )(*pieces, in_blocks, out_blocks)


def score_kernel(groups, both_ref, near_high_ref, near_low_ref, *refs):
    fetched_refs, (scores_ref, high_ref, low_ref) = refs[:-3], refs[-3:]
    chunks, count = both_ref.shape[0], both_ref.shape[1] // 2
    near = near_high_ref.shape[0]
    half = fetched_refs[0].shape[0]
    piece = half // groups
    group = lax.axis_index("grp")
    for i, ref in enumerate(fetched_refs):
        for g in range(groups):
            at = pl.ds(pl.multiple_of(i * half + (group ^ g) * piece, 16), piece)
            high_ref[at, :], low_ref[at, :] = split2(ref[g * piece : (g + 1) * piece, :])
    for start, q_high_ref, q_low_ref in ((0, near_high_ref, near_low_ref), (near, high_ref, low_ref)):
        total = None
        for c in range(chunks):
            cols = slice(c * CHUNK, (c + 1) * CHUNK)
            by_high = lax.dot_general(both_ref[c], q_high_ref[:, cols], NT, preferred_element_type=F32)
            by_low = lax.dot_general(both_ref[c, 0:count], q_low_ref[:, cols], NT, preferred_element_type=F32)
            part = by_high[0:count] + (by_high[count:] + by_low)
            total = part if total is None else total + part
        scores_ref[:, start : start + total.shape[1]] = total * (1.0 / math.isqrt(chunks * CHUNK))


def score(groups, both, near, fetched):
    rows, columns = len(fetched) * fetched[0].shape[0], fetched[0].shape[1]
    return pl.pallas_call(
        functools.partial(score_kernel, groups),
        out_shape=jax.ShapeDtypeStruct((both.shape[1] // 2, near[0].shape[0] + rows), F32),
        in_specs=[pl.BlockSpec(memory_space=pltpu.VMEM)] * (3 + len(fetched)),
        out_specs=pl.BlockSpec(memory_space=pltpu.VMEM),
        scratch_shapes=[pltpu.VMEM((rows, columns), BF16)] * 2,
        compiler_params=pltpu.CompilerParams(vmem_limit_bytes=(8 + len(fetched)) * MIB),
        name="score",
    )(both, *near, *fetched)


def place_kernel(half, kept_ref, received_ref, out_ref):
    core = lax.axis_index("proj")
    kept, received = kept_ref[...], received_ref[...]
    first = jnp.where(core == 0, kept, received)
    second = jnp.where(core == 0, received, kept)
    for r in range(kept.shape[1] // half):
        at = slice(r * half, (r + 1) * half)
        start = pl.multiple_of((lax.axis_index("dp") ^ r) * 2 * half, 128)
        out_ref[:, pl.ds(start, 2 * half)] = jnp.concatenate([first[:, at], second[:, at]], axis=1)


def place(half, kept, received):
    rows, columns = kept.shape
    return pl.pallas_call(
        functools.partial(place_kernel, half),
        out_shape=jax.ShapeDtypeStruct((rows, 2 * columns), F32),
        in_specs=[pl.BlockSpec(memory_space=pltpu.VMEM)] * 2,
        out_specs=pl.BlockSpec(memory_space=pltpu.VMEM),
        compiler_params=pltpu.CompilerParams(vmem_limit_bytes=8 * MIB),
        name="place",
    )(kept, received)


def hold_kernel(value_ref, after_ref, out_ref):
    out_ref[...] = value_ref[...]


def hold(value, after):
    return pl.pallas_call(
        hold_kernel,
        out_shape=jax.ShapeDtypeStruct(value.shape, value.dtype),
        in_specs=[pl.BlockSpec(memory_space=pltpu.VMEM), pl.BlockSpec(memory_space=pl.ANY)],
        out_specs=pl.BlockSpec(memory_space=pltpu.VMEM),
        compiler_params=pltpu.CompilerParams(vmem_limit_bytes=4 * MIB),
        cost_estimate=pl.CostEstimate(flops=10**9, bytes_accessed=10**6, transcendentals=0),
        name="hold",
    )(value, after)


ORDER = "x21"
E_STAGE = 0
Y_STAGES = (1,)


def body(mesh, activations, out_grads, proj_in, proj_out, lengths, queries):
    groups, n_dp, n_query = mesh.shape["grp"], mesh.shape["dp"], mesh.shape["query"]
    core_bit = 1
    unit = 2 * n_query
    query_bits = [2 * b for b in bits_of(n_query)]
    dp_bits = [b * unit for b in bits_of(n_dp)]
    group_bits = [b * unit * n_dp for b in bits_of(groups)]

    half, piece = pick_queries(queries, groups)
    fetched = [swap(half if r == 1 else piece, mesh, r * unit | core_bit) for r in range(1, n_dp)]

    own = project(activations, out_grads, proj_in, proj_out, half)
    member, live, count = masks(lengths, own)
    other = swap(own, mesh, core_bit)
    own, other, live = lax.optimization_barrier((own, other, live))

    factor = fisher(live, own, other)
    factor, own, other = lax.optimization_barrier((factor, own, other))
    blocks = example_grads(member, count, own, other)[None]
    groups_of = {"x": query_bits, "1": dp_bits[:1], "2": dp_bits[1:]}
    steps = [bit | core_bit for name in ORDER for bit in groups_of[name]]

    def beside(stage, factor, blocks, fetched):
        i = stage - E_STAGE
        if 0 <= i < len(query_bits):
            blocks = hold(blocks, factor)
            blocks = jnp.concatenate([blocks, swap(blocks, mesh, query_bits[i] | core_bit)], axis=0)
        if stage in Y_STAGES:
            first, end = (1, n_dp - 1)
            for r in range(first, end):
                fetched[r] = hold(fetched[r], factor)
                for bit in group_bits:
                    fetched[r] = jnp.concatenate([fetched[r], swap(fetched[r], mesh, bit)], axis=0)
        return blocks

    for step, mask in enumerate(steps):
        blocks = beside(step, factor, blocks, fetched)
        received = swap(factor, mesh, mask)
        if step < len(steps) - 1:
            factor = factor + received
    arranged = arrange_examples(blocks, n_query)
    near = split_near(queries, fetched[0])
    arranged, near, received = lax.optimization_barrier((arranged, near, received))
    both = condition(arranged, *inverses(factor, received), queries.shape[2])

    scores = score(groups, both, near, fetched[1:])
    return place(queries.shape[1] // 2, scores, swap(scores, mesh, core_bit))


def solution(mesh):
    in_specs = (
        P(("grp", "dp", "query"), "proj"),
        P(("grp", "dp", "query"), "proj"),
        P("proj", None),
        P("proj", None),
        P(("grp", "dp", "query"), None),
        P("query", "dp", None),
    )
    out_specs = P(("grp", "dp"), "query")
    return jax.shard_map(
        functools.partial(body, mesh), mesh=mesh, in_specs=in_specs, out_specs=out_specs, check_vma=False
    )
```

```python
import functools
import math

import jax
import jax.numpy as jnp
from jax import lax
from jax.experimental import pallas as pl
from jax.experimental.pallas import tpu as pltpu
from jax.sharding import PartitionSpec as P

F32 = jnp.float32
BF16 = jnp.bfloat16
HIGHEST = lax.Precision.HIGHEST
NT = (((1,), (1,)), ((), ()))
AXES = ("grp", "dp", "query", "proj")
MIB = 2**20
CHUNK = 256
QUERY_STEP = 1


def swap(value, mesh, mask):
    count = math.prod(mesh.shape[axis] for axis in AXES)
    return lax.ppermute(value, AXES, [(i, i ^ mask) for i in range(count)])


def bits_of(size):
    return [1 << b for b in range(size.bit_length() - 1)]


def pick_kernel(groups, queries_hbm, half_ref, piece_ref, sems):
    half, piece = half_ref.shape[0], piece_ref.shape[0]
    core = 1 - lax.axis_index("proj")
    index = core * groups + lax.axis_index("grp")
    copies = [
        pltpu.make_async_copy(queries_hbm.at[0, pl.ds(pl.multiple_of(core * half, 8), half)], half_ref, sems.at[0]),
        pltpu.make_async_copy(queries_hbm.at[0, pl.ds(pl.multiple_of(index * piece, 8), piece)], piece_ref, sems.at[1]),
    ]
    for copy in copies:
        copy.start()
    for copy in copies:
        copy.wait()


def pick_queries(queries, groups):
    rows, columns = queries.shape[1:]
    return pl.pallas_call(
        functools.partial(pick_kernel, groups),
        out_shape=tuple(jax.ShapeDtypeStruct((rows // n, columns), F32) for n in (2, 2 * groups)),
        in_specs=[pl.BlockSpec(memory_space=pl.ANY)],
        out_specs=(pl.BlockSpec(memory_space=pltpu.VMEM),) * 2,
        scratch_shapes=[pltpu.SemaphoreType.DMA((2,))],
        compiler_params=pltpu.CompilerParams(vmem_limit_bytes=4 * MIB),
        cost_estimate=pl.CostEstimate(flops=4 * 10**9, bytes_accessed=10**6, transcendentals=0),
        name="pick_queries",
    )(pltpu.with_memory_space_constraint(queries, pltpu.HBM))


def project_kernel(a_ref, g_ref, p_in_ref, p_out_ref, after_ref, out_ref):
    width = p_in_ref.shape[0]
    out_ref[0:width, :] = lax.dot_general(a_ref[...], p_in_ref[...], NT, preferred_element_type=F32).T
    out_ref[width : 2 * width, :] = lax.dot_general(g_ref[...], p_out_ref[...], NT, preferred_element_type=F32).T


def project(activations, out_grads, proj_in, proj_out, after):
    return pl.pallas_call(
        project_kernel,
        out_shape=jax.ShapeDtypeStruct((2 * proj_in.shape[1], activations.shape[0]), F32),
        in_specs=[pl.BlockSpec(memory_space=pltpu.VMEM)] * 4 + [pl.BlockSpec(memory_space=pl.ANY)],
        out_specs=pl.BlockSpec(memory_space=pltpu.VMEM),
        compiler_params=pltpu.CompilerParams(vmem_limit_bytes=16 * MIB),
        name="project",
    )(activations, out_grads, proj_in.T, proj_out.T, after)


def masks_kernel(lengths_ref, after_ref, member_ref, live_ref, count_ref):
    examples, slots = member_ref.shape
    index = lax.broadcasted_iota(jnp.int32, (examples, 1), 0)
    starts = jnp.zeros((examples, 1), jnp.int32)
    counts = jnp.zeros((examples, 1), jnp.int32)
    begin = jnp.int32(0)
    for e in range(examples):
        length = lengths_ref[0, e]
        starts = jnp.where(index == e, begin, starts)
        counts = jnp.where(index == e, length, counts)
        begin = begin + length
    slot = lax.broadcasted_iota(jnp.int32, (examples, slots), 1)
    member_ref[...] = jnp.where((slot >= starts) & (slot < starts + counts), 1.0, 0.0).astype(BF16)
    live_ref[...] = jnp.where(slot[0:8] < begin, 1.0, 0.0)
    count_ref[...] = jnp.broadcast_to(counts.astype(F32), count_ref.shape)


def masks(lengths, after):
    examples, slots = lengths.shape[1] - 1, after.shape[1]
    return pl.pallas_call(
        masks_kernel,
        out_shape=(
            jax.ShapeDtypeStruct((examples, slots), BF16),
            jax.ShapeDtypeStruct((8, slots), F32),
            jax.ShapeDtypeStruct((examples, 128), F32),
        ),
        in_specs=[pl.BlockSpec(memory_space=pltpu.SMEM), pl.BlockSpec(memory_space=pl.ANY)],
        out_specs=(pl.BlockSpec(memory_space=pltpu.VMEM),) * 3,
        compiler_params=pltpu.CompilerParams(vmem_limit_bytes=4 * MIB),
        cost_estimate=pl.CostEstimate(flops=2 * 10**9, bytes_accessed=10**6, transcendentals=0),
        name="masks",
    )(lengths, after)


def fisher_kernel(live_ref, own_ref, other_ref, out_ref):
    width = out_ref.shape[0]
    both = own_ref[...] + other_ref[...]
    gram = lax.dot_general(both * live_ref[0:1, :], both, NT, precision=HIGHEST, preferred_element_type=F32)
    out_ref[...] = jnp.zeros_like(out_ref)
    out_ref[:, 0:width] = gram[0:width, 0:width]
    out_ref[:, width : 2 * width] = gram[width : 2 * width, width : 2 * width]


def fisher(live, own, other):
    width = own.shape[0] // 2
    return pl.pallas_call(
        fisher_kernel,
        out_shape=jax.ShapeDtypeStruct((width, 128), F32),
        in_specs=[pl.BlockSpec(memory_space=pltpu.VMEM)] * 3,
        out_specs=pl.BlockSpec(memory_space=pltpu.VMEM),
        compiler_params=pltpu.CompilerParams(vmem_limit_bytes=8 * MIB),
        name="fisher",
    )(live, own, other)


def split3(value):
    high = value.astype(BF16)
    rest = value - high.astype(F32)
    middle = rest.astype(BF16)
    return high, middle, (rest - middle.astype(F32)).astype(BF16)


def examples_kernel(member_ref, count_ref, own_ref, other_ref, out_ref):
    width = own_ref.shape[0] // 2
    both = own_ref[...] + other_ref[...]
    inputs, outputs = both[0:width], both[width : 2 * width]
    member, divisor = member_ref[...], count_ref[:, 0:1]
    group = 8
    for first in range(0, width, group):
        outer = jnp.concatenate([outputs[i : i + 1] * inputs for i in range(first, first + group)], axis=0)
        total = None
        for piece in reversed(split3(outer)):
            part = lax.dot_general(member, piece, NT, preferred_element_type=F32)
            total = part if total is None else total + part
        out_ref[:, first * width : (first + group) * width] = total / divisor


def example_grads(member, count, own, other):
    width = own.shape[0] // 2
    return pl.pallas_call(
        examples_kernel,
        out_shape=jax.ShapeDtypeStruct((member.shape[0], width * width), F32),
        in_specs=[pl.BlockSpec(memory_space=pltpu.VMEM)] * 4,
        out_specs=pl.BlockSpec(memory_space=pltpu.VMEM),
        compiler_params=pltpu.CompilerParams(vmem_limit_bytes=8 * MIB),
        cost_estimate=pl.CostEstimate(flops=2 * 10**9, bytes_accessed=10**6, transcendentals=0),
        name="examples",
    )(member, count, own, other)


def split2(value):
    high = value.astype(BF16)
    return high, (value - high.astype(F32)).astype(BF16)


def turn_pairs(load, scratch, width):
    columns, count = scratch.shape
    for c in range(columns // CHUNK):
        scratch[c * CHUNK : (c + 1) * CHUNK, :] = load(c).T
    chunks = []
    for c in range(columns // CHUNK):
        lines = range(c * CHUNK // width, (c + 1) * CHUNK // width)
        chunks.append(jnp.concatenate([scratch[pl.ds(j, width, stride=width), :] for j in lines], axis=0).T)
    return jnp.concatenate(chunks, axis=0)


def arrange_examples_kernel(n_query, blocks_ref, *refs):
    out_refs, (rows, scratch) = refs[:-2], refs[-2:]
    blocks, examples, columns = blocks_ref.shape
    query = lax.axis_index("query")
    for b in range(blocks):
        place = (b // n_query) * n_query + (query ^ (b % n_query))
        rows[pl.ds(pl.multiple_of(place * examples, 8), examples), :] = blocks_ref[b]
    width = math.isqrt(columns)
    turned = turn_pairs(lambda c: rows[:, c * CHUNK : (c + 1) * CHUNK], scratch, width)
    for out_ref, piece in zip(out_refs, split3(turned)):
        out_ref[...] = piece


def arrange_examples(blocks, n_query):
    number, examples, columns = blocks.shape
    count = number * examples
    shape = jax.ShapeDtypeStruct((count * columns // CHUNK, CHUNK), BF16)
    return pl.pallas_call(
        functools.partial(arrange_examples_kernel, n_query),
        out_shape=(shape,) * 3,
        in_specs=[pl.BlockSpec(memory_space=pltpu.VMEM)],
        out_specs=(pl.BlockSpec(memory_space=pltpu.VMEM),) * 3,
        scratch_shapes=[pltpu.VMEM((count, columns), F32), pltpu.VMEM((columns, count), F32)],
        compiler_params=pltpu.CompilerParams(vmem_limit_bytes=12 * MIB),
        name="arrange_examples",
    )(blocks)


def split_near_kernel(own_ref, near_ref, high_ref, low_ref):
    half = near_ref.shape[0]
    start = pl.multiple_of(lax.axis_index("proj") * half, 8)
    for i, value in enumerate((own_ref[0, pl.ds(start, half), :], near_ref[...])):
        at = slice(i * half, (i + 1) * half)
        high_ref[at, :], low_ref[at, :] = split2(value)


def split_near(own, near):
    half, columns = near.shape
    shape = jax.ShapeDtypeStruct((2 * half, columns), BF16)
    return pl.pallas_call(
        split_near_kernel,
        out_shape=(shape, shape),
        in_specs=[pl.BlockSpec(memory_space=pltpu.VMEM)] * 2,
        out_specs=(pl.BlockSpec(memory_space=pltpu.VMEM),) * 2,
        compiler_params=pltpu.CompilerParams(vmem_limit_bytes=6 * MIB),
        name="split_near",
    )(own, near)


def damped(fisher_sum):
    width = fisher_sum.shape[0]
    row = lax.broadcasted_iota(jnp.int32, (width, width), 0)
    column = lax.broadcasted_iota(jnp.int32, (width, width), 1)
    trace = jnp.sum(jnp.where(row == column, fisher_sum, 0.0), keepdims=True)
    return fisher_sum * (width / trace) + jnp.where(row == column, 1.0, 0.0)


def inverse_pair(pair):
    width, group = pair.shape[0], 8
    both = jnp.concatenate([damped(pair[:, 0:width]), damped(pair[:, width : 2 * width])], axis=1)
    state = jnp.concatenate([both] * (128 // (2 * width)), axis=1)
    state = [state[i : i + group] for i in range(0, width, group)]
    lane = lax.broadcasted_iota(jnp.int32, (group, 128), 1)
    own = lane % width
    first = lane - own
    sublane = lax.broadcasted_iota(jnp.int32, (group, 128), 0)

    def spread(value, index):
        return jnp.take_along_axis(value, index, axis=1, mode="promise_in_bounds")

    columns = [[spread(part, first + c) for c in range(4)] for part in state]
    for k in range(0, width, 4):
        at, offset = k // group, k % group
        more = k + 4 < width
        ahead = [[spread(part, first + (k + 4 + c)) for c in range(4)] for part in state] if more else None
        inside = (own >= k) & (own < k + 4)

        def row(value, r):
            return value[offset + r : offset + r + 1, :]

        p = [[row(columns[at][c], r) for c in range(4)] for r in range(4)]
        scale = 1.0 / (p[0][0] * p[1][1] - p[0][1] * p[1][0])
        a = ((p[1][1] * scale, -p[0][1] * scale), (-p[1][0] * scale, p[0][0] * scale))
        right = [[a[r][0] * p[0][c] + a[r][1] * p[1][c] for r in range(2)] for c in (2, 3)]
        s = [[p[r][c] - (p[r][0] * right[c - 2][0] + p[r][1] * right[c - 2][1]) for c in (2, 3)] for r in (2, 3)]
        scale = 1.0 / (s[0][0] * s[1][1] - s[0][1] * s[1][0])
        d = ((s[1][1] * scale, -s[0][1] * scale), (-s[1][0] * scale, s[0][0] * scale))

        def solve(q):
            upper = [a[r][0] * q[0] + a[r][1] * q[1] for r in range(2)]
            rest = [q[r] - (p[r][0] * upper[0] + p[r][1] * upper[1]) for r in (2, 3)]
            lower = [d[r][0] * rest[0] + d[r][1] * rest[1] for r in range(2)]
            return [upper[r] - (right[0][r] * lower[0] + right[1][r] * lower[1]) for r in range(2)] + lower

        def step(i, value, solved):
            c = columns[i]
            value = value - ((c[0] * solved[0] + c[1] * solved[1]) + (c[2] * solved[2] + c[3] * solved[3]))
            if i == at:
                for r in range(4):
                    value = jnp.where(sublane == offset + r, solved[r], value)
            return value

        rows = [jnp.where(own[0:1] == k + r, 1.0, jnp.where(inside[0:1], 0.0, row(state[at], r))) for r in range(4)]
        solved = solve(rows)
        following = columns
        if more:
            solved_ahead = [solve([row(ahead[at][c], r) for r in range(4)]) for c in range(4)]
            following = [[step(i, ahead[i][c], solved_ahead[c]) for c in range(4)] for i in range(len(state))]
        state = [step(i, jnp.where(inside, 0.0, part), solved) for i, part in enumerate(state)]
        columns = following
    return [jnp.concatenate([spread(part, own + start) for part in state], axis=0) for start in (0, width)]


def block_diagonal(tiled):
    width, lanes = tiled.shape
    value = jnp.concatenate([jnp.concatenate([tiled] * (CHUNK // lanes), axis=1)] * (CHUNK // width), axis=0)
    row = lax.broadcasted_iota(jnp.int32, (CHUNK, CHUNK), 0) // width
    column = lax.broadcasted_iota(jnp.int32, (CHUNK, CHUNK), 1) // width
    return jnp.where(row == column, value, 0.0)


def times_blocks(high, middle, low, blocks_ref):
    rows = high.shape[0]
    by_high = jnp.dot(jnp.concatenate([high, middle, low], axis=0), blocks_ref[0], preferred_element_type=F32)
    by_middle = jnp.dot(jnp.concatenate([high, middle], axis=0), blocks_ref[1], preferred_element_type=F32)
    by_low = jnp.dot(high, blocks_ref[2], preferred_element_type=F32)
    small = by_high[2 * rows :] + by_middle[rows:] + by_low
    return by_high[0:rows] + (by_high[rows : 2 * rows] + by_middle[0:rows] + small)


def times_queries(both_ref, high_ref, low_ref):
    chunks, count = both_ref.shape[0], both_ref.shape[1] // 2
    total = None
    for c in range(chunks):
        cols = slice(c * CHUNK, (c + 1) * CHUNK)
        by_high = lax.dot_general(both_ref[c], high_ref[:, cols], NT, preferred_element_type=F32)
        by_low = lax.dot_general(both_ref[c, 0:count], low_ref[:, cols], NT, preferred_element_type=F32)
        part = by_high[0:count] + (by_high[count:] + by_low)
        total = part if total is None else total + part
    return total * (1.0 / math.isqrt(chunks * CHUNK))


def condition_kernel(own_ref, other_ref, high_ref, middle_ref, low_ref, near_high_ref, near_low_ref, both_ref, near_ref, in_ref, out_ref, scratch):
    columns, count = scratch.shape
    width = own_ref.shape[0]
    total = own_ref[...] + other_ref[...]
    for ref, inverse in zip((in_ref, out_ref), inverse_pair(total[:, 0 : 2 * width])):
        for piece, value in enumerate(split3(block_diagonal(inverse))):
            ref[piece] = value
    left = times_blocks(high_ref[...], middle_ref[...], low_ref[...], out_ref)
    turned = turn_pairs(lambda c: left[c * count : (c + 1) * count], scratch, width)
    high, low = split2(times_blocks(*split3(turned), in_ref))
    for c in range(columns // CHUNK):
        both_ref[c, 0:count] = high[c * count : (c + 1) * count]
        both_ref[c, count:] = low[c * count : (c + 1) * count]
    near_ref[...] = times_queries(both_ref, near_high_ref, near_low_ref)


def condition(own, other, pieces, near):
    columns = near[0].shape[1]
    count = pieces[0].shape[0] * CHUNK // columns
    return pl.pallas_call(
        condition_kernel,
        out_shape=(
            jax.ShapeDtypeStruct((columns // CHUNK, 2 * count, CHUNK), BF16),
            jax.ShapeDtypeStruct((count, near[0].shape[0]), F32),
        ),
        in_specs=[pl.BlockSpec(memory_space=pltpu.VMEM)] * 7,
        out_specs=(pl.BlockSpec(memory_space=pltpu.VMEM),) * 2,
        scratch_shapes=[pltpu.VMEM((3, CHUNK, CHUNK), BF16)] * 2 + [pltpu.VMEM((columns, count), F32)],
        compiler_params=pltpu.CompilerParams(vmem_limit_bytes=12 * MIB),
        cost_estimate=pl.CostEstimate(flops=4 * 10**9, bytes_accessed=10**6, transcendentals=0),
        name="condition",
    )(own, other, *pieces, *near)


def score_kernel(groups, both_ref, near_ref, *refs):
    fetched_refs, (scores_ref, high_ref, low_ref) = refs[:-3], refs[-3:]
    near = near_ref.shape[1]
    half = fetched_refs[0].shape[0]
    piece = half // groups
    group = lax.axis_index("grp")
    for i, ref in enumerate(fetched_refs):
        for g in range(groups):
            at = pl.ds(pl.multiple_of(i * half + (group ^ g) * piece, 16), piece)
            high_ref[at, :], low_ref[at, :] = split2(ref[g * piece : (g + 1) * piece, :])
    scores_ref[:, 0:near] = near_ref[...]
    scores_ref[:, near:] = times_queries(both_ref, high_ref, low_ref)


def score(groups, both, near, fetched):
    rows, columns = len(fetched) * fetched[0].shape[0], fetched[0].shape[1]
    return pl.pallas_call(
        functools.partial(score_kernel, groups),
        out_shape=jax.ShapeDtypeStruct((near.shape[0], near.shape[1] + rows), F32),
        in_specs=[pl.BlockSpec(memory_space=pltpu.VMEM)] * (2 + len(fetched)),
        out_specs=pl.BlockSpec(memory_space=pltpu.VMEM),
        scratch_shapes=[pltpu.VMEM((rows, columns), BF16)] * 2,
        compiler_params=pltpu.CompilerParams(vmem_limit_bytes=(8 + len(fetched)) * MIB),
        name="score",
    )(both, near, *fetched)


def place_kernel(half, kept_ref, received_ref, out_ref):
    core = lax.axis_index("proj")
    kept, received = kept_ref[...], received_ref[...]
    first = jnp.where(core == 0, kept, received)
    second = jnp.where(core == 0, received, kept)
    for r in range(kept.shape[1] // half):
        at = slice(r * half, (r + 1) * half)
        start = pl.multiple_of((lax.axis_index("dp") ^ r) * 2 * half, 128)
        out_ref[:, pl.ds(start, 2 * half)] = jnp.concatenate([first[:, at], second[:, at]], axis=1)


def place(half, kept, received):
    rows, columns = kept.shape
    return pl.pallas_call(
        functools.partial(place_kernel, half),
        out_shape=jax.ShapeDtypeStruct((rows, 2 * columns), F32),
        in_specs=[pl.BlockSpec(memory_space=pltpu.VMEM)] * 2,
        out_specs=pl.BlockSpec(memory_space=pltpu.VMEM),
        compiler_params=pltpu.CompilerParams(vmem_limit_bytes=8 * MIB),
        name="place",
    )(kept, received)


def hold_kernel(value_ref, after_ref, out_ref):
    out_ref[...] = value_ref[...]


def hold(value, after):
    return pl.pallas_call(
        hold_kernel,
        out_shape=jax.ShapeDtypeStruct(value.shape, value.dtype),
        in_specs=[pl.BlockSpec(memory_space=pltpu.VMEM), pl.BlockSpec(memory_space=pl.ANY)],
        out_specs=pl.BlockSpec(memory_space=pltpu.VMEM),
        compiler_params=pltpu.CompilerParams(vmem_limit_bytes=4 * MIB),
        cost_estimate=pl.CostEstimate(flops=10**9, bytes_accessed=10**6, transcendentals=0),
        name="hold",
    )(value, after)


ORDER = "x21"
E_STAGE = 0
Y_STAGES = (1,)


def body(mesh, activations, out_grads, proj_in, proj_out, lengths, queries):
    groups, n_dp, n_query = mesh.shape["grp"], mesh.shape["dp"], mesh.shape["query"]
    core_bit = 1
    unit = 2 * n_query
    query_bits = [2 * b for b in bits_of(n_query)]
    dp_bits = [b * unit for b in bits_of(n_dp)]
    group_bits = [b * unit * n_dp for b in bits_of(groups)]

    half, piece = pick_queries(queries, groups)
    fetched = [swap(half if r == 1 else piece, mesh, r * unit | core_bit) for r in range(1, n_dp)]

    own = project(activations, out_grads, proj_in, proj_out, half)
    member, live, count = masks(lengths, own)
    other = swap(own, mesh, core_bit)
    own, other, live = lax.optimization_barrier((own, other, live))

    factor = fisher(live, own, other)
    factor, own, other = lax.optimization_barrier((factor, own, other))
    blocks = example_grads(member, count, own, other)[None]
    groups_of = {"x": query_bits, "1": dp_bits[:1], "2": dp_bits[1:]}
    steps = [bit | core_bit for name in ORDER for bit in groups_of[name]]

    def beside(stage, factor, blocks, fetched):
        i = stage - E_STAGE
        if 0 <= i < len(query_bits):
            blocks = hold(blocks, factor)
            blocks = jnp.concatenate([blocks, swap(blocks, mesh, query_bits[i] | core_bit)], axis=0)
        if stage in Y_STAGES:
            first, end = (1, n_dp - 1)
            for r in range(first, end):
                fetched[r] = hold(fetched[r], factor)
                for bit in group_bits:
                    fetched[r] = jnp.concatenate([fetched[r], swap(fetched[r], mesh, bit)], axis=0)
        return blocks

    for step, mask in enumerate(steps):
        blocks = beside(step, factor, blocks, fetched)
        received = swap(factor, mesh, mask)
        if step < len(steps) - 1:
            factor = factor + received
    arranged = arrange_examples(blocks, n_query)
    near = split_near(queries, fetched[0])
    arranged, near, received = lax.optimization_barrier((arranged, near, received))
    both, near = condition(factor, received, arranged, near)

    scores = score(groups, both, near, fetched[1:])
    return place(queries.shape[1] // 2, scores, swap(scores, mesh, core_bit))


def solution(mesh):
    in_specs = (
        P(("grp", "dp", "query"), "proj"),
        P(("grp", "dp", "query"), "proj"),
        P("proj", None),
        P("proj", None),
        P(("grp", "dp", "query"), None),
        P("query", "dp", None),
    )
    out_specs = P(("grp", "dp"), "query")
    return jax.shard_map(
        functools.partial(body, mesh), mesh=mesh, in_specs=in_specs, out_specs=out_specs, check_vma=False
    )
```

```python
import functools
import math

import jax
import jax.numpy as jnp
from jax import lax
from jax.experimental import pallas as pl
from jax.experimental.pallas import tpu as pltpu
from jax.sharding import PartitionSpec as P

F32 = jnp.float32
BF16 = jnp.bfloat16
HIGHEST = lax.Precision.HIGHEST
NT = (((1,), (1,)), ((), ()))
AXES = ("grp", "dp", "query", "proj")
MIB = 2**20
CHUNK = 256
QUERY_STEP = 1


def swap(value, mesh, mask):
    count = math.prod(mesh.shape[axis] for axis in AXES)
    return lax.ppermute(value, AXES, [(i, i ^ mask) for i in range(count)])


def bits_of(size):
    return [1 << b for b in range(size.bit_length() - 1)]


def pick_kernel(groups, queries_hbm, half_ref, piece_ref, sems):
    half, piece = half_ref.shape[0], piece_ref.shape[0]
    core = 1 - lax.axis_index("proj")
    index = core * groups + lax.axis_index("grp")
    copies = [
        pltpu.make_async_copy(queries_hbm.at[0, pl.ds(pl.multiple_of(core * half, 8), half)], half_ref, sems.at[0]),
        pltpu.make_async_copy(queries_hbm.at[0, pl.ds(pl.multiple_of(index * piece, 8), piece)], piece_ref, sems.at[1]),
    ]
    for copy in copies:
        copy.start()
    for copy in copies:
        copy.wait()


def pick_queries(queries, groups):
    rows, columns = queries.shape[1:]
    return pl.pallas_call(
        functools.partial(pick_kernel, groups),
        out_shape=tuple(jax.ShapeDtypeStruct((rows // n, columns), F32) for n in (2, 2 * groups)),
        in_specs=[pl.BlockSpec(memory_space=pl.ANY)],
        out_specs=(pl.BlockSpec(memory_space=pltpu.VMEM),) * 2,
        scratch_shapes=[pltpu.SemaphoreType.DMA((2,))],
        compiler_params=pltpu.CompilerParams(vmem_limit_bytes=4 * MIB),
        cost_estimate=pl.CostEstimate(flops=4 * 10**9, bytes_accessed=10**6, transcendentals=0),
        name="pick_queries",
    )(pltpu.with_memory_space_constraint(queries, pltpu.HBM))


def project_kernel(a_ref, g_ref, p_in_ref, p_out_ref, after_ref, out_ref):
    width = p_in_ref.shape[0]
    out_ref[0:width, :] = lax.dot_general(a_ref[...], p_in_ref[...], NT, preferred_element_type=F32).T
    out_ref[width : 2 * width, :] = lax.dot_general(g_ref[...], p_out_ref[...], NT, preferred_element_type=F32).T


def project(activations, out_grads, proj_in, proj_out, after):
    return pl.pallas_call(
        project_kernel,
        out_shape=jax.ShapeDtypeStruct((2 * proj_in.shape[1], activations.shape[0]), F32),
        in_specs=[pl.BlockSpec(memory_space=pltpu.VMEM)] * 4 + [pl.BlockSpec(memory_space=pl.ANY)],
        out_specs=pl.BlockSpec(memory_space=pltpu.VMEM),
        compiler_params=pltpu.CompilerParams(vmem_limit_bytes=16 * MIB),
        name="project",
    )(activations, out_grads, proj_in.T, proj_out.T, after)


def masks_kernel(lengths_ref, after_ref, member_ref, live_ref, count_ref):
    examples, slots = member_ref.shape
    length = jnp.broadcast_to(lengths_ref[...].astype(F32), (examples, lengths_ref.shape[1]))
    example = lax.broadcasted_iota(jnp.int32, length.shape, 0)
    entry = lax.broadcasted_iota(jnp.int32, length.shape, 1)
    begin = jnp.sum(jnp.where(entry < example, length, 0.0), axis=1, keepdims=True)
    end = jnp.sum(jnp.where(entry <= example, length, 0.0), axis=1, keepdims=True)
    slot = lax.broadcasted_iota(jnp.int32, (examples, slots), 1).astype(F32)
    member_ref[...] = jnp.where((slot >= begin) & (slot < end), 1.0, 0.0).astype(BF16)
    live_ref[...] = jnp.where(slot[0:8] < end[examples - 1 : examples], 1.0, 0.0)
    count_ref[...] = jnp.broadcast_to(end - begin, count_ref.shape)


def masks(lengths, after):
    examples, slots = lengths.shape[1] - 1, after.shape[1]
    return pl.pallas_call(
        masks_kernel,
        out_shape=(
            jax.ShapeDtypeStruct((examples, slots), BF16),
            jax.ShapeDtypeStruct((8, slots), F32),
            jax.ShapeDtypeStruct((examples, 128), F32),
        ),
        in_specs=[pl.BlockSpec(memory_space=pltpu.VMEM), pl.BlockSpec(memory_space=pl.ANY)],
        out_specs=(pl.BlockSpec(memory_space=pltpu.VMEM),) * 3,
        compiler_params=pltpu.CompilerParams(vmem_limit_bytes=4 * MIB),
        cost_estimate=pl.CostEstimate(flops=2 * 10**9, bytes_accessed=10**6, transcendentals=0),
        name="masks",
    )(lengths, after)


def fisher_kernel(live_ref, own_ref, other_ref, out_ref):
    width = out_ref.shape[0]
    both = own_ref[...] + other_ref[...]
    gram = lax.dot_general(both * live_ref[0:1, :], both, NT, precision=HIGHEST, preferred_element_type=F32)
    out_ref[...] = jnp.zeros_like(out_ref)
    out_ref[:, 0:width] = gram[0:width, 0:width]
    out_ref[:, width : 2 * width] = gram[width : 2 * width, width : 2 * width]


def fisher(live, own, other):
    width = own.shape[0] // 2
    return pl.pallas_call(
        fisher_kernel,
        out_shape=jax.ShapeDtypeStruct((width, 128), F32),
        in_specs=[pl.BlockSpec(memory_space=pltpu.VMEM)] * 3,
        out_specs=pl.BlockSpec(memory_space=pltpu.VMEM),
        compiler_params=pltpu.CompilerParams(vmem_limit_bytes=8 * MIB),
        name="fisher",
    )(live, own, other)


def split3(value):
    high = value.astype(BF16)
    rest = value - high.astype(F32)
    middle = rest.astype(BF16)
    return high, middle, (rest - middle.astype(F32)).astype(BF16)


def examples_kernel(member_ref, count_ref, own_ref, other_ref, out_ref):
    width = own_ref.shape[0] // 2
    both = own_ref[...] + other_ref[...]
    inputs, outputs = both[0:width], both[width : 2 * width]
    member, divisor = member_ref[...], count_ref[:, 0:1]
    group = 8
    for first in range(0, width, group):
        outer = jnp.concatenate([outputs[i : i + 1] * inputs for i in range(first, first + group)], axis=0)
        total = None
        for piece in reversed(split3(outer)):
            part = lax.dot_general(member, piece, NT, preferred_element_type=F32)
            total = part if total is None else total + part
        out_ref[:, first * width : (first + group) * width] = total / divisor


def example_grads(member, count, own, other):
    width = own.shape[0] // 2
    return pl.pallas_call(
        examples_kernel,
        out_shape=jax.ShapeDtypeStruct((member.shape[0], width * width), F32),
        in_specs=[pl.BlockSpec(memory_space=pltpu.VMEM)] * 4,
        out_specs=pl.BlockSpec(memory_space=pltpu.VMEM),
        compiler_params=pltpu.CompilerParams(vmem_limit_bytes=8 * MIB),
        cost_estimate=pl.CostEstimate(flops=2 * 10**9, bytes_accessed=10**6, transcendentals=0),
        name="examples",
    )(member, count, own, other)


def split2(value):
    high = value.astype(BF16)
    return high, (value - high.astype(F32)).astype(BF16)


def turn_pairs(load, scratch, width):
    columns, count = scratch.shape
    for c in range(columns // CHUNK):
        scratch[c * CHUNK : (c + 1) * CHUNK, :] = load(c).T
    chunks = []
    for c in range(columns // CHUNK):
        lines = range(c * CHUNK // width, (c + 1) * CHUNK // width)
        chunks.append(jnp.concatenate([scratch[pl.ds(j, width, stride=width), :] for j in lines], axis=0).T)
    return jnp.concatenate(chunks, axis=0)


def arrange_examples_kernel(n_query, blocks_ref, *refs):
    out_refs, (rows, scratch) = refs[:-2], refs[-2:]
    blocks, examples, columns = blocks_ref.shape
    query = lax.axis_index("query")
    for b in range(blocks):
        place = (b // n_query) * n_query + (query ^ (b % n_query))
        rows[pl.ds(pl.multiple_of(place * examples, 8), examples), :] = blocks_ref[b]
    width = math.isqrt(columns)
    turned = turn_pairs(lambda c: rows[:, c * CHUNK : (c + 1) * CHUNK], scratch, width)
    for out_ref, piece in zip(out_refs, split3(turned)):
        out_ref[...] = piece


def arrange_examples(blocks, n_query):
    number, examples, columns = blocks.shape
    count = number * examples
    shape = jax.ShapeDtypeStruct((count * columns // CHUNK, CHUNK), BF16)
    return pl.pallas_call(
        functools.partial(arrange_examples_kernel, n_query),
        out_shape=(shape,) * 3,
        in_specs=[pl.BlockSpec(memory_space=pltpu.VMEM)],
        out_specs=(pl.BlockSpec(memory_space=pltpu.VMEM),) * 3,
        scratch_shapes=[pltpu.VMEM((count, columns), F32), pltpu.VMEM((columns, count), F32)],
        compiler_params=pltpu.CompilerParams(vmem_limit_bytes=12 * MIB),
        name="arrange_examples",
    )(blocks)


def split_near_kernel(own_ref, near_ref, high_ref, low_ref):
    half = near_ref.shape[0]
    start = pl.multiple_of(lax.axis_index("proj") * half, 8)
    for i, value in enumerate((own_ref[0, pl.ds(start, half), :], near_ref[...])):
        at = slice(i * half, (i + 1) * half)
        high_ref[at, :], low_ref[at, :] = split2(value)


def split_near(own, near):
    half, columns = near.shape
    shape = jax.ShapeDtypeStruct((2 * half, columns), BF16)
    return pl.pallas_call(
        split_near_kernel,
        out_shape=(shape, shape),
        in_specs=[pl.BlockSpec(memory_space=pltpu.VMEM)] * 2,
        out_specs=(pl.BlockSpec(memory_space=pltpu.VMEM),) * 2,
        compiler_params=pltpu.CompilerParams(vmem_limit_bytes=6 * MIB),
        name="split_near",
    )(own, near)


def damped(fisher_sum):
    width = fisher_sum.shape[0]
    row = lax.broadcasted_iota(jnp.int32, (width, width), 0)
    column = lax.broadcasted_iota(jnp.int32, (width, width), 1)
    trace = jnp.sum(jnp.where(row == column, fisher_sum, 0.0), keepdims=True)
    return fisher_sum * (width / trace) + jnp.where(row == column, 1.0, 0.0)


def inverse_pair(pair):
    width, group = pair.shape[0], 8
    both = jnp.concatenate([damped(pair[:, 0:width]), damped(pair[:, width : 2 * width])], axis=1)
    state = jnp.concatenate([both] * (128 // (2 * width)), axis=1)
    state = [state[i : i + group] for i in range(0, width, group)]
    lane = lax.broadcasted_iota(jnp.int32, (group, 128), 1)
    own = lane % width
    first = lane - own
    sublane = lax.broadcasted_iota(jnp.int32, (group, 128), 0)

    def spread(value, index):
        return jnp.take_along_axis(value, index, axis=1, mode="promise_in_bounds")

    columns = [[spread(part, first + c) for c in range(4)] for part in state]
    for k in range(0, width, 4):
        at, offset = k // group, k % group
        more = k + 4 < width
        ahead = [[spread(part, first + (k + 4 + c)) for c in range(4)] for part in state] if more else None
        inside = (own >= k) & (own < k + 4)

        def row(value, r):
            return value[offset + r : offset + r + 1, :]

        p = [[row(columns[at][c], r) for c in range(4)] for r in range(4)]
        scale = 1.0 / (p[0][0] * p[1][1] - p[0][1] * p[1][0])
        a = ((p[1][1] * scale, -p[0][1] * scale), (-p[1][0] * scale, p[0][0] * scale))
        right = [[a[r][0] * p[0][c] + a[r][1] * p[1][c] for r in range(2)] for c in (2, 3)]
        s = [[p[r][c] - (p[r][0] * right[c - 2][0] + p[r][1] * right[c - 2][1]) for c in (2, 3)] for r in (2, 3)]
        scale = 1.0 / (s[0][0] * s[1][1] - s[0][1] * s[1][0])
        d = ((s[1][1] * scale, -s[0][1] * scale), (-s[1][0] * scale, s[0][0] * scale))

        def solve(q):
            upper = [a[r][0] * q[0] + a[r][1] * q[1] for r in range(2)]
            rest = [q[r] - (p[r][0] * upper[0] + p[r][1] * upper[1]) for r in (2, 3)]
            lower = [d[r][0] * rest[0] + d[r][1] * rest[1] for r in range(2)]
            return [upper[r] - (right[0][r] * lower[0] + right[1][r] * lower[1]) for r in range(2)] + lower

        def step(i, value, solved):
            c = columns[i]
            value = value - ((c[0] * solved[0] + c[1] * solved[1]) + (c[2] * solved[2] + c[3] * solved[3]))
            if i == at:
                for r in range(4):
                    value = jnp.where(sublane == offset + r, solved[r], value)
            return value

        rows = [jnp.where(own[0:1] == k + r, 1.0, jnp.where(inside[0:1], 0.0, row(state[at], r))) for r in range(4)]
        solved = solve(rows)
        following = columns
        if more:
            solved_ahead = [solve([row(ahead[at][c], r) for r in range(4)]) for c in range(4)]
            following = [[step(i, ahead[i][c], solved_ahead[c]) for c in range(4)] for i in range(len(state))]
        state = [step(i, jnp.where(inside, 0.0, part), solved) for i, part in enumerate(state)]
        columns = following
    return [jnp.concatenate([spread(part, own + start) for part in state], axis=0) for start in (0, width)]


def block_diagonal(tiled):
    width, lanes = tiled.shape
    value = jnp.concatenate([jnp.concatenate([tiled] * (CHUNK // lanes), axis=1)] * (CHUNK // width), axis=0)
    row = lax.broadcasted_iota(jnp.int32, (CHUNK, CHUNK), 0) // width
    column = lax.broadcasted_iota(jnp.int32, (CHUNK, CHUNK), 1) // width
    return jnp.where(row == column, value, 0.0)


def times_blocks(high, middle, low, blocks_ref):
    rows = high.shape[0]
    by_high = jnp.dot(jnp.concatenate([high, middle, low], axis=0), blocks_ref[0], preferred_element_type=F32)
    by_middle = jnp.dot(jnp.concatenate([high, middle], axis=0), blocks_ref[1], preferred_element_type=F32)
    by_low = jnp.dot(high, blocks_ref[2], preferred_element_type=F32)
    small = by_high[2 * rows :] + by_middle[rows:] + by_low
    return by_high[0:rows] + (by_high[rows : 2 * rows] + by_middle[0:rows] + small)


def times_queries(both_ref, high_ref, low_ref):
    chunks, count = both_ref.shape[0], both_ref.shape[1] // 2
    total = None
    for c in range(chunks):
        cols = slice(c * CHUNK, (c + 1) * CHUNK)
        by_high = lax.dot_general(both_ref[c], high_ref[:, cols], NT, preferred_element_type=F32)
        by_low = lax.dot_general(both_ref[c, 0:count], low_ref[:, cols], NT, preferred_element_type=F32)
        part = by_high[0:count] + (by_high[count:] + by_low)
        total = part if total is None else total + part
    return total * (1.0 / math.isqrt(chunks * CHUNK))


def condition_kernel(own_ref, other_ref, high_ref, middle_ref, low_ref, near_high_ref, near_low_ref, both_ref, near_ref, in_ref, out_ref, scratch):
    columns, count = scratch.shape
    width = own_ref.shape[0]
    total = own_ref[...] + other_ref[...]
    for ref, inverse in zip((in_ref, out_ref), inverse_pair(total[:, 0 : 2 * width])):
        for piece, value in enumerate(split3(block_diagonal(inverse))):
            ref[piece] = value
    left = times_blocks(high_ref[...], middle_ref[...], low_ref[...], out_ref)
    turned = turn_pairs(lambda c: left[c * count : (c + 1) * count], scratch, width)
    high, low = split2(times_blocks(*split3(turned), in_ref))
    for c in range(columns // CHUNK):
        both_ref[c, 0:count] = high[c * count : (c + 1) * count]
        both_ref[c, count:] = low[c * count : (c + 1) * count]
    near_ref[...] = times_queries(both_ref, near_high_ref, near_low_ref)


def condition(own, other, pieces, near):
    columns = near[0].shape[1]
    count = pieces[0].shape[0] * CHUNK // columns
    return pl.pallas_call(
        condition_kernel,
        out_shape=(
            jax.ShapeDtypeStruct((columns // CHUNK, 2 * count, CHUNK), BF16),
            jax.ShapeDtypeStruct((count, near[0].shape[0]), F32),
        ),
        in_specs=[pl.BlockSpec(memory_space=pltpu.VMEM)] * 7,
        out_specs=(pl.BlockSpec(memory_space=pltpu.VMEM),) * 2,
        scratch_shapes=[pltpu.VMEM((3, CHUNK, CHUNK), BF16)] * 2 + [pltpu.VMEM((columns, count), F32)],
        compiler_params=pltpu.CompilerParams(vmem_limit_bytes=12 * MIB),
        cost_estimate=pl.CostEstimate(flops=4 * 10**9, bytes_accessed=10**6, transcendentals=0),
        name="condition",
    )(own, other, *pieces, *near)


def score_kernel(groups, both_ref, near_ref, *refs):
    fetched_refs, (scores_ref, high_ref, low_ref) = refs[:-3], refs[-3:]
    near = near_ref.shape[1]
    half = fetched_refs[0].shape[0]
    piece = half // groups
    group = lax.axis_index("grp")
    for i, ref in enumerate(fetched_refs):
        for g in range(groups):
            at = pl.ds(pl.multiple_of(i * half + (group ^ g) * piece, 16), piece)
            high_ref[at, :], low_ref[at, :] = split2(ref[g * piece : (g + 1) * piece, :])
    scores_ref[:, 0:near] = near_ref[...]
    scores_ref[:, near:] = times_queries(both_ref, high_ref, low_ref)


def score(groups, both, near, fetched):
    rows, columns = len(fetched) * fetched[0].shape[0], fetched[0].shape[1]
    return pl.pallas_call(
        functools.partial(score_kernel, groups),
        out_shape=jax.ShapeDtypeStruct((near.shape[0], near.shape[1] + rows), F32),
        in_specs=[pl.BlockSpec(memory_space=pltpu.VMEM)] * (2 + len(fetched)),
        out_specs=pl.BlockSpec(memory_space=pltpu.VMEM),
        scratch_shapes=[pltpu.VMEM((rows, columns), BF16)] * 2,
        compiler_params=pltpu.CompilerParams(vmem_limit_bytes=(8 + len(fetched)) * MIB),
        name="score",
    )(both, near, *fetched)


def place_kernel(half, kept_ref, received_ref, out_ref):
    core = lax.axis_index("proj")
    kept, received = kept_ref[...], received_ref[...]
    first = jnp.where(core == 0, kept, received)
    second = jnp.where(core == 0, received, kept)
    for r in range(kept.shape[1] // half):
        at = slice(r * half, (r + 1) * half)
        start = pl.multiple_of((lax.axis_index("dp") ^ r) * 2 * half, 128)
        out_ref[:, pl.ds(start, 2 * half)] = jnp.concatenate([first[:, at], second[:, at]], axis=1)


def place(half, kept, received):
    rows, columns = kept.shape
    return pl.pallas_call(
        functools.partial(place_kernel, half),
        out_shape=jax.ShapeDtypeStruct((rows, 2 * columns), F32),
        in_specs=[pl.BlockSpec(memory_space=pltpu.VMEM)] * 2,
        out_specs=pl.BlockSpec(memory_space=pltpu.VMEM),
        compiler_params=pltpu.CompilerParams(vmem_limit_bytes=8 * MIB),
        name="place",
    )(kept, received)


def hold_kernel(value_ref, after_ref, out_ref):
    out_ref[...] = value_ref[...]


def hold(value, after):
    return pl.pallas_call(
        hold_kernel,
        out_shape=jax.ShapeDtypeStruct(value.shape, value.dtype),
        in_specs=[pl.BlockSpec(memory_space=pltpu.VMEM), pl.BlockSpec(memory_space=pl.ANY)],
        out_specs=pl.BlockSpec(memory_space=pltpu.VMEM),
        compiler_params=pltpu.CompilerParams(vmem_limit_bytes=4 * MIB),
        cost_estimate=pl.CostEstimate(flops=10**9, bytes_accessed=10**6, transcendentals=0),
        name="hold",
    )(value, after)


ORDER = "x21"
E_STAGE = 0
Y_STAGES = (1,)


def body(mesh, activations, out_grads, proj_in, proj_out, lengths, queries):
    groups, n_dp, n_query = mesh.shape["grp"], mesh.shape["dp"], mesh.shape["query"]
    core_bit = 1
    unit = 2 * n_query
    query_bits = [2 * b for b in bits_of(n_query)]
    dp_bits = [b * unit for b in bits_of(n_dp)]
    group_bits = [b * unit * n_dp for b in bits_of(groups)]

    half, piece = pick_queries(queries, groups)
    fetched = [swap(piece, mesh, r * unit | core_bit) for r in range(2, n_dp)]

    own = project(activations, out_grads, proj_in, proj_out, half)
    half, own = lax.optimization_barrier((half, own))
    fetched = [swap(half, mesh, unit | core_bit)] + fetched
    member, live, count = masks(lengths, own)
    other = swap(own, mesh, core_bit)
    own, other, live = lax.optimization_barrier((own, other, live))

    factor = fisher(live, own, other)
    factor, own, other = lax.optimization_barrier((factor, own, other))
    blocks = example_grads(member, count, own, other)[None]
    groups_of = {"x": query_bits, "1": dp_bits[:1], "2": dp_bits[1:]}
    steps = [bit | core_bit for name in ORDER for bit in groups_of[name]]

    def beside(stage, factor, blocks, fetched):
        i = stage - E_STAGE
        if 0 <= i < len(query_bits):
            blocks = hold(blocks, factor)
            blocks = jnp.concatenate([blocks, swap(blocks, mesh, query_bits[i] | core_bit)], axis=0)
        if stage in Y_STAGES:
            first, end = (1, n_dp - 1)
            for r in range(first, end):
                fetched[r] = hold(fetched[r], factor)
                for bit in group_bits:
                    fetched[r] = jnp.concatenate([fetched[r], swap(fetched[r], mesh, bit)], axis=0)
        return blocks

    for step, mask in enumerate(steps):
        blocks = beside(step, factor, blocks, fetched)
        received = swap(factor, mesh, mask)
        if step < len(steps) - 1:
            factor = factor + received
    arranged = arrange_examples(blocks, n_query)
    near = split_near(queries, fetched[0])
    arranged, near, received = lax.optimization_barrier((arranged, near, received))
    both, near = condition(factor, received, arranged, near)

    scores = score(groups, both, near, fetched[1:])
    return place(queries.shape[1] // 2, scores, swap(scores, mesh, core_bit))


def solution(mesh):
    in_specs = (
        P(("grp", "dp", "query"), "proj"),
        P(("grp", "dp", "query"), "proj"),
        P("proj", None),
        P("proj", None),
        P(("grp", "dp", "query"), None),
        P("query", "dp", None),
    )
    out_specs = P(("grp", "dp"), "query")
    return jax.shard_map(
        functools.partial(body, mesh), mesh=mesh, in_specs=in_specs, out_specs=out_specs, check_vma=False
    )
```

```python
import functools
import math

import jax
import jax.numpy as jnp
from jax import lax
from jax.experimental import pallas as pl
from jax.experimental.pallas import tpu as pltpu
from jax.sharding import PartitionSpec as P

F32 = jnp.float32
BF16 = jnp.bfloat16
HIGHEST = lax.Precision.HIGHEST
NT = (((1,), (1,)), ((), ()))
AXES = ("grp", "dp", "query", "proj")
MIB = 2**20
CHUNK = 256
QUERY_STEP = 1


def swap(value, mesh, mask):
    count = math.prod(mesh.shape[axis] for axis in AXES)
    return lax.ppermute(value, AXES, [(i, i ^ mask) for i in range(count)])


def bits_of(size):
    return [1 << b for b in range(size.bit_length() - 1)]


def pick_kernel(groups, queries_hbm, half_ref, piece_ref, sems):
    half, piece = half_ref.shape[0], piece_ref.shape[0]
    group = lax.axis_index("grp")
    core = (lax.axis_index("proj") + group + 1) % 2
    index = core * groups + group
    copies = [
        pltpu.make_async_copy(queries_hbm.at[0, pl.ds(pl.multiple_of(core * half, 8), half)], half_ref, sems.at[0]),
        pltpu.make_async_copy(queries_hbm.at[0, pl.ds(pl.multiple_of(index * piece, 8), piece)], piece_ref, sems.at[1]),
    ]
    for copy in copies:
        copy.start()
    for copy in copies:
        copy.wait()


def pick_queries(queries, groups):
    rows, columns = queries.shape[1:]
    return pl.pallas_call(
        functools.partial(pick_kernel, groups),
        out_shape=tuple(jax.ShapeDtypeStruct((rows // n, columns), F32) for n in (2, 2 * groups)),
        in_specs=[pl.BlockSpec(memory_space=pl.ANY)],
        out_specs=(pl.BlockSpec(memory_space=pltpu.VMEM),) * 2,
        scratch_shapes=[pltpu.SemaphoreType.DMA((2,))],
        compiler_params=pltpu.CompilerParams(vmem_limit_bytes=4 * MIB),
        cost_estimate=pl.CostEstimate(flops=4 * 10**9, bytes_accessed=10**6, transcendentals=0),
        name="pick_queries",
    )(pltpu.with_memory_space_constraint(queries, pltpu.HBM))


def project_kernel(a_ref, g_ref, p_in_ref, p_out_ref, after_ref, out_ref):
    width = p_in_ref.shape[0]
    out_ref[0:width, :] = lax.dot_general(a_ref[...], p_in_ref[...], NT, preferred_element_type=F32).T
    out_ref[width : 2 * width, :] = lax.dot_general(g_ref[...], p_out_ref[...], NT, preferred_element_type=F32).T


def project(activations, out_grads, proj_in, proj_out, after):
    return pl.pallas_call(
        project_kernel,
        out_shape=jax.ShapeDtypeStruct((2 * proj_in.shape[1], activations.shape[0]), F32),
        in_specs=[pl.BlockSpec(memory_space=pltpu.VMEM)] * 4 + [pl.BlockSpec(memory_space=pl.ANY)],
        out_specs=pl.BlockSpec(memory_space=pltpu.VMEM),
        compiler_params=pltpu.CompilerParams(vmem_limit_bytes=16 * MIB),
        name="project",
    )(activations, out_grads, proj_in.T, proj_out.T, after)


def masks_kernel(lengths_ref, after_ref, member_ref, live_ref, count_ref):
    examples, slots = member_ref.shape
    length = jnp.broadcast_to(lengths_ref[...].astype(F32), (examples, lengths_ref.shape[1]))
    example = lax.broadcasted_iota(jnp.int32, length.shape, 0)
    entry = lax.broadcasted_iota(jnp.int32, length.shape, 1)
    begin = jnp.sum(jnp.where(entry < example, length, 0.0), axis=1, keepdims=True)
    end = jnp.sum(jnp.where(entry <= example, length, 0.0), axis=1, keepdims=True)
    slot = lax.broadcasted_iota(jnp.int32, (examples, slots), 1).astype(F32)
    member_ref[...] = jnp.where((slot >= begin) & (slot < end), 1.0, 0.0).astype(BF16)
    live_ref[...] = jnp.where(slot[0:8] < end[examples - 1 : examples], 1.0, 0.0)
    count_ref[...] = jnp.broadcast_to(end - begin, count_ref.shape)


def masks(lengths, after):
    examples, slots = lengths.shape[1] - 1, after.shape[1]
    return pl.pallas_call(
        masks_kernel,
        out_shape=(
            jax.ShapeDtypeStruct((examples, slots), BF16),
            jax.ShapeDtypeStruct((8, slots), F32),
            jax.ShapeDtypeStruct((examples, 128), F32),
        ),
        in_specs=[pl.BlockSpec(memory_space=pltpu.VMEM), pl.BlockSpec(memory_space=pl.ANY)],
        out_specs=(pl.BlockSpec(memory_space=pltpu.VMEM),) * 3,
        compiler_params=pltpu.CompilerParams(vmem_limit_bytes=4 * MIB),
        cost_estimate=pl.CostEstimate(flops=2 * 10**9, bytes_accessed=10**6, transcendentals=0),
        name="masks",
    )(lengths, after)


def fisher_kernel(live_ref, own_ref, other_ref, out_ref):
    width = out_ref.shape[0]
    both = own_ref[...] + other_ref[...]
    gram = lax.dot_general(both * live_ref[0:1, :], both, NT, precision=HIGHEST, preferred_element_type=F32)
    out_ref[...] = jnp.zeros_like(out_ref)
    out_ref[:, 0:width] = gram[0:width, 0:width]
    out_ref[:, width : 2 * width] = gram[width : 2 * width, width : 2 * width]


def fisher(live, own, other):
    width = own.shape[0] // 2
    return pl.pallas_call(
        fisher_kernel,
        out_shape=jax.ShapeDtypeStruct((width, 128), F32),
        in_specs=[pl.BlockSpec(memory_space=pltpu.VMEM)] * 3,
        out_specs=pl.BlockSpec(memory_space=pltpu.VMEM),
        compiler_params=pltpu.CompilerParams(vmem_limit_bytes=8 * MIB),
        name="fisher",
    )(live, own, other)


def split3(value):
    high = value.astype(BF16)
    rest = value - high.astype(F32)
    middle = rest.astype(BF16)
    return high, middle, (rest - middle.astype(F32)).astype(BF16)


def examples_kernel(member_ref, count_ref, own_ref, other_ref, out_ref):
    width = own_ref.shape[0] // 2
    both = own_ref[...] + other_ref[...]
    inputs, outputs = both[0:width], both[width : 2 * width]
    member, divisor = member_ref[...], count_ref[:, 0:1]
    group = 8
    for first in range(0, width, group):
        outer = jnp.concatenate([outputs[i : i + 1] * inputs for i in range(first, first + group)], axis=0)
        total = None
        for piece in reversed(split3(outer)):
            part = lax.dot_general(member, piece, NT, preferred_element_type=F32)
            total = part if total is None else total + part
        out_ref[:, first * width : (first + group) * width] = total / divisor


def example_grads(member, count, own, other):
    width = own.shape[0] // 2
    return pl.pallas_call(
        examples_kernel,
        out_shape=jax.ShapeDtypeStruct((member.shape[0], width * width), F32),
        in_specs=[pl.BlockSpec(memory_space=pltpu.VMEM)] * 4,
        out_specs=pl.BlockSpec(memory_space=pltpu.VMEM),
        compiler_params=pltpu.CompilerParams(vmem_limit_bytes=8 * MIB),
        cost_estimate=pl.CostEstimate(flops=2 * 10**9, bytes_accessed=10**6, transcendentals=0),
        name="examples",
    )(member, count, own, other)


def split2(value):
    high = value.astype(BF16)
    return high, (value - high.astype(F32)).astype(BF16)


def turn_pairs(load, scratch, width):
    columns, count = scratch.shape
    for c in range(columns // CHUNK):
        scratch[c * CHUNK : (c + 1) * CHUNK, :] = load(c).T
    chunks = []
    for c in range(columns // CHUNK):
        lines = range(c * CHUNK // width, (c + 1) * CHUNK // width)
        chunks.append(jnp.concatenate([scratch[pl.ds(j, width, stride=width), :] for j in lines], axis=0).T)
    return jnp.concatenate(chunks, axis=0)


def arrange_examples_kernel(n_query, blocks_ref, *refs):
    out_refs, (rows, scratch) = refs[:-2], refs[-2:]
    blocks, examples, columns = blocks_ref.shape
    query = lax.axis_index("query")
    for b in range(blocks):
        place = (b // n_query) * n_query + (query ^ (b % n_query))
        rows[pl.ds(pl.multiple_of(place * examples, 8), examples), :] = blocks_ref[b]
    width = math.isqrt(columns)
    turned = turn_pairs(lambda c: rows[:, c * CHUNK : (c + 1) * CHUNK], scratch, width)
    for out_ref, piece in zip(out_refs, split3(turned)):
        out_ref[...] = piece


def arrange_examples(blocks, n_query):
    number, examples, columns = blocks.shape
    count = number * examples
    shape = jax.ShapeDtypeStruct((count * columns // CHUNK, CHUNK), BF16)
    return pl.pallas_call(
        functools.partial(arrange_examples_kernel, n_query),
        out_shape=(shape,) * 3,
        in_specs=[pl.BlockSpec(memory_space=pltpu.VMEM)],
        out_specs=(pl.BlockSpec(memory_space=pltpu.VMEM),) * 3,
        scratch_shapes=[pltpu.VMEM((count, columns), F32), pltpu.VMEM((columns, count), F32)],
        compiler_params=pltpu.CompilerParams(vmem_limit_bytes=12 * MIB),
        name="arrange_examples",
    )(blocks)


def split_near_kernel(own_ref, near_ref, high_ref, low_ref):
    half = near_ref.shape[0]
    start = pl.multiple_of((lax.axis_index("proj") + lax.axis_index("grp")) % 2 * half, 8)
    for i, value in enumerate((own_ref[0, pl.ds(start, half), :], near_ref[...])):
        at = slice(i * half, (i + 1) * half)
        high_ref[at, :], low_ref[at, :] = split2(value)


def split_near(own, near):
    half, columns = near.shape
    shape = jax.ShapeDtypeStruct((2 * half, columns), BF16)
    return pl.pallas_call(
        split_near_kernel,
        out_shape=(shape, shape),
        in_specs=[pl.BlockSpec(memory_space=pltpu.VMEM)] * 2,
        out_specs=(pl.BlockSpec(memory_space=pltpu.VMEM),) * 2,
        compiler_params=pltpu.CompilerParams(vmem_limit_bytes=6 * MIB),
        name="split_near",
    )(own, near)


def damped(fisher_sum):
    width = fisher_sum.shape[0]
    row = lax.broadcasted_iota(jnp.int32, (width, width), 0)
    column = lax.broadcasted_iota(jnp.int32, (width, width), 1)
    trace = jnp.sum(jnp.where(row == column, fisher_sum, 0.0), keepdims=True)
    return fisher_sum * (width / trace) + jnp.where(row == column, 1.0, 0.0)


def inverse_pair(pair):
    width, group = pair.shape[0], 8
    both = jnp.concatenate([damped(pair[:, 0:width]), damped(pair[:, width : 2 * width])], axis=1)
    state = jnp.concatenate([both] * (128 // (2 * width)), axis=1)
    state = [state[i : i + group] for i in range(0, width, group)]
    lane = lax.broadcasted_iota(jnp.int32, (group, 128), 1)
    own = lane % width
    first = lane - own
    sublane = lax.broadcasted_iota(jnp.int32, (group, 128), 0)

    def spread(value, index):
        return jnp.take_along_axis(value, index, axis=1, mode="promise_in_bounds")

    columns = [[spread(part, first + c) for c in range(4)] for part in state]
    for k in range(0, width, 4):
        at, offset = k // group, k % group
        more = k + 4 < width
        ahead = [[spread(part, first + (k + 4 + c)) for c in range(4)] for part in state] if more else None
        inside = (own >= k) & (own < k + 4)

        def row(value, r):
            return value[offset + r : offset + r + 1, :]

        p = [[row(columns[at][c], r) for c in range(4)] for r in range(4)]
        scale = 1.0 / (p[0][0] * p[1][1] - p[0][1] * p[1][0])
        a = ((p[1][1] * scale, -p[0][1] * scale), (-p[1][0] * scale, p[0][0] * scale))
        right = [[a[r][0] * p[0][c] + a[r][1] * p[1][c] for r in range(2)] for c in (2, 3)]
        s = [[p[r][c] - (p[r][0] * right[c - 2][0] + p[r][1] * right[c - 2][1]) for c in (2, 3)] for r in (2, 3)]
        scale = 1.0 / (s[0][0] * s[1][1] - s[0][1] * s[1][0])
        d = ((s[1][1] * scale, -s[0][1] * scale), (-s[1][0] * scale, s[0][0] * scale))

        def solve(q):
            upper = [a[r][0] * q[0] + a[r][1] * q[1] for r in range(2)]
            rest = [q[r] - (p[r][0] * upper[0] + p[r][1] * upper[1]) for r in (2, 3)]
            lower = [d[r][0] * rest[0] + d[r][1] * rest[1] for r in range(2)]
            return [upper[r] - (right[0][r] * lower[0] + right[1][r] * lower[1]) for r in range(2)] + lower

        def step(i, value, solved):
            c = columns[i]
            value = value - ((c[0] * solved[0] + c[1] * solved[1]) + (c[2] * solved[2] + c[3] * solved[3]))
            if i == at:
                for r in range(4):
                    value = jnp.where(sublane == offset + r, solved[r], value)
            return value

        rows = [jnp.where(own[0:1] == k + r, 1.0, jnp.where(inside[0:1], 0.0, row(state[at], r))) for r in range(4)]
        solved = solve(rows)
        following = columns
        if more:
            solved_ahead = [solve([row(ahead[at][c], r) for r in range(4)]) for c in range(4)]
            following = [[step(i, ahead[i][c], solved_ahead[c]) for c in range(4)] for i in range(len(state))]
        state = [step(i, jnp.where(inside, 0.0, part), solved) for i, part in enumerate(state)]
        columns = following
    return [jnp.concatenate([spread(part, own + start) for part in state], axis=0) for start in (0, width)]


def block_diagonal(tiled):
    width, lanes = tiled.shape
    value = jnp.concatenate([jnp.concatenate([tiled] * (CHUNK // lanes), axis=1)] * (CHUNK // width), axis=0)
    row = lax.broadcasted_iota(jnp.int32, (CHUNK, CHUNK), 0) // width
    column = lax.broadcasted_iota(jnp.int32, (CHUNK, CHUNK), 1) // width
    return jnp.where(row == column, value, 0.0)


def times_blocks(high, middle, low, blocks_ref):
    rows = high.shape[0]
    by_high = jnp.dot(jnp.concatenate([high, middle, low], axis=0), blocks_ref[0], preferred_element_type=F32)
    by_middle = jnp.dot(jnp.concatenate([high, middle], axis=0), blocks_ref[1], preferred_element_type=F32)
    by_low = jnp.dot(high, blocks_ref[2], preferred_element_type=F32)
    small = by_high[2 * rows :] + by_middle[rows:] + by_low
    return by_high[0:rows] + (by_high[rows : 2 * rows] + by_middle[0:rows] + small)


def times_queries(both_ref, high_ref, low_ref):
    chunks, count = both_ref.shape[0], both_ref.shape[1] // 2
    total = None
    for c in range(chunks):
        cols = slice(c * CHUNK, (c + 1) * CHUNK)
        by_high = lax.dot_general(both_ref[c], high_ref[:, cols], NT, preferred_element_type=F32)
        by_low = lax.dot_general(both_ref[c, 0:count], low_ref[:, cols], NT, preferred_element_type=F32)
        part = by_high[0:count] + (by_high[count:] + by_low)
        total = part if total is None else total + part
    return total * (1.0 / math.isqrt(chunks * CHUNK))


def condition_kernel(own_ref, other_ref, high_ref, middle_ref, low_ref, near_high_ref, near_low_ref, both_ref, near_ref, in_ref, out_ref, scratch):
    columns, count = scratch.shape
    width = own_ref.shape[0]
    total = own_ref[...] + other_ref[...]
    for ref, inverse in zip((in_ref, out_ref), inverse_pair(total[:, 0 : 2 * width])):
        for piece, value in enumerate(split3(block_diagonal(inverse))):
            ref[piece] = value
    left = times_blocks(high_ref[...], middle_ref[...], low_ref[...], out_ref)
    turned = turn_pairs(lambda c: left[c * count : (c + 1) * count], scratch, width)
    high, low = split2(times_blocks(*split3(turned), in_ref))
    for c in range(columns // CHUNK):
        both_ref[c, 0:count] = high[c * count : (c + 1) * count]
        both_ref[c, count:] = low[c * count : (c + 1) * count]
    near_ref[...] = times_queries(both_ref, near_high_ref, near_low_ref)


def condition(own, other, pieces, near):
    columns = near[0].shape[1]
    count = pieces[0].shape[0] * CHUNK // columns
    return pl.pallas_call(
        condition_kernel,
        out_shape=(
            jax.ShapeDtypeStruct((columns // CHUNK, 2 * count, CHUNK), BF16),
            jax.ShapeDtypeStruct((count, near[0].shape[0]), F32),
        ),
        in_specs=[pl.BlockSpec(memory_space=pltpu.VMEM)] * 7,
        out_specs=(pl.BlockSpec(memory_space=pltpu.VMEM),) * 2,
        scratch_shapes=[pltpu.VMEM((3, CHUNK, CHUNK), BF16)] * 2 + [pltpu.VMEM((columns, count), F32)],
        compiler_params=pltpu.CompilerParams(vmem_limit_bytes=12 * MIB),
        cost_estimate=pl.CostEstimate(flops=4 * 10**9, bytes_accessed=10**6, transcendentals=0),
        name="condition",
    )(own, other, *pieces, *near)


def score_kernel(groups, both_ref, near_ref, *refs):
    fetched_refs, (scores_ref, high_ref, low_ref) = refs[:-3], refs[-3:]
    near = near_ref.shape[1]
    half = fetched_refs[0].shape[0]
    piece = half // groups
    group = lax.axis_index("grp")
    for i, ref in enumerate(fetched_refs):
        for g in range(groups):
            at = pl.ds(pl.multiple_of(i * half + (group ^ g) * piece, 16), piece)
            high_ref[at, :], low_ref[at, :] = split2(ref[g * piece : (g + 1) * piece, :])
    scores_ref[:, 0:near] = near_ref[...]
    scores_ref[:, near:] = times_queries(both_ref, high_ref, low_ref)


def score(groups, both, near, fetched):
    rows, columns = len(fetched) * fetched[0].shape[0], fetched[0].shape[1]
    return pl.pallas_call(
        functools.partial(score_kernel, groups),
        out_shape=jax.ShapeDtypeStruct((near.shape[0], near.shape[1] + rows), F32),
        in_specs=[pl.BlockSpec(memory_space=pltpu.VMEM)] * (2 + len(fetched)),
        out_specs=pl.BlockSpec(memory_space=pltpu.VMEM),
        scratch_shapes=[pltpu.VMEM((rows, columns), BF16)] * 2,
        compiler_params=pltpu.CompilerParams(vmem_limit_bytes=(8 + len(fetched)) * MIB),
        name="score",
    )(both, near, *fetched)


def place_kernel(half, kept_ref, received_ref, out_ref):
    core = (lax.axis_index("proj") + lax.axis_index("grp")) % 2
    kept, received = kept_ref[...], received_ref[...]
    first = jnp.where(core == 0, kept, received)
    second = jnp.where(core == 0, received, kept)
    for r in range(kept.shape[1] // half):
        at = slice(r * half, (r + 1) * half)
        start = pl.multiple_of((lax.axis_index("dp") ^ r) * 2 * half, 128)
        out_ref[:, pl.ds(start, 2 * half)] = jnp.concatenate([first[:, at], second[:, at]], axis=1)


def place(half, kept, received):
    rows, columns = kept.shape
    return pl.pallas_call(
        functools.partial(place_kernel, half),
        out_shape=jax.ShapeDtypeStruct((rows, 2 * columns), F32),
        in_specs=[pl.BlockSpec(memory_space=pltpu.VMEM)] * 2,
        out_specs=pl.BlockSpec(memory_space=pltpu.VMEM),
        compiler_params=pltpu.CompilerParams(vmem_limit_bytes=8 * MIB),
        name="place",
    )(kept, received)


def hold_kernel(value_ref, after_ref, out_ref):
    out_ref[...] = value_ref[...]


def hold(value, after):
    return pl.pallas_call(
        hold_kernel,
        out_shape=jax.ShapeDtypeStruct(value.shape, value.dtype),
        in_specs=[pl.BlockSpec(memory_space=pltpu.VMEM), pl.BlockSpec(memory_space=pl.ANY)],
        out_specs=pl.BlockSpec(memory_space=pltpu.VMEM),
        compiler_params=pltpu.CompilerParams(vmem_limit_bytes=4 * MIB),
        cost_estimate=pl.CostEstimate(flops=10**9, bytes_accessed=10**6, transcendentals=0),
        name="hold",
    )(value, after)


ORDER = "x21"
E_STAGE = 0
Y_STAGES = (1,)


def body(mesh, activations, out_grads, proj_in, proj_out, lengths, queries):
    groups, n_dp, n_query = mesh.shape["grp"], mesh.shape["dp"], mesh.shape["query"]
    core_bit = 1
    unit = 2 * n_query
    query_bits = [2 * b for b in bits_of(n_query)]
    dp_bits = [b * unit for b in bits_of(n_dp)]
    group_bits = [b * unit * n_dp for b in bits_of(groups)]

    half, piece = pick_queries(queries, groups)
    fetched = [swap(piece, mesh, r * unit | core_bit) for r in range(2, n_dp)]

    own = project(activations, out_grads, proj_in, proj_out, half)
    half, own = lax.optimization_barrier((half, own))
    fetched = [swap(half, mesh, unit | core_bit)] + fetched
    member, live, count = masks(lengths, own)
    other = swap(own, mesh, core_bit)
    own, other, live = lax.optimization_barrier((own, other, live))

    factor = fisher(live, own, other)
    factor, own, other = lax.optimization_barrier((factor, own, other))
    blocks = example_grads(member, count, own, other)[None]
    groups_of = {"x": query_bits, "1": dp_bits[:1], "2": dp_bits[1:]}
    steps = [bit | core_bit for name in ORDER for bit in groups_of[name]]

    def beside(stage, factor, blocks, fetched):
        i = stage - E_STAGE
        if 0 <= i < len(query_bits):
            blocks = hold(blocks, factor)
            blocks = jnp.concatenate([blocks, swap(blocks, mesh, query_bits[i] | core_bit)], axis=0)
        if stage in Y_STAGES:
            first, end = (1, n_dp - 1)
            for r in range(first, end):
                fetched[r] = hold(fetched[r], factor)
                for bit in group_bits:
                    fetched[r] = jnp.concatenate([fetched[r], swap(fetched[r], mesh, bit | (core_bit if bit == group_bits[0] else 0))], axis=0)
        return blocks

    for step, mask in enumerate(steps):
        blocks = beside(step, factor, blocks, fetched)
        received = swap(factor, mesh, mask)
        if step < len(steps) - 1:
            factor = factor + received
    arranged = arrange_examples(blocks, n_query)
    near = split_near(queries, fetched[0])
    arranged, near, received = lax.optimization_barrier((arranged, near, received))
    both, near = condition(factor, received, arranged, near)

    scores = score(groups, both, near, fetched[1:])
    return place(queries.shape[1] // 2, scores, swap(scores, mesh, core_bit))


def solution(mesh):
    in_specs = (
        P(("grp", "dp", "query"), "proj"),
        P(("grp", "dp", "query"), "proj"),
        P("proj", None),
        P("proj", None),
        P(("grp", "dp", "query"), None),
        P("query", "dp", None),
    )
    out_specs = P(("grp", "dp"), "query")
    return jax.shard_map(
        functools.partial(body, mesh), mesh=mesh, in_specs=in_specs, out_specs=out_specs, check_vma=False
    )
```

```python
import functools
import math

import jax
import jax.numpy as jnp
from jax import lax
from jax.experimental import pallas as pl
from jax.experimental.pallas import tpu as pltpu
from jax.sharding import PartitionSpec as P

F32 = jnp.float32
BF16 = jnp.bfloat16
HIGHEST = lax.Precision.HIGHEST
NT = (((1,), (1,)), ((), ()))
AXES = ("grp", "dp", "query", "proj")
MIB = 2**20
CHUNK = 256
QUERY_STEP = 1


def swap(value, mesh, mask):
    count = math.prod(mesh.shape[axis] for axis in AXES)
    return lax.ppermute(value, AXES, [(i, i ^ mask) for i in range(count)])


def bits_of(size):
    return [1 << b for b in range(size.bit_length() - 1)]


def pick_kernel(groups, queries_hbm, half_ref, piece_ref, sems):
    half, piece = half_ref.shape[0], piece_ref.shape[0]
    core = 1 - lax.axis_index("proj")
    index = core * groups + lax.axis_index("grp")
    copies = [
        pltpu.make_async_copy(queries_hbm.at[0, pl.ds(pl.multiple_of(core * half, 8), half)], half_ref, sems.at[0]),
        pltpu.make_async_copy(queries_hbm.at[0, pl.ds(pl.multiple_of(index * piece, 8), piece)], piece_ref, sems.at[1]),
    ]
    for copy in copies:
        copy.start()
    for copy in copies:
        copy.wait()


def pick_queries(queries, groups):
    rows, columns = queries.shape[1:]
    return pl.pallas_call(
        functools.partial(pick_kernel, groups),
        out_shape=tuple(jax.ShapeDtypeStruct((rows // n, columns), F32) for n in (2, 2 * groups)),
        in_specs=[pl.BlockSpec(memory_space=pl.ANY)],
        out_specs=(pl.BlockSpec(memory_space=pltpu.VMEM),) * 2,
        scratch_shapes=[pltpu.SemaphoreType.DMA((2,))],
        compiler_params=pltpu.CompilerParams(vmem_limit_bytes=4 * MIB),
        cost_estimate=pl.CostEstimate(flops=4 * 10**9, bytes_accessed=10**6, transcendentals=0),
        name="pick_queries",
    )(pltpu.with_memory_space_constraint(queries, pltpu.HBM))


def project_kernel(a_ref, g_ref, p_in_ref, p_out_ref, after_ref, out_ref):
    width = p_in_ref.shape[0]
    out_ref[0:width, :] = lax.dot_general(a_ref[...], p_in_ref[...], NT, preferred_element_type=F32).T
    out_ref[width : 2 * width, :] = lax.dot_general(g_ref[...], p_out_ref[...], NT, preferred_element_type=F32).T


def project(activations, out_grads, proj_in, proj_out, after):
    return pl.pallas_call(
        project_kernel,
        out_shape=jax.ShapeDtypeStruct((2 * proj_in.shape[1], activations.shape[0]), F32),
        in_specs=[pl.BlockSpec(memory_space=pltpu.VMEM)] * 4 + [pl.BlockSpec(memory_space=pl.ANY)],
        out_specs=pl.BlockSpec(memory_space=pltpu.VMEM),
        compiler_params=pltpu.CompilerParams(vmem_limit_bytes=16 * MIB),
        name="project",
    )(activations, out_grads, proj_in.T, proj_out.T, after)


def masks_kernel(lengths_ref, after_ref, member_ref, live_ref, count_ref):
    examples, slots = member_ref.shape
    length = jnp.broadcast_to(lengths_ref[...].astype(F32), (examples, lengths_ref.shape[1]))
    example = lax.broadcasted_iota(jnp.int32, length.shape, 0)
    entry = lax.broadcasted_iota(jnp.int32, length.shape, 1)
    begin = jnp.sum(jnp.where(entry < example, length, 0.0), axis=1, keepdims=True)
    end = jnp.sum(jnp.where(entry <= example, length, 0.0), axis=1, keepdims=True)
    slot = lax.broadcasted_iota(jnp.int32, (examples, slots), 1).astype(F32)
    member_ref[...] = jnp.where((slot >= begin) & (slot < end), 1.0, 0.0).astype(BF16)
    live_ref[...] = jnp.where(slot[0:8] < end[examples - 1 : examples], 1.0, 0.0)
    count_ref[...] = jnp.broadcast_to(end - begin, count_ref.shape)


def masks(lengths, after):
    examples, slots = lengths.shape[1] - 1, after.shape[1]
    return pl.pallas_call(
        masks_kernel,
        out_shape=(
            jax.ShapeDtypeStruct((examples, slots), BF16),
            jax.ShapeDtypeStruct((8, slots), F32),
            jax.ShapeDtypeStruct((examples, 128), F32),
        ),
        in_specs=[pl.BlockSpec(memory_space=pltpu.VMEM), pl.BlockSpec(memory_space=pl.ANY)],
        out_specs=(pl.BlockSpec(memory_space=pltpu.VMEM),) * 3,
        compiler_params=pltpu.CompilerParams(vmem_limit_bytes=4 * MIB),
        cost_estimate=pl.CostEstimate(flops=2 * 10**9, bytes_accessed=10**6, transcendentals=0),
        name="masks",
    )(lengths, after)


def fisher_kernel(live_ref, own_ref, other_ref, out_ref):
    width = out_ref.shape[0]
    both = own_ref[...] + other_ref[...]
    gram = lax.dot_general(both * live_ref[0:1, :], both, NT, precision=HIGHEST, preferred_element_type=F32)
    out_ref[...] = jnp.zeros_like(out_ref)
    out_ref[:, 0:width] = gram[0:width, 0:width]
    out_ref[:, width : 2 * width] = gram[width : 2 * width, width : 2 * width]


def fisher(live, own, other):
    width = own.shape[0] // 2
    return pl.pallas_call(
        fisher_kernel,
        out_shape=jax.ShapeDtypeStruct((width, 128), F32),
        in_specs=[pl.BlockSpec(memory_space=pltpu.VMEM)] * 3,
        out_specs=pl.BlockSpec(memory_space=pltpu.VMEM),
        compiler_params=pltpu.CompilerParams(vmem_limit_bytes=8 * MIB),
        name="fisher",
    )(live, own, other)


def split3(value):
    high = value.astype(BF16)
    rest = value - high.astype(F32)
    middle = rest.astype(BF16)
    return high, middle, (rest - middle.astype(F32)).astype(BF16)


def examples_kernel(member_ref, count_ref, own_ref, other_ref, out_ref):
    width = own_ref.shape[0] // 2
    both = own_ref[...] + other_ref[...]
    inputs, outputs = both[0:width], both[width : 2 * width]
    member, divisor = member_ref[...], count_ref[:, 0:1]
    group = 16
    for first in range(0, width, group):
        outer = jnp.concatenate([outputs[i : i + 1] * inputs for i in range(first, first + group)], axis=0)
        total = None
        for piece in reversed(split3(outer)):
            part = lax.dot_general(member, piece, NT, preferred_element_type=F32)
            total = part if total is None else total + part
        out_ref[:, first * width : (first + group) * width] = total / divisor


def example_grads(member, count, own, other):
    width = own.shape[0] // 2
    return pl.pallas_call(
        examples_kernel,
        out_shape=jax.ShapeDtypeStruct((member.shape[0], width * width), F32),
        in_specs=[pl.BlockSpec(memory_space=pltpu.VMEM)] * 4,
        out_specs=pl.BlockSpec(memory_space=pltpu.VMEM),
        compiler_params=pltpu.CompilerParams(vmem_limit_bytes=8 * MIB),
        cost_estimate=pl.CostEstimate(flops=2 * 10**9, bytes_accessed=10**6, transcendentals=0),
        name="examples",
    )(member, count, own, other)


def split2(value):
    high = value.astype(BF16)
    return high, (value - high.astype(F32)).astype(BF16)


def turn_pairs(load, scratch, width):
    columns, count = scratch.shape
    for c in range(columns // CHUNK):
        scratch[c * CHUNK : (c + 1) * CHUNK, :] = load(c).T
    chunks = []
    for c in range(columns // CHUNK):
        lines = range(c * CHUNK // width, (c + 1) * CHUNK // width)
        chunks.append(jnp.concatenate([scratch[pl.ds(j, width, stride=width), :] for j in lines], axis=0).T)
    return jnp.concatenate(chunks, axis=0)


def arrange_examples_kernel(n_query, blocks_ref, *refs):
    out_refs, (rows, scratch) = refs[:-2], refs[-2:]
    blocks, examples, columns = blocks_ref.shape
    query = lax.axis_index("query")
    for b in range(blocks):
        place = (b // n_query) * n_query + (query ^ (b % n_query))
        rows[pl.ds(pl.multiple_of(place * examples, 8), examples), :] = blocks_ref[b]
    width = math.isqrt(columns)
    turned = turn_pairs(lambda c: rows[:, c * CHUNK : (c + 1) * CHUNK], scratch, width)
    for out_ref, piece in zip(out_refs, split3(turned)):
        out_ref[...] = piece


def arrange_examples(blocks, n_query):
    number, examples, columns = blocks.shape
    count = number * examples
    shape = jax.ShapeDtypeStruct((count * columns // CHUNK, CHUNK), BF16)
    return pl.pallas_call(
        functools.partial(arrange_examples_kernel, n_query),
        out_shape=(shape,) * 3,
        in_specs=[pl.BlockSpec(memory_space=pltpu.VMEM)],
        out_specs=(pl.BlockSpec(memory_space=pltpu.VMEM),) * 3,
        scratch_shapes=[pltpu.VMEM((count, columns), F32), pltpu.VMEM((columns, count), F32)],
        compiler_params=pltpu.CompilerParams(vmem_limit_bytes=12 * MIB),
        name="arrange_examples",
    )(blocks)


def split_near_kernel(own_ref, near_ref, high_ref, low_ref):
    half = near_ref.shape[0]
    start = pl.multiple_of(lax.axis_index("proj") * half, 8)
    for i, value in enumerate((own_ref[0, pl.ds(start, half), :], near_ref[...])):
        at = slice(i * half, (i + 1) * half)
        high_ref[at, :], low_ref[at, :] = split2(value)


def split_near(own, near):
    half, columns = near.shape
    shape = jax.ShapeDtypeStruct((2 * half, columns), BF16)
    return pl.pallas_call(
        split_near_kernel,
        out_shape=(shape, shape),
        in_specs=[pl.BlockSpec(memory_space=pltpu.VMEM)] * 2,
        out_specs=(pl.BlockSpec(memory_space=pltpu.VMEM),) * 2,
        compiler_params=pltpu.CompilerParams(vmem_limit_bytes=6 * MIB),
        name="split_near",
    )(own, near)


def damped(fisher_sum):
    width = fisher_sum.shape[0]
    row = lax.broadcasted_iota(jnp.int32, (width, width), 0)
    column = lax.broadcasted_iota(jnp.int32, (width, width), 1)
    trace = jnp.sum(jnp.where(row == column, fisher_sum, 0.0), keepdims=True)
    return fisher_sum * (width / trace) + jnp.where(row == column, 1.0, 0.0)


def inverse_pair(pair):
    width, group = pair.shape[0], 8
    both = jnp.concatenate([damped(pair[:, 0:width]), damped(pair[:, width : 2 * width])], axis=1)
    state = jnp.concatenate([both] * (128 // (2 * width)), axis=1)
    state = [state[i : i + group] for i in range(0, width, group)]
    lane = lax.broadcasted_iota(jnp.int32, (group, 128), 1)
    own = lane % width
    first = lane - own
    sublane = lax.broadcasted_iota(jnp.int32, (group, 128), 0)

    def spread(value, index):
        return jnp.take_along_axis(value, index, axis=1, mode="promise_in_bounds")

    columns = [[spread(part, first + c) for c in range(4)] for part in state]
    for k in range(0, width, 4):
        at, offset = k // group, k % group
        more = k + 4 < width
        ahead = [[spread(part, first + (k + 4 + c)) for c in range(4)] for part in state] if more else None
        inside = (own >= k) & (own < k + 4)

        def row(value, r):
            return value[offset + r : offset + r + 1, :]

        p = [[row(columns[at][c], r) for c in range(4)] for r in range(4)]
        scale = 1.0 / (p[0][0] * p[1][1] - p[0][1] * p[1][0])
        a = ((p[1][1] * scale, -p[0][1] * scale), (-p[1][0] * scale, p[0][0] * scale))
        right = [[a[r][0] * p[0][c] + a[r][1] * p[1][c] for r in range(2)] for c in (2, 3)]
        s = [[p[r][c] - (p[r][0] * right[c - 2][0] + p[r][1] * right[c - 2][1]) for c in (2, 3)] for r in (2, 3)]
        scale = 1.0 / (s[0][0] * s[1][1] - s[0][1] * s[1][0])
        d = ((s[1][1] * scale, -s[0][1] * scale), (-s[1][0] * scale, s[0][0] * scale))

        def solve(q):
            upper = [a[r][0] * q[0] + a[r][1] * q[1] for r in range(2)]
            rest = [q[r] - (p[r][0] * upper[0] + p[r][1] * upper[1]) for r in (2, 3)]
            lower = [d[r][0] * rest[0] + d[r][1] * rest[1] for r in range(2)]
            return [upper[r] - (right[0][r] * lower[0] + right[1][r] * lower[1]) for r in range(2)] + lower

        def step(i, value, solved):
            c = columns[i]
            value = value - ((c[0] * solved[0] + c[1] * solved[1]) + (c[2] * solved[2] + c[3] * solved[3]))
            if i == at:
                for r in range(4):
                    value = jnp.where(sublane == offset + r, solved[r], value)
            return value

        rows = [jnp.where(own[0:1] == k + r, 1.0, jnp.where(inside[0:1], 0.0, row(state[at], r))) for r in range(4)]
        solved = solve(rows)
        following = columns
        if more:
            solved_ahead = [solve([row(ahead[at][c], r) for r in range(4)]) for c in range(4)]
            following = [[step(i, ahead[i][c], solved_ahead[c]) for c in range(4)] for i in range(len(state))]
        state = [step(i, jnp.where(inside, 0.0, part), solved) for i, part in enumerate(state)]
        columns = following
    return [jnp.concatenate([spread(part, own + start) for part in state], axis=0) for start in (0, width)]


def block_diagonal(tiled):
    width, lanes = tiled.shape
    value = jnp.concatenate([jnp.concatenate([tiled] * (CHUNK // lanes), axis=1)] * (CHUNK // width), axis=0)
    row = lax.broadcasted_iota(jnp.int32, (CHUNK, CHUNK), 0) // width
    column = lax.broadcasted_iota(jnp.int32, (CHUNK, CHUNK), 1) // width
    return jnp.where(row == column, value, 0.0)


def times_blocks(high, middle, low, blocks_ref):
    rows = high.shape[0]
    by_high = jnp.dot(jnp.concatenate([high, middle, low], axis=0), blocks_ref[0], preferred_element_type=F32)
    by_middle = jnp.dot(jnp.concatenate([high, middle], axis=0), blocks_ref[1], preferred_element_type=F32)
    by_low = jnp.dot(high, blocks_ref[2], preferred_element_type=F32)
    small = by_high[2 * rows :] + by_middle[rows:] + by_low
    return by_high[0:rows] + (by_high[rows : 2 * rows] + by_middle[0:rows] + small)


def times_queries(both_ref, high_ref, low_ref):
    chunks, count = both_ref.shape[0], both_ref.shape[1] // 2
    total = None
    for c in range(chunks):
        cols = slice(c * CHUNK, (c + 1) * CHUNK)
        by_high = lax.dot_general(both_ref[c], high_ref[:, cols], NT, preferred_element_type=F32)
        by_low = lax.dot_general(both_ref[c, 0:count], low_ref[:, cols], NT, preferred_element_type=F32)
        part = by_high[0:count] + (by_high[count:] + by_low)
        total = part if total is None else total + part
    return total * (1.0 / math.isqrt(chunks * CHUNK))


def condition_kernel(own_ref, other_ref, high_ref, middle_ref, low_ref, near_high_ref, near_low_ref, both_ref, near_ref, in_ref, out_ref, scratch):
    columns, count = scratch.shape
    width = own_ref.shape[0]
    total = own_ref[...] + other_ref[...]
    for ref, inverse in zip((in_ref, out_ref), inverse_pair(total[:, 0 : 2 * width])):
        for piece, value in enumerate(split3(block_diagonal(inverse))):
            ref[piece] = value
    left = times_blocks(high_ref[...], middle_ref[...], low_ref[...], out_ref)
    turned = turn_pairs(lambda c: left[c * count : (c + 1) * count], scratch, width)
    high, low = split2(times_blocks(*split3(turned), in_ref))
    for c in range(columns // CHUNK):
        both_ref[c, 0:count] = high[c * count : (c + 1) * count]
        both_ref[c, count:] = low[c * count : (c + 1) * count]
    near_ref[...] = times_queries(both_ref, near_high_ref, near_low_ref)


def condition(own, other, pieces, near):
    columns = near[0].shape[1]
    count = pieces[0].shape[0] * CHUNK // columns
    return pl.pallas_call(
        condition_kernel,
        out_shape=(
            jax.ShapeDtypeStruct((columns // CHUNK, 2 * count, CHUNK), BF16),
            jax.ShapeDtypeStruct((count, near[0].shape[0]), F32),
        ),
        in_specs=[pl.BlockSpec(memory_space=pltpu.VMEM)] * 7,
        out_specs=(pl.BlockSpec(memory_space=pltpu.VMEM),) * 2,
        scratch_shapes=[pltpu.VMEM((3, CHUNK, CHUNK), BF16)] * 2 + [pltpu.VMEM((columns, count), F32)],
        compiler_params=pltpu.CompilerParams(vmem_limit_bytes=12 * MIB),
        cost_estimate=pl.CostEstimate(flops=4 * 10**9, bytes_accessed=10**6, transcendentals=0),
        name="condition",
    )(own, other, *pieces, *near)


def score_kernel(groups, both_ref, near_ref, *refs):
    fetched_refs, (scores_ref, high_ref, low_ref) = refs[:-3], refs[-3:]
    near = near_ref.shape[1]
    half = fetched_refs[0].shape[0]
    piece = half // groups
    group = lax.axis_index("grp")
    for i, ref in enumerate(fetched_refs):
        for g in range(groups):
            at = pl.ds(pl.multiple_of(i * half + (group ^ g) * piece, 16), piece)
            high_ref[at, :], low_ref[at, :] = split2(ref[g * piece : (g + 1) * piece, :])
    scores_ref[:, 0:near] = near_ref[...]
    scores_ref[:, near:] = times_queries(both_ref, high_ref, low_ref)


def score(groups, both, near, fetched):
    rows, columns = len(fetched) * fetched[0].shape[0], fetched[0].shape[1]
    return pl.pallas_call(
        functools.partial(score_kernel, groups),
        out_shape=jax.ShapeDtypeStruct((near.shape[0], near.shape[1] + rows), F32),
        in_specs=[pl.BlockSpec(memory_space=pltpu.VMEM)] * (2 + len(fetched)),
        out_specs=pl.BlockSpec(memory_space=pltpu.VMEM),
        scratch_shapes=[pltpu.VMEM((rows, columns), BF16)] * 2,
        compiler_params=pltpu.CompilerParams(vmem_limit_bytes=(8 + len(fetched)) * MIB),
        name="score",
    )(both, near, *fetched)


def place_kernel(half, kept_ref, received_ref, out_ref):
    core = lax.axis_index("proj")
    kept, received = kept_ref[...], received_ref[...]
    first = jnp.where(core == 0, kept, received)
    second = jnp.where(core == 0, received, kept)
    for r in range(kept.shape[1] // half):
        at = slice(r * half, (r + 1) * half)
        start = pl.multiple_of((lax.axis_index("dp") ^ r) * 2 * half, 128)
        out_ref[:, pl.ds(start, 2 * half)] = jnp.concatenate([first[:, at], second[:, at]], axis=1)


def place(half, kept, received):
    rows, columns = kept.shape
    return pl.pallas_call(
        functools.partial(place_kernel, half),
        out_shape=jax.ShapeDtypeStruct((rows, 2 * columns), F32),
        in_specs=[pl.BlockSpec(memory_space=pltpu.VMEM)] * 2,
        out_specs=pl.BlockSpec(memory_space=pltpu.VMEM),
        compiler_params=pltpu.CompilerParams(vmem_limit_bytes=8 * MIB),
        name="place",
    )(kept, received)


def hold_kernel(value_ref, after_ref, out_ref):
    out_ref[...] = value_ref[...]


def hold(value, after):
    return pl.pallas_call(
        hold_kernel,
        out_shape=jax.ShapeDtypeStruct(value.shape, value.dtype),
        in_specs=[pl.BlockSpec(memory_space=pltpu.VMEM), pl.BlockSpec(memory_space=pl.ANY)],
        out_specs=pl.BlockSpec(memory_space=pltpu.VMEM),
        compiler_params=pltpu.CompilerParams(vmem_limit_bytes=4 * MIB),
        cost_estimate=pl.CostEstimate(flops=10**9, bytes_accessed=10**6, transcendentals=0),
        name="hold",
    )(value, after)


ORDER = "x21"
E_STAGE = 0
Y_STAGES = (1,)


def body(mesh, activations, out_grads, proj_in, proj_out, lengths, queries):
    groups, n_dp, n_query = mesh.shape["grp"], mesh.shape["dp"], mesh.shape["query"]
    core_bit = 1
    unit = 2 * n_query
    query_bits = [2 * b for b in bits_of(n_query)]
    dp_bits = [b * unit for b in bits_of(n_dp)]
    group_bits = [b * unit * n_dp for b in bits_of(groups)]

    half, piece = pick_queries(queries, groups)
    fetched = [swap(piece, mesh, r * unit | core_bit) for r in range(n_dp - 1, 1, -1)][::-1]

    own = project(activations, out_grads, proj_in, proj_out, half)
    half, own = lax.optimization_barrier((half, own))
    fetched = [swap(half, mesh, unit | core_bit)] + fetched
    member, live, count = masks(lengths, own)
    other = swap(own, mesh, core_bit)
    own, other, live = lax.optimization_barrier((own, other, live))

    factor = fisher(live, own, other)
    factor, own, other = lax.optimization_barrier((factor, own, other))
    blocks = example_grads(member, count, own, other)[None]
    groups_of = {"x": query_bits, "1": dp_bits[:1], "2": dp_bits[1:]}
    steps = [bit | core_bit for name in ORDER for bit in groups_of[name]]

    def beside(stage, factor, blocks, fetched):
        i = stage - E_STAGE
        if 0 <= i < len(query_bits):
            blocks = hold(blocks, factor)
            blocks = jnp.concatenate([blocks, swap(blocks, mesh, query_bits[i] | core_bit)], axis=0)
        if stage in Y_STAGES:
            first, end = (1, n_dp - 1)
            for r in range(end - 1, first - 1, -1):
                fetched[r] = hold(fetched[r], factor)
                for bit in group_bits:
                    fetched[r] = jnp.concatenate([fetched[r], swap(fetched[r], mesh, bit)], axis=0)
        return blocks

    for step, mask in enumerate(steps):
        blocks = beside(step, factor, blocks, fetched)
        received = swap(factor, mesh, mask)
        if step < len(steps) - 1:
            factor = factor + received
    arranged = arrange_examples(blocks, n_query)
    near = split_near(queries, fetched[0])
    arranged, near, received = lax.optimization_barrier((arranged, near, received))
    both, near = condition(factor, received, arranged, near)

    scores = score(groups, both, near, fetched[1:])
    return place(queries.shape[1] // 2, scores, swap(scores, mesh, core_bit))


def solution(mesh):
    in_specs = (
        P(("grp", "dp", "query"), "proj"),
        P(("grp", "dp", "query"), "proj"),
        P("proj", None),
        P("proj", None),
        P(("grp", "dp", "query"), None),
        P("query", "dp", None),
    )
    out_specs = P(("grp", "dp"), "query")
    return jax.shard_map(
        functools.partial(body, mesh), mesh=mesh, in_specs=in_specs, out_specs=out_specs, check_vma=False
    )
```
